32 devices in a mesh: fsdp: 16 (over z, x, core), seq: 2 (over y).
Axes of the slice: x: 2, y: 2, z: 4, core: 2. Of those that a mesh axis runs over, the one named last changes fastest.
Arguments:
- tokens: bfloat16 [32768, 512], P(('fsdp', 'seq')), may hold values from -6 to 6
- w_query: bfloat16 [512, 512], P('fsdp'), may hold values from -0.5 to 0.5
- w_key: bfloat16 [512, 512], P('fsdp'), may hold values from -0.25 to 0.25
- w_value: bfloat16 [512, 512], P('fsdp'), may hold values from -0.25 to 0.25
- w_control: bfloat16 [512, 512], P('fsdp'), may hold values from -0.5 to 0.5
- w_out: bfloat16 [512, 512], P('fsdp'), may hold values from -0.75 to 0.75
- w_up: bfloat16 [512, 2048], P('fsdp'), may hold values from -0.25 to 0.25
- w_down: bfloat16 [2048, 512], P('fsdp'), may hold values from -0.1875 to 0.1875
- gain_attn: bfloat16 [512], P('fsdp'), may hold values from 0.5 to 1.5
- gain_ffn: bfloat16 [512], P('fsdp'), may hold values from 0.5 to 1.5
- bias_up: bfloat16 [2048], P('fsdp'), may hold values from -3 to 3
- bias_down: bfloat16 [512], P('fsdp'), may hold values from -3 to 3
- cotangent: bfloat16 [32768, 512], P(('fsdp', 'seq')), may hold values from -6 to 6
Outputs:
- layer_out: bfloat16 [32768, 512], P(('fsdp', 'seq'))
- grad_tokens: float32 [32768, 512], P(('fsdp', 'seq'))
- grad_w_query: float32 [512, 512], P('fsdp')
- grad_w_key: float32 [512, 512], P('fsdp')
- grad_w_value: float32 [512, 512], P('fsdp')
- grad_w_control: float32 [512, 512], P('fsdp')
- grad_w_out: float32 [512, 512], P('fsdp')
- grad_w_up: float32 [512, 2048], P('fsdp')
- grad_w_down: float32 [2048, 512], P('fsdp')
- grad_gain_attn: float32 [512], P('fsdp')
- grad_gain_ffn: float32 [512], P('fsdp')
- grad_bias_up: float32 [2048], P('fsdp')
- grad_bias_down: float32 [512], P('fsdp')
The draws below stay inside these ranges and needn't reach their ends.
All inputs are finite; a program needn't handle non-finite values.
Results may differ from the reference program's by a relative error of at most 0.02.
The reference program's roundings to bfloat16 on the way count: a program that leaves them out, or rounds other values in their place, can miss the bound.
Values may be sent and summed in bfloat16 or wider, within the bound.
No kernel may reach another device: no remote copies, remote signals or barrier semaphores. Data moves between devices by JAX's collectives and lax.ppermute only.
A program may use at most 128 MiB of HBM per device.

```python
import math
import jax
import jax.numpy as jnp
from jax import lax

D = 512
H = 8
HEAD = 64
SLOTS = 64
FF = 2048
LEN = 2048
SEQS = 16
TOKENS = 32768


def with_spikes(values, own_key, source, target, parts, factor):
    def block_of(dim):
        return (jnp.arange(values.shape[dim]) // (values.shape[dim] // parts)).reshape((-1,) + (1,) * (values.ndim - 1 - dim))

    first = jax.random.permutation(own_key, parts)[block_of(target)]
    second = (block_of(target) + parts // 2) % parts
    return jnp.where((block_of(source) == first) | (block_of(source) == second), factor * values, values)


def steps_of(stream_key, shape, pieces, least, top_value):
    def one(dim, shards_of):
        draws = jax.random.uniform(jax.random.fold_in(jax.random.fold_in(stream_key, 6), dim), (shards_of,), jnp.float32, least / len(pieces), top_value / len(pieces))
        return jnp.repeat(jnp.exp(draws), shape[dim] // shards_of).reshape((-1,) + (1,) * (len(shape) - dim - 1))

    factor_of = one(*pieces[0])
    for cut in pieces[1:]:
        factor_of = factor_of * one(*cut)
    return factor_of


def normal_values(stream_key, extent, scale, limit, cuts=(), kind=jnp.bfloat16):
    values = jax.random.normal(stream_key, extent, jnp.float32) * scale
    if len(cuts) > 0:
        values = steps_of(stream_key, extent, cuts, -0.22, 0.18) * values
    return jnp.clip(values, min=-limit, max=limit).astype(kind)


def gaussian_with(key, extent, scale, limit, cuts, heavy, held_as=jnp.bfloat16):
    entries = scale * jax.random.normal(key, extent, jnp.float32)
    if cuts:
        entries = entries * steps_of(key, extent, cuts, -0.22, 0.18)
    return jnp.clip(with_spikes(entries, jax.random.fold_in(key, 3), *heavy), -limit, limit).astype(held_as)


def setup_inputs(seed: int = 0) -> dict:
    arg_keys = jax.random.split(jax.random.key(seed), 14)
    return {
        "tokens": normal_values(arg_keys[0], (TOKENS, D), 1.0, 6.0, ((0, 32),)),
        "w_query": normal_values(arg_keys[1], (D, D), (D // 4) ** -0.5, 0.5, ((0, 16),)),
        "w_key": normal_values(arg_keys[2], (D, D), D ** -0.5, 0.25, ((0, 16),)),
        "w_value": normal_values(arg_keys[3], (D, D), D ** -0.5, 0.25, ((0, 16),)),
        "w_control": normal_values(arg_keys[4], (D, H * SLOTS), (D // 4) ** -0.5, 0.5, ((0, 16),)),
        "w_out": normal_values(arg_keys[5], (D, D), (D // 8) ** -0.5, 0.75, ((0, 16),)),
        "w_up": normal_values(arg_keys[6], (D, FF), D ** -0.5, 0.25, ((0, 16),)),
        "w_down": normal_values(arg_keys[7], (FF, D), (FF // 2) ** -0.5, 0.1875, ((0, 16),)),
        "gain_attn": jnp.clip(1.0 + 0.1 * jax.random.normal(arg_keys[8], (D,), jnp.float32), 0.5, 1.5).astype(jnp.bfloat16),
        "gain_ffn": jnp.clip(1.0 + 0.1 * jax.random.normal(arg_keys[9], (D,), jnp.float32), 0.5, 1.5).astype(jnp.bfloat16),
        "bias_up": normal_values(arg_keys[10], (FF,), 0.5, 3.0, ((0, 16),)),
        "bias_down": normal_values(arg_keys[11], (D,), 0.5, 3.0, ((0, 16),)),
        "cotangent": gaussian_with(arg_keys[12], (TOKENS, D), 1.0, 6.0, ((0, 32),), (0, 1, 32, 2.75)),
    }


exact_precision = lax.Precision.HIGHEST

@jax.custom_vjp
def low(v):
    return lax.optimization_barrier(v.astype(jnp.bfloat16)).astype(jnp.float32)

@jax.custom_vjp
def low_back(v):
    return v

def low_keep(v):
    return (low(v), None)

def low_pass(kept, grad):
    return (grad,)

def back_keep(v):
    return (v, None)

def back_low(kept, grad):
    return (low(grad),)
low.defvjp(low_keep, low_pass)
low_back.defvjp(back_keep, back_low)

def normalize(source):
    average = lax.optimization_barrier(jnp.mean(source, axis=-1, keepdims=True))
    centred = source - average
    spread = lax.optimization_barrier(jnp.mean(centred * centred, axis=-1, keepdims=True))
    return centred * lax.rsqrt(spread + 1e-05)

def mix_block(carry, block):
    memory_slot_keys, memory_slot_values, totals = carry
    block_rows = block.shape[0]
    query_segment = block[:, :, 0:HEAD]
    key_segment = block[:, :, HEAD:2 * HEAD]
    value_segment = block[:, :, 2 * HEAD:3 * HEAD]
    stored_entries = jnp.exp(block[:, :, 3 * HEAD:3 * HEAD + SLOTS])
    places = jnp.arange(block_rows)
    lower_mask = (places[:, None] >= places[None, :]).astype(jnp.float32)
    pair_scores = jnp.einsum('thd,ihd->hti', query_segment, key_segment, precision=exact_precision) * lower_mask[None]
    running = jnp.einsum('ti,ihm->thm', lower_mask, stored_entries, precision=exact_precision) + totals[None]
    fraction_top = jnp.einsum('hti,ihm->thm', pair_scores, stored_entries, precision=exact_precision)
    fraction_top = fraction_top + jnp.einsum('aek,exk->aex', query_segment, memory_slot_keys, precision=exact_precision)
    slot_score = fraction_top * HEAD ** (-0.5) / running
    read_weight = jax.nn.softmax(slot_score, axis=-1)
    weight_scaled_rows = read_weight / running
    recall = jnp.einsum('thm,ihm->hti', weight_scaled_rows, stored_entries, precision=exact_precision) * lower_mask[None]
    output_segment = jnp.einsum('hti,ihd->thd', recall, value_segment, precision=exact_precision)
    output_segment = output_segment + jnp.einsum('jkx,kxo->jko', weight_scaled_rows, memory_slot_values, precision=exact_precision)
    memory_slot_keys = memory_slot_keys + jnp.einsum('uwz,uwq->wzq', stored_entries, key_segment, precision=exact_precision)
    memory_slot_values = memory_slot_values + jnp.einsum('uwz,uwq->wzq', stored_entries, value_segment, precision=exact_precision)
    totals = totals + lax.optimization_barrier(jnp.sum(stored_entries, axis=0))
    return ((memory_slot_keys, memory_slot_values, totals), output_segment)

def mixer(packed):
    length, heads, width = packed.shape
    block_rows = min(512, length)
    blocks = packed.reshape(length // block_rows, block_rows, heads, width)
    start = (jnp.zeros((heads, SLOTS, HEAD), jnp.float32), jnp.zeros((heads, SLOTS, HEAD), jnp.float32), jnp.zeros((heads, SLOTS), jnp.float32))
    _, outputs = lax.scan(jax.checkpoint(mix_block), start, blocks)
    return outputs.reshape(length, heads, HEAD)

def layer(source, w_query, w_key, w_value, w_control, w_out, w_up, w_down, gain_attn, gain_ffn, bias_up, bias_down):
    count = source.shape[0]
    attn_input = low(normalize(source) * gain_attn)

    def project(weight, width):
        return low(low_back(jnp.dot(attn_input, weight, precision=exact_precision))).reshape(count, H, width)
    packed = jnp.concatenate([project(w_query, HEAD), project(w_key, HEAD), project(w_value, HEAD), project(w_control, SLOTS)], axis=2)
    groups = count // LEN
    mixed = jax.vmap(mixer)(packed.reshape(groups, LEN, H, 3 * HEAD + SLOTS)).reshape(count, D)
    mixed = low_back(low(mixed))
    branch = low_back(jnp.dot(mixed, w_out, precision=exact_precision))
    resid = source + branch
    ffn_input = low(normalize(resid) * gain_ffn)
    pre_act = low_back(jnp.dot(ffn_input, w_up, precision=exact_precision) + bias_up)
    hidden = low(jax.nn.silu(pre_act))
    return resid + (jnp.dot(hidden, w_down, precision=exact_precision) + bias_down)

def reference(tokens, w_query, w_key, w_value, w_control, w_out, w_up, w_down, gain_attn, gain_ffn, bias_up, bias_down, cotangent):
    params = tuple((p.astype(jnp.float32) for p in (w_query, w_key, w_value, w_control, w_out, w_up, w_down, gain_attn, gain_ffn, bias_up, bias_down)))
    group = math.gcd(SEQS, max(1, 4096 // LEN))
    turns = SEQS // group
    inputs = tokens.astype(jnp.float32).reshape(turns, group * LEN, D)
    cotangents = cotangent.astype(jnp.float32).reshape(turns, group * LEN, D)

    def one_turn(totals, pair):
        source, grad_out = pair
        result, pull = jax.vjp(layer, source, *params)
        grads = pull(grad_out)
        totals = tuple((a + b for a, b in zip(totals, grads[1:])))
        return (totals, (result.astype(jnp.bfloat16), grads[0]))
    zeros = tuple((jnp.zeros_like(p) for p in params))
    totals, (results, grad_in) = lax.scan(one_turn, zeros, (inputs, cotangents))
    return (results.reshape(TOKENS, D), grad_in.reshape(TOKENS, D), totals[0], totals[1], totals[2], totals[3], totals[4], totals[5], totals[6], totals[7], totals[8], totals[9], totals[10])
```

```python
from functools import partial
import jax
import jax.numpy as jnp
from jax import lax
from jax.experimental import pallas as pl
from jax.experimental.pallas import tpu as pltpu
from jax.sharding import PartitionSpec as P

F32 = jnp.float32
BF16 = jnp.bfloat16
HEAD = 64
QUAD = 256
SCALE = HEAD ** -0.5
CHUNK = 128
VMEM_LIMIT = 60 * 1024 * 1024


def mm(a, b):
    return lax.dot_general(a, b, (((1,), (0,)), ((), ())), preferred_element_type=F32)


def mm_t(a, b):
    return lax.dot_general(a, b, (((1,), (1,)), ((), ())), preferred_element_type=F32)


def t_mm(a, b):
    return lax.dot_general(a, b, (((0,), (0,)), ((), ())), preferred_element_type=F32)


def iota(shape, dim):
    return lax.broadcasted_iota(jnp.int32, shape, dim)


def normalize(x):
    centred = x - jnp.mean(x, axis=-1, keepdims=True)
    spread = jnp.mean(centred * centred, axis=-1, keepdims=True)
    factor = lax.rsqrt(spread + 1e-05)
    return centred * factor, factor


def norm_back(g, normed, factor):
    first = jnp.mean(g, axis=-1, keepdims=True)
    second = jnp.mean(g * normed, axis=-1, keepdims=True)
    return factor * (g - first - normed * second)


def blocks_of(x):
    lane = iota(x.shape, 1) // HEAD
    zero = jnp.zeros_like(x)
    return jnp.concatenate([jnp.where(lane == h, x, zero) for h in range(4)], axis=0)


def tri(x, lower):
    c = x.shape[0]
    row, col = iota(x.shape, 0), iota(x.shape, 1) % c
    keep = row >= col if lower else row <= col
    return jnp.where(keep, x, 0.0).astype(BF16)


def per_head(x, op, neutral):
    parts = []
    for p in range(x.shape[1] // 128):
        v = x[:, p * 128 : (p + 1) * 128]
        low = iota(v.shape, 1) < HEAD
        a = op(jnp.where(low, v, neutral), axis=-1, keepdims=True)
        b = op(jnp.where(low, neutral, v), axis=-1, keepdims=True)
        parts.append(jnp.where(low, a, b))
    return jnp.concatenate(parts, axis=1)


def head_square():
    return iota((QUAD, QUAD), 0) // HEAD == iota((QUAD, QUAD), 1) // HEAD


STATE = 2 * HEAD + 8


def store_state(st_ref, first, second, total):
    square = head_square()
    for g in range(st_ref.shape[0]):
        for k, ref in enumerate((first, second)):
            x = jnp.where(square, ref[g], 0.0)
            st_ref[g, k * HEAD : (k + 1) * HEAD, :] = x[0:64] + x[64:128] + x[128:192] + x[192:256]
        st_ref[g, 2 * HEAD :, :] = jnp.broadcast_to(total[0:1, g * QUAD : (g + 1) * QUAD], (8, QUAD))


def load_state(st_ref, first, second, total):
    square = head_square()
    for g in range(st_ref.shape[0]):
        for k, ref in enumerate((first, second)):
            x = st_ref[g, k * HEAD : (k + 1) * HEAD, :]
            ref[g] = jnp.where(square, jnp.concatenate([x] * 4, axis=0), 0.0)
        total[:, g * QUAD : (g + 1) * QUAD] = st_ref[g, 2 * HEAD :, :]


def hi_lo(x):
    hi = x.astype(BF16)
    return hi, (x - hi.astype(F32)).astype(BF16)


def spread_vector(vecs, me, n, r, k, each, total):
    pick = (iota((n, n * r), 1) == iota((n, n * r), 0) * r + k).astype(BF16)
    rows = mm(pick, vecs).astype(BF16)
    tile = (iota((128, total), 1) % each == iota((128, total), 0)).astype(BF16)
    wide = mm(rows, tile)
    own = iota((n, total), 1) // each == (iota((n, total), 0) ^ me)
    return jnp.sum(jnp.where(own, wide, 0.0), axis=0, keepdims=True)


def gather_vector(vec, me, n, each):
    total = vec.shape[1]
    own = iota((n, total), 1) // each == (iota((n, total), 0) ^ me)
    wide = jnp.where(own, vec, 0.0).astype(BF16)
    tile = (iota((128, total), 1) % each == iota((128, total), 0)).astype(BF16)
    return mm_t(wide, tile).astype(BF16)


def project_kernel(n, r, me_ref, tok_ref, *refs):
    pieces = refs[:n]
    att_ref, pack_ref, st_ref, w_ref, vec_out, kt_ref, mv_ref, tot_ref, vecs, sems, vsems = refs[n:]
    d = w_ref.shape[0]
    wide = w_ref.shape[1]
    me = me_ref[0]

    @pl.when(pl.program_id(0) == 0)
    def _():
        copies = []
        for j in range(n):
            at = pl.multiple_of((me ^ j) * r, r)
            copies.append(pltpu.make_async_copy(pieces[j].at[:, pl.ds(0, wide)], w_ref.at[pl.ds(at, r), :], sems.at[j]))
            copies.append(pltpu.make_async_copy(pieces[j].at[:, pl.ds(wide, 128)], vecs.at[pl.ds(j * r, r), :], vsems.at[j]))
        for c in copies:
            c.start()
        kt_ref[...] = jnp.zeros_like(kt_ref)
        mv_ref[...] = jnp.zeros_like(mv_ref)
        tot_ref[...] = jnp.zeros_like(tot_ref)
        for c in copies:
            c.wait()
        vec_out[...] = vecs[...]

    gain = spread_vector(vecs[...], me, n, r, 0, r, d)
    normed, _ = normalize(tok_ref[...].astype(F32))
    att = (normed * gain).astype(BF16)
    att_ref[...] = att
    cols = []
    for p in range(4):
        full = mm(att, w_ref[:, p * d : (p + 1) * d]).astype(BF16)
        pack_ref[:, p * d : (p + 1) * d] = full
        cols.append(full)
    written = jnp.exp(cols[3].astype(F32)).astype(BF16)
    for g in range(d // QUAD):
        s = slice(g * QUAD, (g + 1) * QUAD)
        kt_ref[g] += t_mm(cols[1][:, s], written[:, s])
        mv_ref[g] += t_mm(written[:, s], cols[2][:, s])
    tot_ref[0:1, :] += jnp.sum(written.astype(F32), axis=0, keepdims=True)

    @pl.when(pl.program_id(0) == pl.num_programs(0) - 1)
    def _():
        store_state(st_ref, kt_ref, mv_ref, tot_ref)


def project(me, tokens, pieces, rows=256):
    t, d = tokens.shape
    n = len(pieces)
    r = pieces[0].shape[0]
    wide = 4 * d
    g = d // QUAD
    const = lambda *shape: pl.BlockSpec(shape, lambda i: (0,) * len(shape))
    return pl.pallas_call(
        partial(project_kernel, n, r),
        grid=(t // rows,),
        in_specs=[pl.BlockSpec(memory_space=pltpu.SMEM), pl.BlockSpec((rows, d), lambda i: (i, 0))]
        + [pl.BlockSpec(memory_space=pl.ANY)] * n,
        out_specs=[
            pl.BlockSpec((rows, d), lambda i: (i, 0)),
            pl.BlockSpec((rows, wide), lambda i: (i, 0)),
            const(g, STATE, QUAD),
            const(d, wide),
            const(n * r, 128),
        ],
        out_shape=[
            jax.ShapeDtypeStruct((t, d), BF16),
            jax.ShapeDtypeStruct((t, wide), BF16),
            jax.ShapeDtypeStruct((g, STATE, QUAD), F32),
            jax.ShapeDtypeStruct((d, wide), BF16),
            jax.ShapeDtypeStruct((n * r, 128), BF16),
        ],
        scratch_shapes=[
            pltpu.VMEM((g, QUAD, QUAD), F32),
            pltpu.VMEM((g, QUAD, QUAD), F32),
            pltpu.VMEM((8, d), F32),
            pltpu.VMEM((n * r, 128), BF16),
            pltpu.SemaphoreType.DMA((n,)),
            pltpu.SemaphoreType.DMA((n,)),
        ],
        compiler_params=pltpu.CompilerParams(vmem_limit_bytes=VMEM_LIMIT),
        cost_estimate=pl.CostEstimate(flops=2 * t * d * wide, bytes_accessed=12 << 20, transcendentals=t * d),
        name="project",
    )(me, tokens, *pieces)


def mix_kernel(pack_ref, st_in, mix_ref, read_ref, score_ref, inv_ref, kts_ref, mvs_ref, kt, mv, tot):
    d = mix_ref.shape[1]
    rows = mix_ref.shape[0]

    @pl.when(pl.program_id(0) == 0)
    def _():
        load_state(st_in, kt, mv, tot)

    c = CHUNK
    square = head_square()
    ones = (iota((c, c), 0) >= iota((c, c), 1)).astype(BF16)
    for b in range(rows // c):
        rr = slice(b * c, (b + 1) * c)
        for g in range(d // QUAD):
            s = slice(g * QUAD, (g + 1) * QUAD)
            q, k, v, u = (pack_ref[rr, p * d + g * QUAD : p * d + (g + 1) * QUAD] for p in range(4))
            written = jnp.exp(u.astype(F32)).astype(BF16)
            wb = blocks_of(written)
            pairs = tri(mm_t(q, blocks_of(k)), True)
            ktb, mvb = kt[g].astype(BF16), mv[g].astype(BF16)
            kts_ref[b, g] = ktb
            mvs_ref[b, g] = mvb
            top = mm(pairs, wb) + mm(q, ktb)
            total = mm(ones, written) + tot[0:1, s]
            inv = 1.0 / total
            score = top * SCALE * inv
            e = jnp.exp(score - per_head(score, jnp.max, -jnp.inf))
            read = e / per_head(e, jnp.sum, 0.0)
            scaled = (read * inv).astype(BF16)
            recall = tri(mm_t(scaled, wb), True)
            out = mm(recall, blocks_of(v)) + mm(scaled, mvb)
            mix_ref[rr, s] = out.astype(BF16)
            read_ref[rr, s] = read
            score_ref[rr, s] = score
            inv_ref[rr, s] = inv
            kt[g] += jnp.where(square, t_mm(k, written), 0.0)
            mv[g] += jnp.where(square, t_mm(written, v), 0.0)
            tot[0:1, s] = total[c - 1 : c, :]


def mix(packed, state, rows=256):
    t, wide = packed.shape
    d = wide // 4
    g = d // QUAD
    const = lambda *shape: pl.BlockSpec(shape, lambda i: (0,) * len(shape))
    per = rows // CHUNK
    row = lambda w: pl.BlockSpec((rows, w), lambda i: (i, 0))
    return pl.pallas_call(
        mix_kernel,
        grid=(t // rows,),
        in_specs=[row(wide), const(g, STATE, QUAD)],
        out_specs=[row(d)] * 4 + [pl.BlockSpec((per, g, QUAD, QUAD), lambda i: (i, 0, 0, 0))] * 2,
        out_shape=[jax.ShapeDtypeStruct((t, d), BF16)] + [jax.ShapeDtypeStruct((t, d), F32)] * 3
        + [jax.ShapeDtypeStruct((t // CHUNK, g, QUAD, QUAD), BF16)] * 2,
        scratch_shapes=[pltpu.VMEM((g, QUAD, QUAD), F32), pltpu.VMEM((g, QUAD, QUAD), F32), pltpu.VMEM((8, d), F32)],
        compiler_params=pltpu.CompilerParams(vmem_limit_bytes=VMEM_LIMIT),
        cost_estimate=pl.CostEstimate(flops=6 * 10**9, bytes_accessed=16 << 20, transcendentals=2 * t * d),
        name="mix",
    )(packed, state)


def ffn_kernel(n, r, me_ref, vec_ref, mixed_ref, tok_ref, cot_ref, *refs):
    pieces = refs[:n]
    out_ref, gres_ref, gmix_ref, even_ref, odd_ref = refs[n : n + 5]
    w_out, w_up, w_down, hid, gpre, fin, gbr, grads, sems, osems = refs[n + 5 :]
    t, d = mixed_ref.shape
    ff = w_up.shape[1]
    me = me_ref[0]
    mult = ff // d
    copies = []
    for j in range(n):
        own = me ^ j
        at = pl.multiple_of(own * r, r)
        copies.append(pltpu.make_async_copy(pieces[j].at[:, pl.ds(0, ff)], w_up.at[pl.ds(at, r), :], sems.at[0, j]))
        for m in range(mult):
            to = pl.multiple_of(own * r * mult + m * r, r)
            copies.append(
                pltpu.make_async_copy(pieces[j].at[:, pl.ds(ff + m * d, d)], w_down.at[pl.ds(to, r), :], sems.at[2 + m, j])
            )
        copies.append(pltpu.make_async_copy(pieces[j].at[:, pl.ds(2 * ff, d)], w_out.at[pl.ds(at, r), :], sems.at[1, j]))
    for c in copies:
        c.start()
    vecs = vec_ref[...]
    gain = spread_vector(vecs, me, n, r, 1, r, d)
    b_up = spread_vector(vecs, me, n, r, 2, r * mult, ff)
    b_down = spread_vector(vecs, me, n, r, 3, r, d)
    for c in copies:
        c.wait()

    rows = 256
    part = 512
    zero = jnp.zeros((1, d), F32)

    def body(i, carry):
        ggain, gbup, gbdown = carry
        at = pl.multiple_of(i * rows, rows)
        rs = pl.ds(at, rows)
        cot = cot_ref[rs, :]
        cotf = cot.astype(F32)
        resid = tok_ref[rs, :].astype(F32) + mm(mixed_ref[rs, :], w_out[...])
        normed, factor = normalize(resid)
        ffn_in = (normed * gain).astype(BF16)
        fin[rs, :] = ffn_in
        total = jnp.zeros((rows, d), F32)
        gin = jnp.zeros((rows, d), F32)
        sums = []
        for p in range(ff // part):
            ps = slice(p * part, (p + 1) * part)
            pre = mm(ffn_in, w_up[:, ps]) + b_up[:, ps]
            sig = 1.0 / (1.0 + jnp.exp(-pre))
            hidden = (pre * sig).astype(BF16)
            hid[rs, ps] = hidden
            total += mm(hidden, w_down[ps, :])
            gh = mm_t(cot, w_down[ps, :])
            gp = (gh * (sig * (1.0 + pre * (1.0 - sig)))).astype(BF16)
            gpre[rs, ps] = gp
            sums.append(jnp.sum(gp.astype(F32), axis=0, keepdims=True))
            gin += mm_t(gp, w_up[:, ps])
        out_ref[rs, :] = (resid + (total + b_down)).astype(BF16)
        gres = cotf + norm_back(gin * gain, normed, factor)
        gres_ref[rs, :] = gres
        gb = gres.astype(BF16)
        gbr[rs, :] = gb
        gmix_ref[rs, :] = mm_t(gb, w_out[...]).astype(BF16)
        return (
            ggain + jnp.sum(gin * normed, axis=0, keepdims=True),
            gbup + jnp.concatenate(sums, axis=1),
            gbdown + jnp.sum(cotf, axis=0, keepdims=True),
        )

    ggain, gbup, gbdown = lax.fori_loop(0, t // rows, body, (zero, jnp.zeros((1, ff), F32), zero))
    for p in range(ff // part):
        ps = slice(p * part, (p + 1) * part)
        w_up[:, ps] = t_mm(fin[...], gpre[:, ps]).astype(BF16)
        w_down[ps, :] = t_mm(hid[:, ps], cot_ref[...]).astype(BF16)
    w_out[...] = t_mm(mixed_ref[...], gbr[...]).astype(BF16)
    va = gather_vector(ggain, me, n, r)
    vb = gather_vector(gbup, me, n, r * mult)
    vc = gather_vector(gbdown, me, n, r)
    row = iota((n, r, 128), 1)
    grads[...] = jnp.where(
        row == 1, va[:, None, :].astype(F32),
        jnp.where(row == 2, vb[:, None, :].astype(F32), jnp.where(row == 3, vc[:, None, :].astype(F32), 0.0)),
    ).astype(BF16)
    outs = []
    for j in range(n):
        own = me ^ j
        at = pl.multiple_of(own * r, r)
        dst = (odd_ref if j % 2 else even_ref).at[j // 2]
        outs.append(pltpu.make_async_copy(w_up.at[pl.ds(at, r), :], dst.at[:, pl.ds(0, ff)], osems.at[0, j]))
        for m in range(mult):
            frm = pl.multiple_of(own * r * mult + m * r, r)
            outs.append(
                pltpu.make_async_copy(w_down.at[pl.ds(frm, r), :], dst.at[:, pl.ds(ff + m * d, d)], osems.at[3 + m, j])
            )
        outs.append(pltpu.make_async_copy(w_out.at[pl.ds(at, r), :], dst.at[:, pl.ds(2 * ff, d)], osems.at[1, j]))
        outs.append(pltpu.make_async_copy(grads.at[j], dst.at[:, pl.ds(2 * ff + d, 128)], osems.at[2, j]))
    for c in outs:
        c.start()
    for c in outs:
        c.wait()


def ffn(me, vecs, mixed, tokens, cot, pieces, ff):
    t, d = tokens.shape
    n = len(pieces)
    r = pieces[0].shape[0]
    whole = pl.BlockSpec(memory_space=pltpu.VMEM)
    hbm = pl.BlockSpec(memory_space=pl.ANY)
    width = 2 * ff + d + 128
    mult = ff // d
    return pl.pallas_call(
        partial(ffn_kernel, n, r),
        in_specs=[pl.BlockSpec(memory_space=pltpu.SMEM)] + [whole] * 4 + [hbm] * n,
        out_specs=[whole] * 3 + [hbm] * 2,
        out_shape=[
            jax.ShapeDtypeStruct((t, d), BF16),
            jax.ShapeDtypeStruct((t, d), F32),
            jax.ShapeDtypeStruct((t, d), BF16),
            jax.ShapeDtypeStruct((n // 2, r, width), BF16),
            jax.ShapeDtypeStruct((n // 2, r, width), BF16),
        ],
        scratch_shapes=[
            pltpu.VMEM((d, d), BF16),
            pltpu.VMEM((d, ff), BF16),
            pltpu.VMEM((ff, d), BF16),
            pltpu.VMEM((t, ff), BF16),
            pltpu.VMEM((t, ff), BF16),
            pltpu.VMEM((t, d), BF16),
            pltpu.VMEM((t, d), BF16),
            pltpu.VMEM((n, r, 128), BF16),
            pltpu.SemaphoreType.DMA((2 + mult, n)),
            pltpu.SemaphoreType.DMA((3 + mult, n)),
        ],
        compiler_params=pltpu.CompilerParams(vmem_limit_bytes=VMEM_LIMIT),
        cost_estimate=pl.CostEstimate(flops=12 * t * d * ff, bytes_accessed=20 << 20, transcendentals=t * ff),
        name="ffn",
    )(me, vecs, mixed, tokens, cot, *pieces)


def read_back_kernel(pack_ref, gmix_ref, read_ref, score_ref, inv_ref, kts_ref, mvs_ref,
                     gq_ref, a_ref, u_ref, gtot_ref, st_ref, gk_ref, gv_ref, gt_ref):
    rows, d = gmix_ref.shape

    @pl.when(pl.program_id(0) == 0)
    def _():
        gk_ref[...] = jnp.zeros_like(gk_ref)
        gv_ref[...] = jnp.zeros_like(gv_ref)
        gt_ref[...] = jnp.zeros_like(gt_ref)

    c = CHUNK
    for b in range(rows // c):
        rr = slice(b * c, (b + 1) * c)
        for g in range(d // QUAD):
            s = slice(g * QUAD, (g + 1) * QUAD)
            q, k, v, w = (pack_ref[rr, p * d + g * QUAD : p * d + (g + 1) * QUAD] for p in range(4))
            written = jnp.exp(w.astype(F32)).astype(BF16)
            wb = blocks_of(written)
            gm = gmix_ref[rr, s]
            read, score, inv = read_ref[rr, s], score_ref[rr, s], inv_ref[rr, s]
            gpair = tri(mm_t(gm, blocks_of(v)), True)
            gread = (mm(gpair, wb) + mm_t(gm, mvs_ref[b, g])) * inv
            weighted = read * gread
            gscore = weighted - read * per_head(weighted, jnp.sum, 0.0)
            a = (gscore * inv * SCALE).astype(BF16)
            u = (read * inv).astype(BF16)
            gtot = (gscore * score + weighted) * inv
            spair = tri(mm_t(a, wb), True)
            gq_ref[rr, s] = (mm(spair, blocks_of(k)) + mm_t(a, kts_ref[b, g])).astype(BF16)
            a_ref[rr, s] = a
            u_ref[rr, s] = u
            gtot_ref[rr, s] = gtot
            gk_ref[g] += t_mm(a, q)
            gv_ref[g] += t_mm(u, gm)
            gt_ref[0:1, s] += jnp.sum(gtot, axis=0, keepdims=True)

    @pl.when(pl.program_id(0) == pl.num_programs(0) - 1)
    def _():
        store_state(st_ref, gk_ref, gv_ref, gt_ref)


def read_back(packed, gmix, read, score, inv, kts, mvs, rows=256):
    t, wide = packed.shape
    d = wide // 4
    g = d // QUAD
    const = lambda *shape: pl.BlockSpec(shape, lambda i: (0,) * len(shape))
    per = rows // CHUNK
    row = lambda w: pl.BlockSpec((rows, w), lambda i: (i, 0))
    st = pl.BlockSpec((per, g, QUAD, QUAD), lambda i: (i, 0, 0, 0))
    return pl.pallas_call(
        read_back_kernel,
        grid=(t // rows,),
        in_specs=[row(wide), row(d), row(d), row(d), row(d), st, st],
        out_specs=[row(d)] * 4 + [const(g, STATE, QUAD)],
        out_shape=[jax.ShapeDtypeStruct((t, d), BF16)] * 3 + [jax.ShapeDtypeStruct((t, d), F32)]
        + [jax.ShapeDtypeStruct((g, STATE, QUAD), F32)],
        scratch_shapes=[pltpu.VMEM((g, QUAD, QUAD), F32), pltpu.VMEM((g, QUAD, QUAD), F32), pltpu.VMEM((8, d), F32)],
        compiler_params=pltpu.CompilerParams(vmem_limit_bytes=VMEM_LIMIT),
        cost_estimate=pl.CostEstimate(flops=6 * 10**9, bytes_accessed=20 << 20, transcendentals=t * d),
        name="read_back",
    )(packed, gmix, read, score, inv, kts, mvs)


def write_back_kernel(pack_ref, gmix_ref, a_ref, u_ref, gtot_ref, st_in, out_ref, gk, gv, gt):
    rows, d = gmix_ref.shape

    @pl.when(pl.program_id(0) == 0)
    def _():
        load_state(st_in, gk, gv, gt)

    c = CHUNK
    square = head_square()
    ones = (iota((c, c), 0) <= iota((c, c), 1)).astype(BF16)
    for b in reversed(range(rows // c)):
        rr = slice(b * c, (b + 1) * c)
        for g in range(d // QUAD):
            s = slice(g * QUAD, (g + 1) * QUAD)
            q, k, v, w = (pack_ref[rr, p * d + g * QUAD : p * d + (g + 1) * QUAD] for p in range(4))
            wf = jnp.exp(w.astype(F32))
            written = wf.astype(BF16)
            gm, a, u = gmix_ref[rr, s], a_ref[rr, s], u_ref[rr, s]
            gtot = gtot_ref[rr, s]
            hi, lo = hi_lo(gtot)
            after = mm(ones, hi) + mm(ones, lo) + gt[0:1, s]
            qb, gb, ab, ub = blocks_of(q), blocks_of(gm), blocks_of(a), blocks_of(u)
            gkb, gvb = gk[g].astype(BF16), gv[g].astype(BF16)
            pt = tri(mm_t(k, qb), False)
            gp = tri(mm_t(v, gb), False)
            st = tri(mm_t(written, ab), False)
            rt = tri(mm_t(written, ub), False)
            gw = mm(pt, ab) + mm(gp, ub) + mm_t(k, gkb) + mm_t(v, gvb)
            gkey = mm(st, qb) + mm(written, gkb)
            gval = mm(rt, gb) + mm(written, gvb)
            out_ref[rr, g * QUAD : (g + 1) * QUAD] = gkey.astype(BF16)
            out_ref[rr, d + g * QUAD : d + (g + 1) * QUAD] = gval.astype(BF16)
            out_ref[rr, 2 * d + g * QUAD : 2 * d + (g + 1) * QUAD] = (wf * (gw - after)).astype(BF16)
            gk[g] += jnp.where(square, t_mm(a, q), 0.0)
            gv[g] += jnp.where(square, t_mm(u, gm), 0.0)
            gt[0:1, s] = after[0:1, :]


def write_back(packed, gmix, a, u, gtot, state, rows=256):
    t, wide = packed.shape
    d = wide // 4
    g = d // QUAD
    last = t // rows - 1
    const = lambda *shape: pl.BlockSpec(shape, lambda i: (0,) * len(shape))
    row = lambda w: pl.BlockSpec((rows, w), lambda i: (last - i, 0))
    return pl.pallas_call(
        write_back_kernel,
        grid=(t // rows,),
        in_specs=[row(wide), row(d), row(d), row(d), row(d), const(g, STATE, QUAD)],
        out_specs=row(3 * d),
        out_shape=jax.ShapeDtypeStruct((t, 3 * d), BF16),
        scratch_shapes=[pltpu.VMEM((g, QUAD, QUAD), F32), pltpu.VMEM((g, QUAD, QUAD), F32), pltpu.VMEM((8, d), F32)],
        compiler_params=pltpu.CompilerParams(vmem_limit_bytes=VMEM_LIMIT),
        cost_estimate=pl.CostEstimate(flops=9 * 10**9, bytes_accessed=16 << 20, transcendentals=t * d),
        name="write_back",
    )(packed, gmix, a, u, gtot, state)


def weight_grad_kernel(n, r, me_ref, att_ref, gq_ref, gkvc_ref, even_ref, odd_ref, acc, sems):
    d = att_ref.shape[1]
    me = me_ref[0]
    acc[:, 0:d] = t_mm(att_ref[...], gq_ref[...]).astype(BF16)
    for p in range(3):
        acc[:, (p + 1) * d : (p + 2) * d] = t_mm(att_ref[...], gkvc_ref[:, p * d : (p + 1) * d]).astype(BF16)
    outs = []
    for j in range(n):
        at = pl.multiple_of((me ^ j) * r, r)
        dst = (odd_ref if j % 2 else even_ref).at[j // 2]
        outs.append(pltpu.make_async_copy(acc.at[pl.ds(at, r), :], dst, sems.at[j]))
    for c in outs:
        c.start()
    for c in outs:
        c.wait()


def weight_grad(me, att, gq, gkvc, n):
    t, d = att.shape
    r = d // n
    whole = pl.BlockSpec(memory_space=pltpu.VMEM)
    hbm = pl.BlockSpec(memory_space=pl.ANY)
    return pl.pallas_call(
        partial(weight_grad_kernel, n, r),
        in_specs=[pl.BlockSpec(memory_space=pltpu.SMEM)] + [whole] * 3,
        out_specs=[hbm] * 2,
        out_shape=[jax.ShapeDtypeStruct((n // 2, r, 4 * d), BF16)] * 2,
        scratch_shapes=[pltpu.VMEM((d, 4 * d), BF16), pltpu.SemaphoreType.DMA((n,))],
        compiler_params=pltpu.CompilerParams(vmem_limit_bytes=VMEM_LIMIT),
        cost_estimate=pl.CostEstimate(flops=8 * t * d * d, bytes_accessed=7 << 20, transcendentals=0),
        name="weight_grad",
    )(me, att, gq, gkvc)


def input_grad_kernel(n, r, me_ref, vec_ref, tok_ref, gq_ref, gkvc_ref, w_ref, gres_ref, out_ref):
    d = tok_ref.shape[1]
    gain = spread_vector(vec_ref[...], me_ref[0], n, r, 0, r, d)
    gin = mm_t(gq_ref[...], w_ref[:, 0:d]) + mm_t(gkvc_ref[...], w_ref[:, d:])
    normed, factor = normalize(tok_ref[...].astype(F32))
    out_ref[...] = gres_ref[...] + norm_back(gin * gain, normed, factor)


def input_grad(me, vecs, tokens, gq, gkvc, w, gres, n, rows=256):
    t, d = tokens.shape
    r = d // n
    const = lambda *shape: pl.BlockSpec(shape, lambda i: (0,) * len(shape))
    row = lambda w: pl.BlockSpec((rows, w), lambda i: (i, 0))
    return pl.pallas_call(
        partial(input_grad_kernel, n, r),
        grid=(t // rows,),
        in_specs=[pl.BlockSpec(memory_space=pltpu.SMEM), const(n * r, 128), row(d), row(d), row(3 * d), const(d, 4 * d), row(d)],
        out_specs=row(d),
        out_shape=jax.ShapeDtypeStruct((t, d), F32),
        compiler_params=pltpu.CompilerParams(vmem_limit_bytes=VMEM_LIMIT),
        cost_estimate=pl.CostEstimate(flops=8 * t * d * d, bytes_accessed=12 << 20, transcendentals=0),
        name="input_grad",
    )(me, vecs, tokens, gq, gkvc, w, gres)


def swap(x, mask, n):
    return lax.ppermute(x, "fsdp", [(i, i ^ mask) for i in range(n)])


def gather(shard, n):
    even = [shard] + [swap(shard, 2 * i, n) for i in range(1, n // 2)]
    odd = [swap(x, 1, n) for x in even]
    return [x for pair in zip(even, odd) for x in pair]


def scatter_sum(even, odd, n, seqs):
    mine = (even.astype(F32) + swap(odd, 1, n).astype(F32)).astype(BF16)
    parts = [mine[0]] + [swap(mine[i], 2 * i, n) for i in range(1, n // 2)]
    total = sum(p.astype(F32) for p in parts)
    step = 1
    while step < seqs:
        total = total + lax.ppermute(total, "seq", [(i, i ^ step) for i in range(seqs)])
        step *= 2
    return total


def shift(x, by, seqs):
    return lax.ppermute(x, "seq", [(i, i + by) for i in range(seqs) if 0 <= i + by < seqs])


def others(state, direction, seqs):
    if seqs == 1:
        return jnp.zeros_like(state)
    total = shift(state, direction, seqs)
    step = 1
    while step < seqs - 1:
        total = total + shift(total, direction * step, seqs)
        step *= 2
    return total


def on_device(n, seqs, tokens, w_query, w_key, w_value, w_control, w_out, w_up, w_down,
              gain_attn, gain_ffn, bias_up, bias_down, cotangent):
    r, d = w_query.shape
    ff = w_up.shape[1]
    mult = ff // d
    me = lax.axis_index("fsdp").astype(jnp.int32).reshape(1)
    lanes = lambda v: jnp.pad(v, (0, 128 - v.shape[0]))
    vec = jnp.pad(jnp.stack([lanes(gain_attn), lanes(gain_ffn), lanes(bias_up), lanes(bias_down)]), ((0, r - 4), (0, 0)))
    first = jnp.concatenate([w_query, w_key, w_value, w_control, vec], axis=1)
    second = jnp.concatenate([w_up] + [w_down[m * r : (m + 1) * r] for m in range(mult)] + [w_out], axis=1)
    att_pieces = gather(first, n)
    ffn_pieces = gather(second, n)
    att, packed, state, w_att, vecs = project(me, tokens, att_pieces)
    mixed, read, score, inv, kts, mvs = mix(packed, others(state, 1, seqs))
    layer_out, gres, gmix, even, odd = ffn(me, vecs, mixed, tokens, cotangent, ffn_pieces, ff)
    ffn_share = scatter_sum(even, odd, n, seqs)
    gq, a, u, gtot, gstate = read_back(packed, gmix, read, score, inv, kts, mvs)
    gkvc = write_back(packed, gmix, a, u, gtot, others(gstate, -1, seqs))
    even, odd = weight_grad(me, att, gq, gkvc, n)
    grad_tokens = input_grad(me, vecs, tokens, gq, gkvc, w_att, gres, n)
    att_share = scatter_sum(even, odd, n, seqs)
    gain_share = jnp.sum(att_share * first[:, : 4 * d].astype(F32), axis=1) / gain_attn.astype(F32)
    up, down, out, vec = (
        ffn_share[:, :ff],
        ffn_share[:, ff : 2 * ff],
        ffn_share[:, 2 * ff : 2 * ff + d],
        ffn_share[:, 2 * ff + d :],
    )
    down = jnp.concatenate([down[:, m * d : (m + 1) * d] for m in range(mult)], axis=0)
    return (
        layer_out,
        grad_tokens,
        att_share[:, 0:d],
        att_share[:, d : 2 * d],
        att_share[:, 2 * d : 3 * d],
        att_share[:, 3 * d :],
        out,
        up,
        down,
        gain_share,
        vec[1, :r],
        vec[2, : r * mult],
        vec[3, :r],
    )


def solution(mesh):
    tokens = P(("fsdp", "seq"), None)
    matrix = P("fsdp", None)
    vector = P("fsdp")
    return jax.shard_map(
        partial(on_device, mesh.shape["fsdp"], mesh.shape["seq"]),
        mesh=mesh,
        in_specs=(tokens,) + (matrix,) * 7 + (vector,) * 4 + (tokens,),
        out_specs=(tokens, tokens) + (matrix,) * 7 + (vector,) * 4,
        check_vma=False,
    )
```

```python
from functools import partial
import jax
import jax.numpy as jnp
from jax import lax
from jax.experimental import pallas as pl
from jax.experimental.pallas import tpu as pltpu
from jax.sharding import PartitionSpec as P

F32 = jnp.float32
BF16 = jnp.bfloat16
HEAD = 64
QUAD = 256
SCALE = HEAD ** -0.5
CHUNK = 128
VMEM_LIMIT = 60 * 1024 * 1024


def mm(a, b):
    return lax.dot_general(a, b, (((1,), (0,)), ((), ())), preferred_element_type=F32)


def mm_t(a, b):
    return lax.dot_general(a, b, (((1,), (1,)), ((), ())), preferred_element_type=F32)


def t_mm(a, b):
    return lax.dot_general(a, b, (((0,), (0,)), ((), ())), preferred_element_type=F32)


def iota(shape, dim):
    return lax.broadcasted_iota(jnp.int32, shape, dim)


def normalize(x):
    centred = x - jnp.mean(x, axis=-1, keepdims=True)
    spread = jnp.mean(centred * centred, axis=-1, keepdims=True)
    factor = lax.rsqrt(spread + 1e-05)
    return centred * factor, factor


def norm_back(g, normed, factor):
    first = jnp.mean(g, axis=-1, keepdims=True)
    second = jnp.mean(g * normed, axis=-1, keepdims=True)
    return factor * (g - first - normed * second)


def blocks_of(x):
    lane = iota(x.shape, 1) // HEAD
    zero = jnp.zeros_like(x)
    return jnp.concatenate([jnp.where(lane == h, x, zero) for h in range(4)], axis=0)


def tri(x, lower):
    c = x.shape[0]
    row, col = iota(x.shape, 0), iota(x.shape, 1) % c
    keep = row >= col if lower else row <= col
    return jnp.where(keep, x, 0.0).astype(BF16)


def per_head(x, op, neutral):
    parts = []
    for p in range(x.shape[1] // 128):
        v = x[:, p * 128 : (p + 1) * 128]
        low = iota(v.shape, 1) < HEAD
        a = op(jnp.where(low, v, neutral), axis=-1, keepdims=True)
        b = op(jnp.where(low, neutral, v), axis=-1, keepdims=True)
        parts.append(jnp.where(low, a, b))
    return jnp.concatenate(parts, axis=1)


def head_square():
    return iota((QUAD, QUAD), 0) // HEAD == iota((QUAD, QUAD), 1) // HEAD


STATE = 2 * HEAD + 8


def store_state(st_ref, first, second, total):
    square = head_square()
    for g in range(st_ref.shape[0]):
        for k, ref in enumerate((first, second)):
            x = jnp.where(square, ref[g], 0.0)
            st_ref[g, k * HEAD : (k + 1) * HEAD, :] = x[0:64] + x[64:128] + x[128:192] + x[192:256]
        st_ref[g, 2 * HEAD :, :] = jnp.broadcast_to(total[0:1, g * QUAD : (g + 1) * QUAD], (8, QUAD))


def load_state(st_ref, first, second, total):
    square = head_square()
    for g in range(st_ref.shape[0]):
        for k, ref in enumerate((first, second)):
            x = st_ref[g, k * HEAD : (k + 1) * HEAD, :]
            ref[g] = jnp.where(square, jnp.concatenate([x] * 4, axis=0), 0.0)
        total[:, g * QUAD : (g + 1) * QUAD] = st_ref[g, 2 * HEAD :, :]


def hi_lo(x):
    hi = x.astype(BF16)
    return hi, (x - hi.astype(F32)).astype(BF16)


def spread_vector(vecs, me, n, r, k, each, total):
    pick = (iota((n, n * r), 1) == iota((n, n * r), 0) * r + k).astype(BF16)
    rows = mm(pick, vecs).astype(BF16)
    tile = (iota((128, total), 1) % each == iota((128, total), 0)).astype(BF16)
    wide = mm(rows, tile)
    own = iota((n, total), 1) // each == (iota((n, total), 0) ^ me)
    return jnp.sum(jnp.where(own, wide, 0.0), axis=0, keepdims=True)


def gather_vector(vec, me, n, each):
    total = vec.shape[1]
    own = iota((n, total), 1) // each == (iota((n, total), 0) ^ me)
    wide = jnp.where(own, vec, 0.0).astype(BF16)
    tile = (iota((128, total), 1) % each == iota((128, total), 0)).astype(BF16)
    return mm_t(wide, tile).astype(BF16)


def piece_refs(where, refs):
    return [refs[a] if row is None else refs[a].at[row] for a, row in where]


def pack_kernel(q, k, v, c, o, up, down, gain_a, gain_f, b_up, b_down, first, second):
    r, d = q.shape
    ff = up.shape[1]
    for p, ref in enumerate((q, k, v, c)):
        first[:, p * d : (p + 1) * d] = ref[...]
    tile = jnp.zeros((r, 128), F32)
    row, col = iota((r, 128), 0), iota((r, 128), 1)
    for i, ref in enumerate((gain_a, gain_f, b_up, b_down)):
        length = ref.shape[1]
        wide = jnp.broadcast_to(ref[...].astype(F32), (r, length))
        if length < 128:
            wide = jnp.concatenate([wide, jnp.zeros((r, 128 - length), F32)], axis=1)
        tile = jnp.where(row == i, wide, tile)
    first[:, 4 * d :] = tile.astype(BF16)
    second[:, 2 * ff + d :] = tile.astype(BF16)
    second[:, :ff] = up[...]
    for m in range(ff // d):
        second[:, ff + m * d : ff + (m + 1) * d] = down[m * r : (m + 1) * r, :]
    second[:, 2 * ff : 2 * ff + d] = o[...]


def pack(q, k, v, c, o, up, down, gain_a, gain_f, b_up, b_down):
    r, d = q.shape
    ff = up.shape[1]
    return pl.pallas_call(
        pack_kernel,
        out_shape=[jax.ShapeDtypeStruct((r, 4 * d + 128), BF16), jax.ShapeDtypeStruct((r, 2 * ff + d + 128), BF16)],
        cost_estimate=pl.CostEstimate(flops=0, bytes_accessed=1 << 20, transcendentals=0),
        name="pack",
    )(q, k, v, c, o, up, down, *(x.reshape(1, -1) for x in (gain_a, gain_f, b_up, b_down)))


def stack_kernel(*refs):
    for i, ref in enumerate(refs[:-1]):
        refs[-1][i] = ref[...]


def stack(items):
    return pl.pallas_call(
        stack_kernel,
        out_shape=jax.ShapeDtypeStruct((len(items),) + items[0].shape, items[0].dtype),
        cost_estimate=pl.CostEstimate(flops=0, bytes_accessed=2 << 20, transcendentals=0),
        name="stack",
    )(*items)


def project_kernel(where, arrays, r, me_ref, tok_ref, *refs):
    n = len(where)
    pieces = piece_refs(where, refs)
    att_ref, pack_ref, st_ref, w_ref, vec_out, kt_ref, mv_ref, tot_ref, vecs, sems, vsems = refs[arrays:]
    d = w_ref.shape[0]
    wide = w_ref.shape[1]
    me = me_ref[0]

    @pl.when(pl.program_id(0) == 0)
    def _():
        copies = []
        for j in range(n):
            at = pl.multiple_of((me ^ j) * r, r)
            copies.append(pltpu.make_async_copy(pieces[j].at[:, pl.ds(0, wide)], w_ref.at[pl.ds(at, r), :], sems.at[j]))
            copies.append(pltpu.make_async_copy(pieces[j].at[:, pl.ds(wide, 128)], vecs.at[pl.ds(j * r, r), :], vsems.at[j]))
        for c in copies:
            c.start()
        kt_ref[...] = jnp.zeros_like(kt_ref)
        mv_ref[...] = jnp.zeros_like(mv_ref)
        tot_ref[...] = jnp.zeros_like(tot_ref)
        for c in copies:
            c.wait()
        vec_out[...] = vecs[...]

    gain = spread_vector(vecs[...], me, n, r, 0, r, d)
    normed, _ = normalize(tok_ref[...].astype(F32))
    att = (normed * gain).astype(BF16)
    att_ref[...] = att
    cols = []
    for p in range(4):
        full = mm(att, w_ref[:, p * d : (p + 1) * d]).astype(BF16)
        pack_ref[:, p * d : (p + 1) * d] = full
        cols.append(full)
    written = jnp.exp(cols[3].astype(F32)).astype(BF16)
    for g in range(d // QUAD):
        s = slice(g * QUAD, (g + 1) * QUAD)
        kt_ref[g] += t_mm(cols[1][:, s], written[:, s])
        mv_ref[g] += t_mm(written[:, s], cols[2][:, s])
    tot_ref[0:1, :] += jnp.sum(written.astype(F32), axis=0, keepdims=True)

    @pl.when(pl.program_id(0) == pl.num_programs(0) - 1)
    def _():
        store_state(st_ref, kt_ref, mv_ref, tot_ref)


def project(me, tokens, where, pieces, rows=256):
    t, d = tokens.shape
    n = len(where)
    r = d // n
    wide = 4 * d
    g = d // QUAD
    const = lambda *shape: pl.BlockSpec(shape, lambda i: (0,) * len(shape))
    return pl.pallas_call(
        partial(project_kernel, where, len(pieces), r),
        grid=(t // rows,),
        in_specs=[pl.BlockSpec(memory_space=pltpu.SMEM), pl.BlockSpec((rows, d), lambda i: (i, 0))]
        + [pl.BlockSpec(memory_space=pl.ANY)] * len(pieces),
        out_specs=[
            pl.BlockSpec((rows, d), lambda i: (i, 0)),
            pl.BlockSpec((rows, wide), lambda i: (i, 0)),
            const(g, STATE, QUAD),
            const(d, wide),
            const(n * r, 128),
        ],
        out_shape=[
            jax.ShapeDtypeStruct((t, d), BF16),
            jax.ShapeDtypeStruct((t, wide), BF16),
            jax.ShapeDtypeStruct((g, STATE, QUAD), F32),
            jax.ShapeDtypeStruct((d, wide), BF16),
            jax.ShapeDtypeStruct((n * r, 128), BF16),
        ],
        scratch_shapes=[
            pltpu.VMEM((g, QUAD, QUAD), F32),
            pltpu.VMEM((g, QUAD, QUAD), F32),
            pltpu.VMEM((8, d), F32),
            pltpu.VMEM((n * r, 128), BF16),
            pltpu.SemaphoreType.DMA((n,)),
            pltpu.SemaphoreType.DMA((n,)),
        ],
        compiler_params=pltpu.CompilerParams(vmem_limit_bytes=VMEM_LIMIT),
        cost_estimate=pl.CostEstimate(flops=2 * t * d * wide, bytes_accessed=12 << 20, transcendentals=t * d),
        name="project",
    )(me, tokens, *pieces)


def mix_kernel(pack_ref, st_in, mix_ref, read_ref, score_ref, inv_ref, kts_ref, mvs_ref, kt, mv, tot):
    d = mix_ref.shape[1]
    rows = mix_ref.shape[0]

    @pl.when(pl.program_id(0) == 0)
    def _():
        load_state(st_in, kt, mv, tot)

    c = CHUNK
    square = head_square()
    ones = (iota((c, c), 0) >= iota((c, c), 1)).astype(BF16)
    for b in range(rows // c):
        rr = slice(b * c, (b + 1) * c)
        for g in range(d // QUAD):
            s = slice(g * QUAD, (g + 1) * QUAD)
            q, k, v, u = (pack_ref[rr, p * d + g * QUAD : p * d + (g + 1) * QUAD] for p in range(4))
            written = jnp.exp(u.astype(F32)).astype(BF16)
            wb = blocks_of(written)
            pairs = tri(mm_t(q, blocks_of(k)), True)
            ktb, mvb = kt[g].astype(BF16), mv[g].astype(BF16)
            kts_ref[b, g] = ktb
            mvs_ref[b, g] = mvb
            top = mm(pairs, wb) + mm(q, ktb)
            total = mm(ones, written) + tot[0:1, s]
            inv = 1.0 / total
            score = top * SCALE * inv
            e = jnp.exp(score - per_head(score, jnp.max, -jnp.inf))
            read = e / per_head(e, jnp.sum, 0.0)
            scaled = (read * inv).astype(BF16)
            recall = tri(mm_t(scaled, wb), True)
            out = mm(recall, blocks_of(v)) + mm(scaled, mvb)
            mix_ref[rr, s] = out.astype(BF16)
            read_ref[rr, s] = read
            score_ref[rr, s] = score
            inv_ref[rr, s] = inv
            kt[g] += jnp.where(square, t_mm(k, written), 0.0)
            mv[g] += jnp.where(square, t_mm(written, v), 0.0)
            tot[0:1, s] = total[c - 1 : c, :]


def mix(packed, state, rows=256):
    t, wide = packed.shape
    d = wide // 4
    g = d // QUAD
    const = lambda *shape: pl.BlockSpec(shape, lambda i: (0,) * len(shape))
    per = rows // CHUNK
    row = lambda w: pl.BlockSpec((rows, w), lambda i: (i, 0))
    return pl.pallas_call(
        mix_kernel,
        grid=(t // rows,),
        in_specs=[row(wide), const(g, STATE, QUAD)],
        out_specs=[row(d)] * 4 + [pl.BlockSpec((per, g, QUAD, QUAD), lambda i: (i, 0, 0, 0))] * 2,
        out_shape=[jax.ShapeDtypeStruct((t, d), BF16)] + [jax.ShapeDtypeStruct((t, d), F32)] * 3
        + [jax.ShapeDtypeStruct((t // CHUNK, g, QUAD, QUAD), BF16)] * 2,
        scratch_shapes=[pltpu.VMEM((g, QUAD, QUAD), F32), pltpu.VMEM((g, QUAD, QUAD), F32), pltpu.VMEM((8, d), F32)],
        compiler_params=pltpu.CompilerParams(vmem_limit_bytes=VMEM_LIMIT),
        cost_estimate=pl.CostEstimate(flops=6 * 10**9, bytes_accessed=16 << 20, transcendentals=2 * t * d),
        name="mix",
    )(packed, state)


def ffn_kernel(n, mixed_ref, tok_ref, cot_ref, full_ref, out_ref, gres_ref, gmix_ref, grad_ref,
               w_out, w_up, w_down, vecs, hid, gpre, fin, gbr, sems, osems):
    t, d = mixed_ref.shape
    ff = w_up.shape[1]
    r = d // n
    mult = ff // d

    def moves(hbm, sem, out):
        yield w_up, hbm.at[:, pl.ds(0, ff)], sem.at[0]
        yield w_out, hbm.at[:, pl.ds(2 * ff, d)], sem.at[1]
        yield vecs, hbm.at[:, pl.ds(2 * ff + d, 128)], sem.at[2]
        for j in range(n):
            for m in range(mult):
                at = (j * mult + m) * r
                yield w_down.at[pl.ds(at, r), :], hbm.at[pl.ds(j * r, r), pl.ds(ff + m * d, d)], sem.at[3 + j * mult + m]

    copies = [pltpu.make_async_copy(h, v, s) for v, h, s in moves(full_ref, sems, False)]
    for c in copies:
        c.start()
    for c in copies:
        c.wait()
    gain = spread_vector(vecs[...], 0, n, r, 1, r, d)
    b_up = spread_vector(vecs[...], 0, n, r, 2, r * mult, ff)
    b_down = spread_vector(vecs[...], 0, n, r, 3, r, d)

    rows = 256
    part = 512
    zero = jnp.zeros((1, d), F32)

    def body(i, carry):
        ggain, gbup, gbdown = carry
        at = pl.multiple_of(i * rows, rows)
        rs = pl.ds(at, rows)
        cot = cot_ref[rs, :]
        cotf = cot.astype(F32)
        resid = tok_ref[rs, :].astype(F32) + mm(mixed_ref[rs, :], w_out[...])
        normed, factor = normalize(resid)
        ffn_in = (normed * gain).astype(BF16)
        fin[rs, :] = ffn_in
        total = jnp.zeros((rows, d), F32)
        gin = jnp.zeros((rows, d), F32)
        sums = []
        for p in range(ff // part):
            ps = slice(p * part, (p + 1) * part)
            pre = mm(ffn_in, w_up[:, ps]) + b_up[:, ps]
            sig = 1.0 / (1.0 + jnp.exp(-pre))
            hidden = (pre * sig).astype(BF16)
            hid[rs, ps] = hidden
            total += mm(hidden, w_down[ps, :])
            gh = mm_t(cot, w_down[ps, :])
            gp = (gh * (sig * (1.0 + pre * (1.0 - sig)))).astype(BF16)
            gpre[rs, ps] = gp
            sums.append(jnp.sum(gp.astype(F32), axis=0, keepdims=True))
            gin += mm_t(gp, w_up[:, ps])
        out_ref[rs, :] = (resid + (total + b_down)).astype(BF16)
        gres = cotf + norm_back(gin * gain, normed, factor)
        gres_ref[rs, :] = gres
        gb = gres.astype(BF16)
        gbr[rs, :] = gb
        gmix_ref[rs, :] = mm_t(gb, w_out[...]).astype(BF16)
        return (
            ggain + jnp.sum(gin * normed, axis=0, keepdims=True),
            gbup + jnp.concatenate(sums, axis=1),
            gbdown + jnp.sum(cotf, axis=0, keepdims=True),
        )

    ggain, gbup, gbdown = lax.fori_loop(0, t // rows, body, (zero, jnp.zeros((1, ff), F32), zero))
    for p in range(ff // part):
        ps = slice(p * part, (p + 1) * part)
        w_up[:, ps] = t_mm(fin[...], gpre[:, ps]).astype(BF16)
        w_down[ps, :] = t_mm(hid[:, ps], cot_ref[...]).astype(BF16)
    w_out[...] = t_mm(mixed_ref[...], gbr[...]).astype(BF16)
    va = gather_vector(ggain, 0, n, r)
    vb = gather_vector(gbup, 0, n, r * mult)
    vc = gather_vector(gbdown, 0, n, r)
    for j in range(n):
        row = iota((r, 128), 0)
        pick = lambda v, i, rest: jnp.where(row == i, jnp.broadcast_to(v[j : j + 1].astype(F32), (r, 128)), rest)
        tile = pick(va, 1, pick(vb, 2, pick(vc, 3, jnp.zeros((r, 128), F32))))
        vecs[j * r : (j + 1) * r, :] = tile.astype(BF16)
    copies = [pltpu.make_async_copy(v, h, s) for v, h, s in moves(grad_ref, osems, True)]
    for c in copies:
        c.start()
    for c in copies:
        c.wait()


def ffn(mixed, tokens, cot, full, ff, n):
    t, d = tokens.shape
    whole = pl.BlockSpec(memory_space=pltpu.VMEM)
    hbm = pl.BlockSpec(memory_space=pl.ANY)
    return pl.pallas_call(
        partial(ffn_kernel, n),
        in_specs=[whole] * 3 + [hbm],
        out_specs=[whole] * 3 + [hbm],
        out_shape=[
            jax.ShapeDtypeStruct((t, d), BF16),
            jax.ShapeDtypeStruct((t, d), F32),
            jax.ShapeDtypeStruct((t, d), BF16),
            jax.ShapeDtypeStruct(full.shape, BF16),
        ],
        scratch_shapes=[
            pltpu.VMEM((d, d), BF16),
            pltpu.VMEM((d, ff), BF16),
            pltpu.VMEM((ff, d), BF16),
            pltpu.VMEM((d, 128), BF16),
            pltpu.VMEM((t, ff), BF16),
            pltpu.VMEM((t, ff), BF16),
            pltpu.VMEM((t, d), BF16),
            pltpu.VMEM((t, d), BF16),
            pltpu.SemaphoreType.DMA((3 + n * (ff // d),)),
            pltpu.SemaphoreType.DMA((3 + n * (ff // d),)),
        ],
        compiler_params=pltpu.CompilerParams(vmem_limit_bytes=VMEM_LIMIT),
        cost_estimate=pl.CostEstimate(flops=12 * t * d * ff, bytes_accessed=20 << 20, transcendentals=t * ff),
        name="ffn",
    )(mixed, tokens, cot, full)


def read_back_kernel(pack_ref, gmix_ref, read_ref, score_ref, inv_ref, kts_ref, mvs_ref,
                     gq_ref, a_ref, u_ref, gtot_ref, st_ref, gk_ref, gv_ref, gt_ref):
    rows, d = gmix_ref.shape

    @pl.when(pl.program_id(0) == 0)
    def _():
        gk_ref[...] = jnp.zeros_like(gk_ref)
        gv_ref[...] = jnp.zeros_like(gv_ref)
        gt_ref[...] = jnp.zeros_like(gt_ref)

    c = CHUNK
    for b in range(rows // c):
        rr = slice(b * c, (b + 1) * c)
        for g in range(d // QUAD):
            s = slice(g * QUAD, (g + 1) * QUAD)
            q, k, v, w = (pack_ref[rr, p * d + g * QUAD : p * d + (g + 1) * QUAD] for p in range(4))
            written = jnp.exp(w.astype(F32)).astype(BF16)
            wb = blocks_of(written)
            gm = gmix_ref[rr, s]
            read, score, inv = read_ref[rr, s], score_ref[rr, s], inv_ref[rr, s]
            gpair = tri(mm_t(gm, blocks_of(v)), True)
            gread = (mm(gpair, wb) + mm_t(gm, mvs_ref[b, g])) * inv
            weighted = read * gread
            gscore = weighted - read * per_head(weighted, jnp.sum, 0.0)
            a = (gscore * inv * SCALE).astype(BF16)
            u = (read * inv).astype(BF16)
            gtot = (gscore * score + weighted) * inv
            spair = tri(mm_t(a, wb), True)
            gq_ref[rr, s] = (mm(spair, blocks_of(k)) + mm_t(a, kts_ref[b, g])).astype(BF16)
            a_ref[rr, s] = a
            u_ref[rr, s] = u
            gtot_ref[rr, s] = gtot
            gk_ref[g] += t_mm(a, q)
            gv_ref[g] += t_mm(u, gm)
            gt_ref[0:1, s] += jnp.sum(gtot, axis=0, keepdims=True)

    @pl.when(pl.program_id(0) == pl.num_programs(0) - 1)
    def _():
        store_state(st_ref, gk_ref, gv_ref, gt_ref)


def read_back(packed, gmix, read, score, inv, kts, mvs, rows=256):
    t, wide = packed.shape
    d = wide // 4
    g = d // QUAD
    const = lambda *shape: pl.BlockSpec(shape, lambda i: (0,) * len(shape))
    per = rows // CHUNK
    row = lambda w: pl.BlockSpec((rows, w), lambda i: (i, 0))
    st = pl.BlockSpec((per, g, QUAD, QUAD), lambda i: (i, 0, 0, 0))
    return pl.pallas_call(
        read_back_kernel,
        grid=(t // rows,),
        in_specs=[row(wide), row(d), row(d), row(d), row(d), st, st],
        out_specs=[row(d)] * 4 + [const(g, STATE, QUAD)],
        out_shape=[jax.ShapeDtypeStruct((t, d), BF16)] * 3 + [jax.ShapeDtypeStruct((t, d), F32)]
        + [jax.ShapeDtypeStruct((g, STATE, QUAD), F32)],
        scratch_shapes=[pltpu.VMEM((g, QUAD, QUAD), F32), pltpu.VMEM((g, QUAD, QUAD), F32), pltpu.VMEM((8, d), F32)],
        compiler_params=pltpu.CompilerParams(vmem_limit_bytes=VMEM_LIMIT),
        cost_estimate=pl.CostEstimate(flops=6 * 10**9, bytes_accessed=20 << 20, transcendentals=t * d),
        name="read_back",
    )(packed, gmix, read, score, inv, kts, mvs)


def write_back_kernel(pack_ref, gmix_ref, a_ref, u_ref, gtot_ref, st_in, out_ref, gk, gv, gt):
    rows, d = gmix_ref.shape

    @pl.when(pl.program_id(0) == 0)
    def _():
        load_state(st_in, gk, gv, gt)

    c = CHUNK
    square = head_square()
    ones = (iota((c, c), 0) <= iota((c, c), 1)).astype(BF16)
    for b in reversed(range(rows // c)):
        rr = slice(b * c, (b + 1) * c)
        for g in range(d // QUAD):
            s = slice(g * QUAD, (g + 1) * QUAD)
            q, k, v, w = (pack_ref[rr, p * d + g * QUAD : p * d + (g + 1) * QUAD] for p in range(4))
            wf = jnp.exp(w.astype(F32))
            written = wf.astype(BF16)
            gm, a, u = gmix_ref[rr, s], a_ref[rr, s], u_ref[rr, s]
            gtot = gtot_ref[rr, s]
            hi, lo = hi_lo(gtot)
            after = mm(ones, hi) + mm(ones, lo) + gt[0:1, s]
            qb, gb, ab, ub = blocks_of(q), blocks_of(gm), blocks_of(a), blocks_of(u)
            gkb, gvb = gk[g].astype(BF16), gv[g].astype(BF16)
            pt = tri(mm_t(k, qb), False)
            gp = tri(mm_t(v, gb), False)
            st = tri(mm_t(written, ab), False)
            rt = tri(mm_t(written, ub), False)
            gw = mm(pt, ab) + mm(gp, ub) + mm_t(k, gkb) + mm_t(v, gvb)
            gkey = mm(st, qb) + mm(written, gkb)
            gval = mm(rt, gb) + mm(written, gvb)
            out_ref[rr, g * QUAD : (g + 1) * QUAD] = gkey.astype(BF16)
            out_ref[rr, d + g * QUAD : d + (g + 1) * QUAD] = gval.astype(BF16)
            out_ref[rr, 2 * d + g * QUAD : 2 * d + (g + 1) * QUAD] = (wf * (gw - after)).astype(BF16)
            gk[g] += jnp.where(square, t_mm(a, q), 0.0)
            gv[g] += jnp.where(square, t_mm(u, gm), 0.0)
            gt[0:1, s] = after[0:1, :]


def write_back(packed, gmix, a, u, gtot, state, rows=256):
    t, wide = packed.shape
    d = wide // 4
    g = d // QUAD
    last = t // rows - 1
    const = lambda *shape: pl.BlockSpec(shape, lambda i: (0,) * len(shape))
    row = lambda w: pl.BlockSpec((rows, w), lambda i: (last - i, 0))
    return pl.pallas_call(
        write_back_kernel,
        grid=(t // rows,),
        in_specs=[row(wide), row(d), row(d), row(d), row(d), const(g, STATE, QUAD)],
        out_specs=row(3 * d),
        out_shape=jax.ShapeDtypeStruct((t, 3 * d), BF16),
        scratch_shapes=[pltpu.VMEM((g, QUAD, QUAD), F32), pltpu.VMEM((g, QUAD, QUAD), F32), pltpu.VMEM((8, d), F32)],
        compiler_params=pltpu.CompilerParams(vmem_limit_bytes=VMEM_LIMIT),
        cost_estimate=pl.CostEstimate(flops=9 * 10**9, bytes_accessed=16 << 20, transcendentals=t * d),
        name="write_back",
    )(packed, gmix, a, u, gtot, state)


def weight_grad_kernel(n, r, me_ref, att_ref, gq_ref, gkvc_ref, *refs):
    share_refs = refs[:4]
    acc, sems = refs[4:]
    d = att_ref.shape[1]
    me = me_ref[0]
    acc[:, 0:d] = t_mm(att_ref[...], gq_ref[...]).astype(BF16)
    for p in range(3):
        acc[:, (p + 1) * d : (p + 2) * d] = t_mm(att_ref[...], gkvc_ref[:, p * d : (p + 1) * d]).astype(BF16)
    outs = []
    for j in range(n):
        at = pl.multiple_of((me ^ j) * r, r)
        dst = share_refs[j % 4].at[j // 4]
        outs.append(pltpu.make_async_copy(acc.at[pl.ds(at, r), :], dst, sems.at[j]))
    for c in outs:
        c.start()
    for c in outs:
        c.wait()


def weight_grad(me, att, gq, gkvc, n):
    t, d = att.shape
    r = d // n
    whole = pl.BlockSpec(memory_space=pltpu.VMEM)
    hbm = pl.BlockSpec(memory_space=pl.ANY)
    return pl.pallas_call(
        partial(weight_grad_kernel, n, r),
        in_specs=[pl.BlockSpec(memory_space=pltpu.SMEM)] + [whole] * 3,
        out_specs=[hbm] * 4,
        out_shape=[jax.ShapeDtypeStruct((n // 4, r, 4 * d), BF16)] * 4,
        scratch_shapes=[pltpu.VMEM((d, 4 * d), BF16), pltpu.SemaphoreType.DMA((n,))],
        compiler_params=pltpu.CompilerParams(vmem_limit_bytes=VMEM_LIMIT),
        cost_estimate=pl.CostEstimate(flops=8 * t * d * d, bytes_accessed=7 << 20, transcendentals=0),
        name="weight_grad",
    )(me, att, gq, gkvc)


def input_grad_kernel(n, r, me_ref, vec_ref, tok_ref, gq_ref, gkvc_ref, w_ref, gres_ref, out_ref):
    d = tok_ref.shape[1]
    gain = spread_vector(vec_ref[...], me_ref[0], n, r, 0, r, d)
    gin = mm_t(gq_ref[...], w_ref[:, 0:d]) + mm_t(gkvc_ref[...], w_ref[:, d:])
    normed, factor = normalize(tok_ref[...].astype(F32))
    out_ref[...] = gres_ref[...] + norm_back(gin * gain, normed, factor)


def input_grad(me, vecs, tokens, gq, gkvc, w, gres, n, rows=256):
    t, d = tokens.shape
    r = d // n
    const = lambda *shape: pl.BlockSpec(shape, lambda i: (0,) * len(shape))
    row = lambda w: pl.BlockSpec((rows, w), lambda i: (i, 0))
    return pl.pallas_call(
        partial(input_grad_kernel, n, r),
        grid=(t // rows,),
        in_specs=[pl.BlockSpec(memory_space=pltpu.SMEM), const(n * r, 128), row(d), row(d), row(3 * d), const(d, 4 * d), row(d)],
        out_specs=row(d),
        out_shape=jax.ShapeDtypeStruct((t, d), F32),
        compiler_params=pltpu.CompilerParams(vmem_limit_bytes=VMEM_LIMIT),
        cost_estimate=pl.CostEstimate(flops=8 * t * d * d, bytes_accessed=12 << 20, transcendentals=0),
        name="input_grad",
    )(me, vecs, tokens, gq, gkvc, w, gres)


def swap(x, mask, n):
    return lax.ppermute(x, "fsdp", [(i, i ^ mask) for i in range(n)])


def after(x, *first):
    return lax.optimization_barrier((x, *first))[0]


def add(*items):
    return sum(x.astype(F32) for x in items).astype(BF16)


def along_z(shard, n):
    return [shard] + [swap(shard, 4 * k, n) for k in range(1, n // 4)]


def along_x(own, n):
    return [swap(x, 2, n) for x in own]


def shift(x, by, seqs):
    return lax.ppermute(x, "seq", [(i, i + by) for i in range(seqs) if 0 <= i + by < seqs])


def others(state, direction, seqs):
    if seqs == 1:
        return jnp.zeros_like(state)
    total = shift(state, direction, seqs)
    step = 1
    while step < seqs - 1:
        total = total + shift(total, direction * step, seqs)
        step *= 2
    return total


def on_device(n, seqs, tokens, w_query, w_key, w_value, w_control, w_out, w_up, w_down,
              gain_attn, gain_ffn, bias_up, bias_down, cotangent):
    r, d = w_query.shape
    ff = w_up.shape[1]
    mult = ff // d
    me = lax.axis_index("fsdp").astype(jnp.int32).reshape(1)
    first, second = pack(w_query, w_key, w_value, w_control, w_out, w_up, w_down, gain_attn, gain_ffn, bias_up, bias_down)
    depth = n // 4
    own = along_z(first, n)
    full = lax.all_gather(second, "fsdp", axis=0, tiled=True)
    across = along_x(own, n)
    cored = [[swap(x, 1, n) for x in group] for group in (own, across)]
    att_pieces = [x for quad in zip(own, cored[0], across, cored[1]) for x in quad]
    att_where = [(j, None) for j in range(n)]
    att, packed, state, w_att, vecs = project(me, tokens, att_where, att_pieces)
    mixed, read, score, inv, kts, mvs = mix(packed, others(state, 1, seqs))
    layer_out, gres, gmix, ffn_grad = ffn(mixed, tokens, cotangent, full, ff, n)
    ffn_sum = lax.psum_scatter(ffn_grad, "fsdp", scatter_dimension=0, tiled=True)

    def core_sum(shares):
        near, near_core, far, far_core = shares
        return add(near, swap(near_core, 1, n)), add(far, swap(far_core, 1, n))

    def seq_sum(x):
        step = 1
        while step < seqs:
            x = add(x, lax.ppermute(x, "seq", [(i, i ^ step) for i in range(seqs)]))
            step *= 2
        return x.astype(F32)

    gq, a, u, gtot, gstate = read_back(packed, gmix, read, score, inv, kts, mvs)
    gkvc = write_back(packed, gmix, a, u, gtot, others(gstate, -1, seqs))
    shares = weight_grad(me, att, gq, gkvc, n)
    near, far = core_sum(shares)
    grad_tokens = input_grad(me, vecs, tokens, after(gq, near, far), gkvc, w_att, gres, n)
    mine = {k: add(near[k], swap(far[k], 2, n)) for k in range(depth - 1, -1, -1)}
    sent = {k: swap(mine[k], 4 * k, n) if k else mine[k] for k in range(depth)}
    ffn_share = seq_sum(ffn_sum)
    att_share = seq_sum(add(*sent.values()))
    gain_share = jnp.sum(att_share * first[:, : 4 * d].astype(F32), axis=1) / gain_attn.astype(F32)
    up, down, out, vec = (
        ffn_share[:, :ff],
        ffn_share[:, ff : 2 * ff],
        ffn_share[:, 2 * ff : 2 * ff + d],
        ffn_share[:, 2 * ff + d :],
    )
    down = jnp.concatenate([down[:, m * d : (m + 1) * d] for m in range(mult)], axis=0)
    return (
        layer_out,
        grad_tokens,
        att_share[:, 0:d],
        att_share[:, d : 2 * d],
        att_share[:, 2 * d : 3 * d],
        att_share[:, 3 * d :],
        out,
        up,
        down,
        gain_share,
        vec[1, :r],
        vec[2, : r * mult],
        vec[3, :r],
    )


def solution(mesh):
    tokens = P(("fsdp", "seq"), None)
    matrix = P("fsdp", None)
    vector = P("fsdp")
    return jax.shard_map(
        partial(on_device, mesh.shape["fsdp"], mesh.shape["seq"]),
        mesh=mesh,
        in_specs=(tokens,) + (matrix,) * 7 + (vector,) * 4 + (tokens,),
        out_specs=(tokens, tokens) + (matrix,) * 7 + (vector,) * 4,
        check_vma=False,
    )
```

```python
from functools import partial
import jax
import jax.numpy as jnp
from jax import lax
from jax.experimental import pallas as pl
from jax.experimental.pallas import tpu as pltpu
from jax.sharding import PartitionSpec as P

F32 = jnp.float32
BF16 = jnp.bfloat16
HEAD = 64
QUAD = 256
SCALE = HEAD ** -0.5
CHUNK = 128
VMEM_LIMIT = 60 * 1024 * 1024


def mm(a, b):
    return lax.dot_general(a, b, (((1,), (0,)), ((), ())), preferred_element_type=F32)


def mm_t(a, b):
    return lax.dot_general(a, b, (((1,), (1,)), ((), ())), preferred_element_type=F32)


def t_mm(a, b):
    return lax.dot_general(a, b, (((0,), (0,)), ((), ())), preferred_element_type=F32)


def iota(shape, dim):
    return lax.broadcasted_iota(jnp.int32, shape, dim)


def normalize(x):
    centred = x - jnp.mean(x, axis=-1, keepdims=True)
    spread = jnp.mean(centred * centred, axis=-1, keepdims=True)
    factor = lax.rsqrt(spread + 1e-05)
    return centred * factor, factor


def norm_back(g, normed, factor):
    first = jnp.mean(g, axis=-1, keepdims=True)
    second = jnp.mean(g * normed, axis=-1, keepdims=True)
    return factor * (g - first - normed * second)


def blocks_of(x):
    lane = iota(x.shape, 1) // HEAD
    zero = jnp.zeros_like(x)
    return jnp.concatenate([jnp.where(lane == h, x, zero) for h in range(4)], axis=0)


def blocks_t(x):
    xt = x.T
    row = iota(xt.shape, 0) // HEAD
    zero = jnp.zeros_like(xt)
    return jnp.concatenate([jnp.where(row == h, xt, zero) for h in range(4)], axis=1)


def tri(x, lower):
    c = x.shape[0]
    row, col = iota(x.shape, 0), iota(x.shape, 1) % c
    keep = row >= col if lower else row <= col
    return jnp.where(keep, x, 0.0).astype(BF16)


def per_head(x, op, neutral):
    parts = []
    for p in range(x.shape[1] // 128):
        v = x[:, p * 128 : (p + 1) * 128]
        low = iota(v.shape, 1) < HEAD
        a = op(jnp.where(low, v, neutral), axis=-1, keepdims=True)
        b = op(jnp.where(low, neutral, v), axis=-1, keepdims=True)
        parts.append(jnp.where(low, a, b))
    return jnp.concatenate(parts, axis=1)


def head_square():
    return iota((QUAD, QUAD), 0) // HEAD == iota((QUAD, QUAD), 1) // HEAD


STATE = 2 * HEAD + 8


def store_state(st_ref, first, second, total):
    square = head_square()
    for g in range(st_ref.shape[0]):
        for k, ref in enumerate((first, second)):
            x = jnp.where(square, ref[g], 0.0)
            st_ref[g, k * HEAD : (k + 1) * HEAD, :] = x[0:64] + x[64:128] + x[128:192] + x[192:256]
        st_ref[g, 2 * HEAD :, :] = jnp.broadcast_to(total[0:1, g * QUAD : (g + 1) * QUAD], (8, QUAD))


def load_state(st_ref, first, second, total):
    square = head_square()
    for g in range(st_ref.shape[0]):
        for k, ref in enumerate((first, second)):
            x = st_ref[g, k * HEAD : (k + 1) * HEAD, :]
            ref[g] = jnp.where(square, jnp.concatenate([x] * 4, axis=0), 0.0)
        total[:, g * QUAD : (g + 1) * QUAD] = st_ref[g, 2 * HEAD :, :]


def hi_lo(x):
    hi = x.astype(BF16)
    return hi, (x - hi.astype(F32)).astype(BF16)


def spread_vector(vecs, me, n, r, k, each, total):
    pick = (iota((n, n * r), 1) == iota((n, n * r), 0) * r + k).astype(BF16)
    rows = mm(pick, vecs).astype(BF16)
    tile = (iota((128, total), 1) % each == iota((128, total), 0)).astype(BF16)
    wide = mm(rows, tile)
    own = iota((n, total), 1) // each == (iota((n, total), 0) ^ me)
    return jnp.sum(jnp.where(own, wide, 0.0), axis=0, keepdims=True)


def gather_vector(vec, me, n, each):
    total = vec.shape[1]
    own = iota((n, total), 1) // each == (iota((n, total), 0) ^ me)
    wide = jnp.where(own, vec, 0.0).astype(BF16)
    tile = (iota((128, total), 1) % each == iota((128, total), 0)).astype(BF16)
    return mm_t(wide, tile).astype(BF16)


def piece_refs(where, refs):
    return [refs[a] if row is None else refs[a].at[row] for a, row in where]


def pack_kernel(q, k, v, c, o, up, down, gain_a, gain_f, b_up, b_down, first, second):
    r, d = q.shape
    ff = up.shape[1]
    for p, ref in enumerate((q, k, v, c)):
        first[:, p * d : (p + 1) * d] = ref[...]
    tile = jnp.zeros((r, 128), F32)
    row, col = iota((r, 128), 0), iota((r, 128), 1)
    for i, ref in enumerate((gain_a, gain_f, b_up, b_down)):
        length = ref.shape[1]
        wide = jnp.broadcast_to(ref[...].astype(F32), (r, length))
        if length < 128:
            wide = jnp.concatenate([wide, jnp.zeros((r, 128 - length), F32)], axis=1)
        tile = jnp.where(row == i, wide, tile)
    first[:, 4 * d :] = tile.astype(BF16)
    second[:, 2 * ff + d :] = tile.astype(BF16)
    second[:, :ff] = up[...]
    for m in range(ff // d):
        second[:, ff + m * d : ff + (m + 1) * d] = down[m * r : (m + 1) * r, :]
    second[:, 2 * ff : 2 * ff + d] = o[...]


def pack(q, k, v, c, o, up, down, gain_a, gain_f, b_up, b_down):
    r, d = q.shape
    ff = up.shape[1]
    return pl.pallas_call(
        pack_kernel,
        out_shape=[jax.ShapeDtypeStruct((r, 4 * d + 128), BF16), jax.ShapeDtypeStruct((r, 2 * ff + d + 128), BF16)],
        cost_estimate=pl.CostEstimate(flops=0, bytes_accessed=1 << 20, transcendentals=0),
        name="pack",
    )(q, k, v, c, o, up, down, *(x.reshape(1, -1) for x in (gain_a, gain_f, b_up, b_down)))


def stack_kernel(*refs):
    for i, ref in enumerate(refs[:-1]):
        refs[-1][i] = ref[...]


def stack(items):
    return pl.pallas_call(
        stack_kernel,
        out_shape=jax.ShapeDtypeStruct((len(items),) + items[0].shape, items[0].dtype),
        cost_estimate=pl.CostEstimate(flops=0, bytes_accessed=2 << 20, transcendentals=0),
        name="stack",
    )(*items)


def project_kernel(where, arrays, r, me_ref, tok_hbm, *refs):
    n = len(where)
    pieces = piece_refs(where, refs)
    (att_hbm, pack_hbm, st_ref, w_hbm, gain_ref,
     tok, att, pack, w_all, vecs, normed, written, first, second, total, sems, vsems, tsem, osems) = refs[arrays:]
    t, d = att.shape
    wide = 4 * d
    rows = 256
    me = me_ref[0]
    load = pltpu.make_async_copy(tok_hbm, tok, tsem)
    load.start()
    vector_copies, copies = [], []
    for j in range(n):
        at = pl.multiple_of((me ^ j) * r, r)
        copies.append(pltpu.make_async_copy(pieces[j].at[:, pl.ds(0, wide)], w_all.at[pl.ds(at, r), :], sems.at[j]))
        vector_copies.append(pltpu.make_async_copy(pieces[j].at[:, pl.ds(wide, 128)], vecs.at[pl.ds(j * r, r), :], vsems.at[j]))
    for c in vector_copies + copies:
        c.start()
    sent = []

    def send(src, dst):
        copy = pltpu.make_async_copy(src, dst, osems.at[len(sent)])
        copy.start()
        sent.append(copy)

    load.wait()
    for i in range(t // rows):
        rs = pl.ds(i * rows, rows)
        normed[rs, :], _ = normalize(tok[rs, :].astype(F32))
    for c in vector_copies:
        c.wait()
    gain = spread_vector(vecs[...], me, n, r, 0, r, d)
    gain_ref[...] = jnp.broadcast_to(gain, gain_ref.shape)
    for c in copies:
        c.wait()
    send(w_all, w_hbm)
    sums = jnp.zeros((1, d), F32)
    for i in range(t // rows):
        rs = pl.ds(i * rows, rows)
        x = (normed[rs, :] * gain).astype(BF16)
        att[rs, :] = x
        send(att.at[rs, :], att_hbm.at[rs, :])
        for p in (3, 1, 2, 0):
            full = mm(x, w_all[:, p * d : (p + 1) * d]).astype(BF16)
            pack[rs, p * d : (p + 1) * d] = full
            if p == 3:
                new = jnp.exp(full.astype(F32)).astype(BF16)
                written[rs, :] = new
                sums += jnp.sum(new.astype(F32), axis=0, keepdims=True)
        send(pack.at[rs, :], pack_hbm.at[rs, :])
    for g in range(d // QUAD):
        s = slice(g * QUAD, (g + 1) * QUAD)
        first[g] = t_mm(pack[:, d + g * QUAD : d + (g + 1) * QUAD], written[:, s])
        second[g] = t_mm(written[:, s], pack[:, 2 * d + g * QUAD : 2 * d + (g + 1) * QUAD])
    total[...] = jnp.broadcast_to(sums, total.shape)
    store_state(st_ref, first, second, total)
    for c in sent:
        c.wait()


def project(me, tokens, where, pieces):
    t, d = tokens.shape
    n = len(where)
    r = d // n
    wide = 4 * d
    g = d // QUAD
    hbm = pl.BlockSpec(memory_space=pl.ANY)
    vmem = pl.BlockSpec(memory_space=pltpu.VMEM)
    return pl.pallas_call(
        partial(project_kernel, where, len(pieces), r),
        in_specs=[pl.BlockSpec(memory_space=pltpu.SMEM)] + [hbm] * (1 + len(pieces)),
        out_specs=[hbm, hbm, vmem, hbm, vmem],
        out_shape=[
            jax.ShapeDtypeStruct((t, d), BF16),
            jax.ShapeDtypeStruct((t, wide), BF16),
            jax.ShapeDtypeStruct((g, STATE, QUAD), F32),
            jax.ShapeDtypeStruct((d, wide), BF16),
            jax.ShapeDtypeStruct((8, d), F32),
        ],
        scratch_shapes=[
            pltpu.VMEM((t, d), BF16),
            pltpu.VMEM((t, d), BF16),
            pltpu.VMEM((t, wide), BF16),
            pltpu.VMEM((d, wide), BF16),
            pltpu.VMEM((n * r, 128), BF16),
            pltpu.VMEM((t, d), F32),
            pltpu.VMEM((t, d), BF16),
            pltpu.VMEM((g, QUAD, QUAD), F32),
            pltpu.VMEM((g, QUAD, QUAD), F32),
            pltpu.VMEM((8, d), F32),
            pltpu.SemaphoreType.DMA((n,)),
            pltpu.SemaphoreType.DMA((n,)),
            pltpu.SemaphoreType.DMA,
            pltpu.SemaphoreType.DMA((1 + 2 * (t // 256),)),
        ],
        compiler_params=pltpu.CompilerParams(vmem_limit_bytes=VMEM_LIMIT),
        cost_estimate=pl.CostEstimate(flops=2 * t * d * wide, bytes_accessed=12 << 20, transcendentals=t * d),
        name="project",
    )(me, tokens, *pieces)


def mix_kernel(pack_ref, st_in, mix_ref, read_ref, score_ref, inv_ref, kts_ref, mvs_ref, kt, mv, tot):
    d = mix_ref.shape[1]
    rows = mix_ref.shape[0]

    @pl.when(pl.program_id(0) == 0)
    def _():
        load_state(st_in, kt, mv, tot)

    c = CHUNK
    square = head_square()
    ones = (iota((c, c), 0) >= iota((c, c), 1)).astype(BF16)
    units = [(b, g) for b in range(rows // c) for g in range(d // QUAD)]
    at = {(b, g): (slice(b * c, (b + 1) * c), slice(g * QUAD, (g + 1) * QUAD)) for b, g in units}
    part = lambda p: {(b, g): pack_ref[at[b, g][0], p * d + g * QUAD : p * d + (g + 1) * QUAD] for b, g in units}
    q, k, v = part(0), part(1), part(2)
    written = {x: jnp.exp(y.astype(F32)).astype(BF16) for x, y in part(3).items()}
    wb = {x: blocks_of(written[x]) for x in units}
    pairs = {x: tri(mm(q[x], blocks_t(k[x])), True) for x in units}
    ktb, mvb, inv = {}, {}, {}
    for x in units:
        b, g = x
        ktb[x], mvb[x] = kt[g].astype(BF16), mv[g].astype(BF16)
        kts_ref[b, g] = ktb[x]
        mvs_ref[b, g] = mvb[x]
        kt[g] += jnp.where(square, t_mm(k[x], written[x]), 0.0)
        mv[g] += jnp.where(square, t_mm(written[x], v[x]), 0.0)
        total = mm(ones, written[x]) + tot[0:1, at[x][1]]
        tot[0:1, at[x][1]] = total[c - 1 : c, :]
        inv[x] = 1.0 / total
        inv_ref[at[x]] = inv[x]
    score = {x: (mm(pairs[x], wb[x]) + mm(q[x], ktb[x])) * SCALE * inv[x] for x in units}
    for x in units:
        score_ref[at[x]] = score[x]
    e = {x: jnp.exp(score[x] - per_head(score[x], jnp.max, -jnp.inf)) for x in units}
    read = {x: e[x] / per_head(e[x], jnp.sum, 0.0) for x in units}
    for x in units:
        read_ref[at[x]] = read[x]
    scaled = {x: (read[x] * inv[x]).astype(BF16) for x in units}
    recall = {x: tri(mm(scaled[x], blocks_t(written[x])), True) for x in units}
    for x in units:
        mix_ref[at[x]] = (mm(recall[x], blocks_of(v[x])) + mm(scaled[x], mvb[x])).astype(BF16)


def mix(packed, state, rows=256):
    t, wide = packed.shape
    d = wide // 4
    g = d // QUAD
    const = lambda *shape: pl.BlockSpec(shape, lambda i: (0,) * len(shape))
    per = rows // CHUNK
    row = lambda w: pl.BlockSpec((rows, w), lambda i: (i, 0))
    return pl.pallas_call(
        mix_kernel,
        grid=(t // rows,),
        in_specs=[row(wide), const(g, STATE, QUAD)],
        out_specs=[row(d)] * 4 + [pl.BlockSpec((per, g, QUAD, QUAD), lambda i: (i, 0, 0, 0))] * 2,
        out_shape=[jax.ShapeDtypeStruct((t, d), BF16)] + [jax.ShapeDtypeStruct((t, d), F32)] * 3
        + [jax.ShapeDtypeStruct((t // CHUNK, g, QUAD, QUAD), BF16)] * 2,
        scratch_shapes=[pltpu.VMEM((g, QUAD, QUAD), F32), pltpu.VMEM((g, QUAD, QUAD), F32), pltpu.VMEM((8, d), F32)],
        compiler_params=pltpu.CompilerParams(vmem_limit_bytes=VMEM_LIMIT),
        cost_estimate=pl.CostEstimate(flops=6 * 10**9, bytes_accessed=16 << 20, transcendentals=2 * t * d),
        name="mix",
    )(packed, state)


def ffn_kernel(n, mixed_hbm, tok_hbm, cot_hbm, full_ref, out_hbm, gres_hbm, gmix_hbm, grad_ref,
               mixed, tok, cot, outs, gres, gmix, w_out, w_up, w_down, vecs, hid, gpre, fin, gbr, sems, osems):
    t, d = mixed.shape
    ff = w_up.shape[1]
    r = d // n
    mult = ff // d
    rows = 256
    part = 512
    steps = t // rows
    parts = ff // part

    def load(src, dst, i):
        copy = pltpu.make_async_copy(src, dst, sems.at[i])
        copy.start()
        return copy

    down_sem = 3
    early = [
        load(full_ref.at[:, pl.ds(2 * ff, d)], w_out, 0),
        load(mixed_hbm, mixed, 1),
        load(tok_hbm, tok, 2),
        load(full_ref.at[:, pl.ds(2 * ff + d, 128)], vecs, 4),
        load(full_ref.at[:, pl.ds(0, ff)], w_up, 5),
    ]
    late = [load(cot_hbm, cot, 6)]
    down = []
    for j in range(n):
        for m in range(mult):
            down.append((full_ref.at[pl.ds(j * r, r), pl.ds(ff + m * d, d)], w_down.at[pl.ds((j * mult + m) * r, r), :]))
    late += [load(src, dst, 7 + i) for i, (src, dst) in enumerate(down)]
    for c in early:
        c.wait()
    gain = spread_vector(vecs[...], 0, n, r, 1, r, d)
    b_up = spread_vector(vecs[...], 0, n, r, 2, r * mult, ff)
    b_down = spread_vector(vecs[...], 0, n, r, 3, r, d)

    sent = []

    def send(src, dst):
        copy = pltpu.make_async_copy(src, dst, osems.at[len(sent)])
        copy.start()
        sent.append(copy)

    ggain = jnp.zeros((1, d), F32)
    gbdown = jnp.zeros((1, d), F32)
    gbup = [jnp.zeros((1, part), F32)] * parts
    for i in range(steps):
        rs = pl.ds(i * rows, rows)
        resid = tok[rs, :].astype(F32) + mm(mixed[rs, :], w_out[...])
        normed, factor = normalize(resid)
        ffn_in = (normed * gain).astype(BF16)
        fin[rs, :] = ffn_in
        if i == 0:
            for c in late:
                c.wait()
        cot_b = cot[rs, :]
        cotf = cot_b.astype(F32)

        def entry(p):
            ps = slice(p * part, (p + 1) * part)
            return mm(ffn_in, w_up[:, ps]) + b_up[:, ps], mm_t(cot_b, w_down[ps, :])

        ready = entry(0)
        total = gin = None
        for p in range(parts):
            ps = slice(p * part, (p + 1) * part)
            pre, gh = ready
            if p + 1 < parts:
                ready = entry(p + 1)
            sig = 0.5 * jnp.tanh(0.5 * pre) + 0.5
            act = pre * sig
            gp = gh * (sig + act * (1.0 - sig))
            gbup[p] = gbup[p] + jnp.sum(gp, axis=0, keepdims=True)
            act, gp = act.astype(BF16), gp.astype(BF16)
            hid[rs, ps] = act
            gpre[rs, ps] = gp
            x, y = mm(act, w_down[ps, :]), mm_t(gp, w_up[:, ps])
            total, gin = (x, y) if p == 0 else (total + x, gin + y)
        outs[rs, :] = (resid + (total + b_down)).astype(BF16)
        send(outs.at[rs, :], out_hbm.at[rs, :])
        back = cotf + norm_back(gin * gain, normed, factor)
        gres[rs, :] = back
        send(gres.at[rs, :], gres_hbm.at[rs, :])
        back = back.astype(BF16)
        gbr[rs, :] = back
        gmix[rs, :] = mm_t(back, w_out[...]).astype(BF16)
        send(gmix.at[rs, :], gmix_hbm.at[rs, :])
        ggain += jnp.sum(gin * normed, axis=0, keepdims=True)
        gbdown += jnp.sum(cotf, axis=0, keepdims=True)

    for p in range(parts):
        ps = slice(p * part, (p + 1) * part)
        w_up[:, ps] = t_mm(fin[...], gpre[:, ps]).astype(BF16)
        send(w_up.at[:, ps], grad_ref.at[:, ps])
    w_out[...] = t_mm(mixed[...], gbr[...]).astype(BF16)
    send(w_out, grad_ref.at[:, pl.ds(2 * ff, d)])
    va = gather_vector(ggain, 0, n, r)
    vb = gather_vector(jnp.concatenate(gbup, axis=1), 0, n, r * mult)
    vc = gather_vector(gbdown, 0, n, r)
    row = iota((r, 128), 0)
    pick = lambda v, j, i, rest: jnp.where(row == i, jnp.broadcast_to(v[j : j + 1].astype(F32), (r, 128)), rest)
    for j in range(n):
        tile = pick(va, j, 1, pick(vb, j, 2, pick(vc, j, 3, jnp.zeros((r, 128), F32))))
        vecs[j * r : (j + 1) * r, :] = tile.astype(BF16)
    send(vecs, grad_ref.at[:, pl.ds(2 * ff + d, 128)])
    for p in range(parts):
        ps = slice(p * part, (p + 1) * part)
        w_down[ps, :] = t_mm(hid[:, ps], cot[...]).astype(BF16)
        count = part // r
        for i in range(p * count, (p + 1) * count):
            send(down[i][1], grad_ref.at[pl.ds(i // mult * r, r), pl.ds(ff + i % mult * d, d)])
    for c in sent:
        c.wait()


def ffn(mixed, tokens, cot, full, ff, n):
    t, d = tokens.shape
    hbm = pl.BlockSpec(memory_space=pl.ANY)
    moves = n * (ff // d)
    return pl.pallas_call(
        partial(ffn_kernel, n),
        in_specs=[hbm] * 4,
        out_specs=[hbm] * 4,
        out_shape=[
            jax.ShapeDtypeStruct((t, d), BF16),
            jax.ShapeDtypeStruct((t, d), F32),
            jax.ShapeDtypeStruct((t, d), BF16),
            jax.ShapeDtypeStruct(full.shape, BF16),
        ],
        scratch_shapes=[pltpu.VMEM((t, d), BF16)] * 4
        + [pltpu.VMEM((t, d), F32), pltpu.VMEM((t, d), BF16)]
        + [
            pltpu.VMEM((d, d), BF16),
            pltpu.VMEM((d, ff), BF16),
            pltpu.VMEM((ff, d), BF16),
            pltpu.VMEM((d, 128), BF16),
            pltpu.VMEM((t, ff), BF16),
            pltpu.VMEM((t, ff), BF16),
            pltpu.VMEM((t, d), BF16),
            pltpu.VMEM((t, d), BF16),
            pltpu.SemaphoreType.DMA((7 + moves,)),
            pltpu.SemaphoreType.DMA((3 * (t // 256) + ff // 512 + 2 + moves,)),
        ],
        compiler_params=pltpu.CompilerParams(vmem_limit_bytes=VMEM_LIMIT),
        cost_estimate=pl.CostEstimate(flops=12 * t * d * ff, bytes_accessed=20 << 20, transcendentals=t * ff),
        name="ffn",
    )(mixed, tokens, cot, full)


def read_back_kernel(pack_ref, gmix_ref, read_ref, score_ref, inv_ref, kts_ref, mvs_ref,
                     gq_ref, a_ref, u_ref, gtot_ref, st_ref, gk_ref, gv_ref, gt_ref):
    rows, d = gmix_ref.shape

    @pl.when(pl.program_id(0) == 0)
    def _():
        gk_ref[...] = jnp.zeros_like(gk_ref)
        gv_ref[...] = jnp.zeros_like(gv_ref)
        gt_ref[...] = jnp.zeros_like(gt_ref)

    c = CHUNK
    units = [(b, g) for b in range(rows // c) for g in range(d // QUAD)]
    at = {(b, g): (slice(b * c, (b + 1) * c), slice(g * QUAD, (g + 1) * QUAD)) for b, g in units}
    part = lambda p: {(b, g): pack_ref[at[b, g][0], p * d + g * QUAD : p * d + (g + 1) * QUAD] for b, g in units}
    q, k, v = part(0), part(1), part(2)
    written = {x: jnp.exp(y.astype(F32)).astype(BF16) for x, y in part(3).items()}
    wb = {x: blocks_of(written[x]) for x in units}
    gm = {x: gmix_ref[at[x]] for x in units}
    gpair = {x: tri(mm(gm[x], blocks_t(v[x])), True) for x in units}
    weighted = {x: (mm(gpair[x], wb[x]) + mm_t(gm[x], mvs_ref[x])) * inv_ref[at[x]] * read_ref[at[x]] for x in units}
    gscore = {x: weighted[x] - read_ref[at[x]] * per_head(weighted[x], jnp.sum, 0.0) for x in units}
    a, u = {}, {}
    for x in units:
        inv = inv_ref[at[x]]
        a[x] = (gscore[x] * inv * SCALE).astype(BF16)
        u[x] = (read_ref[at[x]] * inv).astype(BF16)
        a_ref[at[x]] = a[x]
        u_ref[at[x]] = u[x]
        gtot = (gscore[x] * score_ref[at[x]] + weighted[x]) * inv
        gtot_ref[at[x]] = gtot
        gt_ref[0:1, at[x][1]] += jnp.sum(gtot, axis=0, keepdims=True)
    spair = {x: tri(mm(a[x], blocks_t(written[x])), True) for x in units}
    for x in units:
        gq_ref[at[x]] = (mm(spair[x], blocks_of(k[x])) + mm_t(a[x], kts_ref[x])).astype(BF16)
    for g in range(d // QUAD):
        s = slice(g * QUAD, (g + 1) * QUAD)
        every = lambda y: jnp.concatenate([y[b, g] for b in range(rows // c)], axis=0)
        gk_ref[g] += t_mm(every(a), every(q))
        gv_ref[g] += t_mm(every(u), every(gm))

    @pl.when(pl.program_id(0) == pl.num_programs(0) - 1)
    def _():
        store_state(st_ref, gk_ref, gv_ref, gt_ref)


def read_back(packed, gmix, read, score, inv, kts, mvs, rows=512):
    t, wide = packed.shape
    d = wide // 4
    g = d // QUAD
    const = lambda *shape: pl.BlockSpec(shape, lambda i: (0,) * len(shape))
    per = rows // CHUNK
    row = lambda w: pl.BlockSpec((rows, w), lambda i: (i, 0))
    st = pl.BlockSpec((per, g, QUAD, QUAD), lambda i: (i, 0, 0, 0))
    return pl.pallas_call(
        read_back_kernel,
        grid=(t // rows,),
        in_specs=[row(wide), row(d), row(d), row(d), row(d), st, st],
        out_specs=[row(d)] * 4 + [const(g, STATE, QUAD)],
        out_shape=[jax.ShapeDtypeStruct((t, d), BF16)] * 3 + [jax.ShapeDtypeStruct((t, d), F32)]
        + [jax.ShapeDtypeStruct((g, STATE, QUAD), F32)],
        scratch_shapes=[pltpu.VMEM((g, QUAD, QUAD), F32), pltpu.VMEM((g, QUAD, QUAD), F32), pltpu.VMEM((8, d), F32)],
        compiler_params=pltpu.CompilerParams(vmem_limit_bytes=VMEM_LIMIT),
        cost_estimate=pl.CostEstimate(flops=6 * 10**9, bytes_accessed=20 << 20, transcendentals=t * d),
        name="read_back",
    )(packed, gmix, read, score, inv, kts, mvs)


def write_back_kernel(n, me_ref, pack_ref, gmix_ref, a_ref, u_ref, gtot_ref, st_in, att_hbm, gq_hbm, out_ref, *refs):
    share_refs = refs[:4]
    gk, gv, gt, att, gq, grads, acc, isems, sems = refs[4:]
    rows, d = gmix_ref.shape
    loads = [pltpu.make_async_copy(att_hbm, att, isems.at[0]), pltpu.make_async_copy(gq_hbm, gq, isems.at[1])]

    @pl.when(pl.program_id(0) == 0)
    def _():
        for x in loads:
            x.start()
        load_state(st_in, gk, gv, gt)

    base = (pl.num_programs(0) - 1 - pl.program_id(0)) * rows
    c = CHUNK
    square = head_square()
    ones = (iota((c, c), 0) <= iota((c, c), 1)).astype(BF16)
    units = [(b, g) for b in reversed(range(rows // c)) for g in range(d // QUAD)]
    at = {(b, g): (slice(b * c, (b + 1) * c), slice(g * QUAD, (g + 1) * QUAD)) for b, g in units}
    part = lambda p: {(b, g): pack_ref[at[b, g][0], p * d + g * QUAD : p * d + (g + 1) * QUAD] for b, g in units}
    q, k, v = part(0), part(1), part(2)
    wf = {x: jnp.exp(y.astype(F32)) for x, y in part(3).items()}
    written = {x: wf[x].astype(BF16) for x in units}
    gm, a, u = ({x: ref[at[x]] for x in units} for ref in (gmix_ref, a_ref, u_ref))
    qb, gb, ab, ub = ({x: blocks_of(y[x]) for x in units} for y in (q, gm, a, u))
    gkb, gvb, after = {}, {}, {}
    for x in units:
        g = x[1]
        gkb[x], gvb[x] = gk[g].astype(BF16), gv[g].astype(BF16)
        gk[g] += jnp.where(square, t_mm(a[x], q[x]), 0.0)
        gv[g] += jnp.where(square, t_mm(u[x], gm[x]), 0.0)
        hi, lo = hi_lo(gtot_ref[at[x]])
        after[x] = mm(ones, hi) + mm(ones, lo) + gt[0:1, at[x][1]]
        gt[0:1, at[x][1]] = after[x][0:1, :]

    def out(p, x, y):
        y = y.astype(BF16)
        cols = slice(p * d + x[1] * QUAD, p * d + (x[1] + 1) * QUAD)
        out_ref[at[x][0], cols] = y
        grads[pl.ds(pl.multiple_of(base + x[0] * c, c), c), cols] = y

    st = {x: tri(mm(written[x], blocks_t(a[x])), False) for x in units}
    rt = {x: tri(mm(written[x], blocks_t(u[x])), False) for x in units}
    for x in units:
        out(0, x, mm(st[x], qb[x]) + mm(written[x], gkb[x]))
    for x in units:
        out(1, x, mm(rt[x], gb[x]) + mm(written[x], gvb[x]))
    pt = {x: tri(mm(k[x], blocks_t(q[x])), False) for x in units}
    gp = {x: tri(mm(v[x], blocks_t(gm[x])), False) for x in units}
    for x in units:
        gw = mm(pt[x], ab[x]) + mm(gp[x], ub[x]) + mm_t(k[x], gkb[x]) + mm_t(v[x], gvb[x])
        out(2, x, wf[x] * (gw - after[x]))

    @pl.when(pl.program_id(0) == pl.num_programs(0) - 1)
    def _():
        for x in loads:
            x.wait()
        r = d // n
        me = me_ref[0]
        acc[:, 0:d] = t_mm(att[...], gq[...]).astype(BF16)
        for p in range(3):
            acc[:, (p + 1) * d : (p + 2) * d] = t_mm(att[...], grads[:, p * d : (p + 1) * d]).astype(BF16)
        outs = []
        for j in range(n):
            frm = pl.multiple_of((me ^ j) * r, r)
            dst = share_refs[j % 4].at[j // 4]
            outs.append(pltpu.make_async_copy(acc.at[pl.ds(frm, r), :], dst, sems.at[j]))
        for x in outs:
            x.start()
        for x in outs:
            x.wait()


def write_back(me, packed, gmix, a, u, gtot, state, att, gq, n, rows=256):
    t, wide = packed.shape
    d = wide // 4
    g = d // QUAD
    r = d // n
    last = t // rows - 1
    const = lambda *shape: pl.BlockSpec(shape, lambda i: (0,) * len(shape))
    row = lambda w: pl.BlockSpec((rows, w), lambda i: (last - i, 0))
    hbm = pl.BlockSpec(memory_space=pl.ANY)
    return pl.pallas_call(
        partial(write_back_kernel, n),
        grid=(t // rows,),
        in_specs=[pl.BlockSpec(memory_space=pltpu.SMEM), row(wide), row(d), row(d), row(d), row(d), const(g, STATE, QUAD), hbm, hbm],
        out_specs=[row(3 * d)] + [hbm] * 4,
        out_shape=[jax.ShapeDtypeStruct((t, 3 * d), BF16)] + [jax.ShapeDtypeStruct((n // 4, r, wide), BF16)] * 4,
        scratch_shapes=[
            pltpu.VMEM((g, QUAD, QUAD), F32),
            pltpu.VMEM((g, QUAD, QUAD), F32),
            pltpu.VMEM((8, d), F32),
            pltpu.VMEM((t, d), BF16),
            pltpu.VMEM((t, d), BF16),
            pltpu.VMEM((t, 3 * d), BF16),
            pltpu.VMEM((d, wide), BF16),
            pltpu.SemaphoreType.DMA((2,)),
            pltpu.SemaphoreType.DMA((n,)),
        ],
        compiler_params=pltpu.CompilerParams(vmem_limit_bytes=VMEM_LIMIT),
        cost_estimate=pl.CostEstimate(flops=11 * 10**9, bytes_accessed=18 << 20, transcendentals=t * d),
        name="write_back",
    )(me, packed, gmix, a, u, gtot, state, att, gq)


def input_grad_kernel(gain_ref, tok_ref, gq_ref, gkvc_ref, w_ref, gres_ref, out_ref):
    d = tok_ref.shape[1]
    gain = gain_ref[0:1, :]
    gin = mm_t(gq_ref[...], w_ref[:, 0:d]) + mm_t(gkvc_ref[...], w_ref[:, d:])
    normed, factor = normalize(tok_ref[...].astype(F32))
    out_ref[...] = gres_ref[...] + norm_back(gin * gain, normed, factor)


def input_grad(gain, tokens, gq, gkvc, w, gres, rows=256):
    t, d = tokens.shape
    const = lambda *shape: pl.BlockSpec(shape, lambda i: (0,) * len(shape))
    row = lambda w: pl.BlockSpec((rows, w), lambda i: (i, 0))
    return pl.pallas_call(
        input_grad_kernel,
        grid=(t // rows,),
        in_specs=[const(8, d), row(d), row(d), row(3 * d), const(d, 4 * d), row(d)],
        out_specs=row(d),
        out_shape=jax.ShapeDtypeStruct((t, d), F32),
        compiler_params=pltpu.CompilerParams(vmem_limit_bytes=VMEM_LIMIT),
        cost_estimate=pl.CostEstimate(flops=8 * t * d * d, bytes_accessed=12 << 20, transcendentals=0),
        name="input_grad",
    )(gain, tokens, gq, gkvc, w, gres)


def swap(x, mask, n):
    return lax.ppermute(x, "fsdp", [(i, i ^ mask) for i in range(n)])


def after(x, *first):
    return lax.optimization_barrier((x, *first))[0]


def add(*items):
    return sum(x.astype(F32) for x in items).astype(BF16)


def along_z(shard, n):
    return [shard] + [swap(shard, 4 * k, n) for k in range(1, n // 4)]


def along_x(own, n):
    return [swap(x, 2, n) for x in own]


def shift(x, by, seqs):
    return lax.ppermute(x, "seq", [(i, i + by) for i in range(seqs) if 0 <= i + by < seqs])


def others(state, direction, seqs):
    if seqs == 1:
        return jnp.zeros_like(state)
    total = shift(state, direction, seqs)
    step = 1
    while step < seqs - 1:
        total = total + shift(total, direction * step, seqs)
        step *= 2
    return total


def on_device(n, seqs, tokens, w_query, w_key, w_value, w_control, w_out, w_up, w_down,
              gain_attn, gain_ffn, bias_up, bias_down, cotangent):
    r, d = w_query.shape
    ff = w_up.shape[1]
    mult = ff // d
    me = lax.axis_index("fsdp").astype(jnp.int32).reshape(1)
    first, second = pack(w_query, w_key, w_value, w_control, w_out, w_up, w_down, gain_attn, gain_ffn, bias_up, bias_down)
    depth = n // 4
    own = along_z(first, n)
    full = lax.all_gather(second, "fsdp", axis=0, tiled=True)
    across = along_x(own, n)
    cored = [[swap(x, 1, n) for x in group] for group in (own, across)]
    att_pieces = [x for quad in zip(own, cored[0], across, cored[1]) for x in quad]
    att_where = [(j, None) for j in range(n)]
    att, packed, state, w_att, gain = project(me, tokens, att_where, att_pieces)
    mixed, read, score, inv, kts, mvs = mix(packed, others(state, 1, seqs))
    layer_out, gres, gmix, ffn_grad = ffn(mixed, tokens, cotangent, full, ff, n)
    ffn_sum = lax.psum_scatter(ffn_grad, "fsdp", scatter_dimension=0, tiled=True)

    def core_sum(shares):
        near, near_core, far, far_core = shares
        return add(near, swap(near_core, 1, n)), add(far, swap(far_core, 1, n))

    def seq_sum(x):
        step = 1
        while step < seqs:
            x = add(x, lax.ppermute(x, "seq", [(i, i ^ step) for i in range(seqs)]))
            step *= 2
        return x.astype(F32)

    gq, a, u, gtot, gstate = read_back(packed, gmix, read, score, inv, kts, mvs)
    gkvc, *shares = write_back(me, packed, gmix, a, u, gtot, others(gstate, -1, seqs), att, gq, n)
    near, far = core_sum(shares)
    grad_tokens = input_grad(gain, tokens, after(gq, near, far), gkvc, w_att, gres)
    mine = {k: add(near[k], swap(far[k], 2, n)) for k in range(depth - 1, -1, -1)}
    sent = {k: swap(mine[k], 4 * k, n) if k else mine[k] for k in range(depth)}
    ffn_share = seq_sum(ffn_sum)
    att_share = seq_sum(add(*sent.values()))
    gain_share = jnp.sum(att_share * first[:, : 4 * d].astype(F32), axis=1) / gain_attn.astype(F32)
    up, down, out, vec = (
        ffn_share[:, :ff],
        ffn_share[:, ff : 2 * ff],
        ffn_share[:, 2 * ff : 2 * ff + d],
        ffn_share[:, 2 * ff + d :],
    )
    down = jnp.concatenate([down[:, m * d : (m + 1) * d] for m in range(mult)], axis=0)
    return (
        layer_out,
        grad_tokens,
        att_share[:, 0:d],
        att_share[:, d : 2 * d],
        att_share[:, 2 * d : 3 * d],
        att_share[:, 3 * d :],
        out,
        up,
        down,
        gain_share,
        vec[1, :r],
        vec[2, : r * mult],
        vec[3, :r],
    )


def solution(mesh):
    tokens = P(("fsdp", "seq"), None)
    matrix = P("fsdp", None)
    vector = P("fsdp")
    return jax.shard_map(
        partial(on_device, mesh.shape["fsdp"], mesh.shape["seq"]),
        mesh=mesh,
        in_specs=(tokens,) + (matrix,) * 7 + (vector,) * 4 + (tokens,),
        out_specs=(tokens, tokens) + (matrix,) * 7 + (vector,) * 4,
        check_vma=False,
    )
```

```python
from functools import partial
import jax
import jax.numpy as jnp
from jax import lax
from jax.experimental import pallas as pl
from jax.experimental.pallas import tpu as pltpu
from jax.sharding import PartitionSpec as P

F32 = jnp.float32
BF16 = jnp.bfloat16
HEAD = 64
QUAD = 256
SCALE = HEAD ** -0.5
CHUNK = 128
VMEM_LIMIT = 60 * 1024 * 1024


def mm(a, b):
    return lax.dot_general(a, b, (((1,), (0,)), ((), ())), preferred_element_type=F32)


def mm_t(a, b):
    return lax.dot_general(a, b, (((1,), (1,)), ((), ())), preferred_element_type=F32)


def t_mm(a, b):
    return lax.dot_general(a, b, (((0,), (0,)), ((), ())), preferred_element_type=F32)


def iota(shape, dim):
    return lax.broadcasted_iota(jnp.int32, shape, dim)


def normalize(x):
    centred = x - jnp.mean(x, axis=-1, keepdims=True)
    spread = jnp.mean(centred * centred, axis=-1, keepdims=True)
    factor = lax.rsqrt(spread + 1e-05)
    return centred * factor, factor


def norm_back(g, normed, factor):
    first = jnp.mean(g, axis=-1, keepdims=True)
    second = jnp.mean(g * normed, axis=-1, keepdims=True)
    return factor * (g - first - normed * second)


def blocks_of(x):
    lane = iota(x.shape, 1) // HEAD
    zero = jnp.zeros_like(x)
    return jnp.concatenate([jnp.where(lane == h, x, zero) for h in range(4)], axis=0)


def blocks_t(x):
    xt = x.T
    row = iota(xt.shape, 0) // HEAD
    zero = jnp.zeros_like(xt)
    return jnp.concatenate([jnp.where(row == h, xt, zero) for h in range(4)], axis=1)


def tri(x, lower):
    c = x.shape[0]
    row, col = iota(x.shape, 0), iota(x.shape, 1) % c
    keep = row >= col if lower else row <= col
    return jnp.where(keep, x, 0.0).astype(BF16)


def per_head(x, op, neutral):
    parts = []
    for p in range(x.shape[1] // 128):
        v = x[:, p * 128 : (p + 1) * 128]
        low = iota(v.shape, 1) < HEAD
        a = op(jnp.where(low, v, neutral), axis=-1, keepdims=True)
        b = op(jnp.where(low, neutral, v), axis=-1, keepdims=True)
        parts.append(jnp.where(low, a, b))
    return jnp.concatenate(parts, axis=1)


def head_square():
    return iota((QUAD, QUAD), 0) // HEAD == iota((QUAD, QUAD), 1) // HEAD


STATE = 2 * HEAD + 16


def store_state(st_ref, first, second, total):
    square = head_square()
    for g in range(st_ref.shape[0]):
        for k, ref in enumerate((first, second)):
            x = jnp.where(square, ref[g], 0.0)
            st_ref[g, k * HEAD : (k + 1) * HEAD, :] = (x[0:64] + x[64:128] + x[128:192] + x[192:256]).astype(BF16)
        hi, lo = hi_lo(total[0:1, g * QUAD : (g + 1) * QUAD])
        row = iota((16, QUAD), 0)
        spread = lambda x: jnp.broadcast_to(x.astype(F32), (16, QUAD))
        st_ref[g, 2 * HEAD :, :] = jnp.where(row == 0, spread(hi), jnp.where(row == 1, spread(lo), 0.0)).astype(BF16)


def load_state(st_ref, first, second, total):
    square = head_square()
    for g in range(st_ref.shape[0]):
        for k, ref in enumerate((first, second)):
            x = st_ref[g, k * HEAD : (k + 1) * HEAD, :].astype(F32)
            ref[g] = jnp.where(square, jnp.concatenate([x] * 4, axis=0), 0.0)
        both = jnp.sum(st_ref[g, 2 * HEAD :, :].astype(F32), axis=0, keepdims=True)
        total[:, g * QUAD : (g + 1) * QUAD] = jnp.broadcast_to(both, (8, QUAD))


def hi_lo(x):
    hi = x.astype(BF16)
    return hi, (x - hi.astype(F32)).astype(BF16)


def spread_vector(vecs, me, n, r, k, each, total):
    pick = (iota((n, n * r), 1) == iota((n, n * r), 0) * r + k).astype(BF16)
    rows = mm(pick, vecs).astype(BF16)
    tile = (iota((128, total), 1) % each == iota((128, total), 0)).astype(BF16)
    wide = mm(rows, tile)
    own = iota((n, total), 1) // each == (iota((n, total), 0) ^ me)
    return jnp.sum(jnp.where(own, wide, 0.0), axis=0, keepdims=True)


def gather_vector(vec, me, n, each):
    total = vec.shape[1]
    own = iota((n, total), 1) // each == (iota((n, total), 0) ^ me)
    wide = jnp.where(own, vec, 0.0).astype(BF16)
    tile = (iota((128, total), 1) % each == iota((128, total), 0)).astype(BF16)
    return mm_t(wide, tile).astype(BF16)


def piece_refs(where, refs):
    return [refs[a] if row is None else refs[a].at[row] for a, row in where]


def pack_kernel(q, k, v, c, o, up, down, gain_a, gain_f, b_up, b_down, first, second):
    r, d = q.shape
    ff = up.shape[1]
    for p, ref in enumerate((q, k, v, c)):
        first[:, p * d : (p + 1) * d] = ref[...]
    tile = jnp.zeros((r, 128), F32)
    row, col = iota((r, 128), 0), iota((r, 128), 1)
    for i, ref in enumerate((gain_a, gain_f, b_up, b_down)):
        length = ref.shape[1]
        wide = jnp.broadcast_to(ref[...].astype(F32), (r, length))
        if length < 128:
            wide = jnp.concatenate([wide, jnp.zeros((r, 128 - length), F32)], axis=1)
        tile = jnp.where(row == i, wide, tile)
    first[:, 4 * d :] = tile.astype(BF16)
    second[:, 2 * ff + d :] = tile.astype(BF16)
    second[:, :ff] = up[...]
    for m in range(ff // d):
        second[:, ff + m * d : ff + (m + 1) * d] = down[m * r : (m + 1) * r, :]
    second[:, 2 * ff : 2 * ff + d] = o[...]


def pack(q, k, v, c, o, up, down, gain_a, gain_f, b_up, b_down):
    r, d = q.shape
    ff = up.shape[1]
    return pl.pallas_call(
        pack_kernel,
        out_shape=[jax.ShapeDtypeStruct((r, 4 * d + 128), BF16), jax.ShapeDtypeStruct((r, 2 * ff + d + 128), BF16)],
        cost_estimate=pl.CostEstimate(flops=0, bytes_accessed=1 << 20, transcendentals=0),
        name="pack",
    )(q, k, v, c, o, up, down, *(x.reshape(1, -1) for x in (gain_a, gain_f, b_up, b_down)))


def stack_kernel(*refs):
    for i, ref in enumerate(refs[:-1]):
        refs[-1][i] = ref[...]


def stack(items):
    return pl.pallas_call(
        stack_kernel,
        out_shape=jax.ShapeDtypeStruct((len(items),) + items[0].shape, items[0].dtype),
        cost_estimate=pl.CostEstimate(flops=0, bytes_accessed=2 << 20, transcendentals=0),
        name="stack",
    )(*items)


def project_kernel(where, arrays, r, me_ref, tok_hbm, *refs):
    n = len(where)
    pieces = piece_refs(where, refs)
    (att_hbm, pack_hbm, st_ref, w_hbm, gain_ref,
     tok, att, pack, w_all, vecs, normed, written, first, second, total, sems, vsems, tsem, osems) = refs[arrays:]
    t, d = att.shape
    wide = 4 * d
    rows = 256
    me = me_ref[0]
    load = pltpu.make_async_copy(tok_hbm, tok, tsem)
    load.start()
    vector_copies, copies = [], []
    for j in range(n):
        at = pl.multiple_of((me ^ j) * r, r)
        copies.append(pltpu.make_async_copy(pieces[j].at[:, pl.ds(0, wide)], w_all.at[pl.ds(at, r), :], sems.at[j]))
        vector_copies.append(pltpu.make_async_copy(pieces[j].at[:, pl.ds(wide, 128)], vecs.at[pl.ds(j * r, r), :], vsems.at[j]))
    for c in vector_copies + copies:
        c.start()
    sent = []

    def send(src, dst):
        copy = pltpu.make_async_copy(src, dst, osems.at[len(sent)])
        copy.start()
        sent.append(copy)

    load.wait()
    for i in range(t // rows):
        rs = pl.ds(i * rows, rows)
        normed[rs, :], _ = normalize(tok[rs, :].astype(F32))
    for c in vector_copies:
        c.wait()
    gain = spread_vector(vecs[...], me, n, r, 0, r, d)
    gain_ref[...] = jnp.broadcast_to(gain, gain_ref.shape)
    for c in copies:
        c.wait()
    send(w_all, w_hbm)
    sums = jnp.zeros((1, d), F32)
    for i in range(t // rows):
        rs = pl.ds(i * rows, rows)
        x = (normed[rs, :] * gain).astype(BF16)
        att[rs, :] = x
        send(att.at[rs, :], att_hbm.at[rs, :])
        for p in (3, 1, 2, 0):
            full = mm(x, w_all[:, p * d : (p + 1) * d]).astype(BF16)
            pack[rs, p * d : (p + 1) * d] = full
            if p == 3:
                new = jnp.exp(full.astype(F32)).astype(BF16)
                written[rs, :] = new
                sums += jnp.sum(new.astype(F32), axis=0, keepdims=True)
        send(pack.at[rs, :], pack_hbm.at[rs, :])
    for g in range(d // QUAD):
        s = slice(g * QUAD, (g + 1) * QUAD)
        first[g] = t_mm(pack[:, d + g * QUAD : d + (g + 1) * QUAD], written[:, s])
        second[g] = t_mm(written[:, s], pack[:, 2 * d + g * QUAD : 2 * d + (g + 1) * QUAD])
    total[...] = jnp.broadcast_to(sums, total.shape)
    store_state(st_ref, first, second, total)
    for c in sent:
        c.wait()


def project(me, tokens, where, pieces):
    t, d = tokens.shape
    n = len(where)
    r = d // n
    wide = 4 * d
    g = d // QUAD
    hbm = pl.BlockSpec(memory_space=pl.ANY)
    vmem = pl.BlockSpec(memory_space=pltpu.VMEM)
    return pl.pallas_call(
        partial(project_kernel, where, len(pieces), r),
        in_specs=[pl.BlockSpec(memory_space=pltpu.SMEM)] + [hbm] * (1 + len(pieces)),
        out_specs=[hbm, hbm, vmem, hbm, vmem],
        out_shape=[
            jax.ShapeDtypeStruct((t, d), BF16),
            jax.ShapeDtypeStruct((t, wide), BF16),
            jax.ShapeDtypeStruct((g, STATE, QUAD), BF16),
            jax.ShapeDtypeStruct((d, wide), BF16),
            jax.ShapeDtypeStruct((8, d), F32),
        ],
        scratch_shapes=[
            pltpu.VMEM((t, d), BF16),
            pltpu.VMEM((t, d), BF16),
            pltpu.VMEM((t, wide), BF16),
            pltpu.VMEM((d, wide), BF16),
            pltpu.VMEM((n * r, 128), BF16),
            pltpu.VMEM((t, d), F32),
            pltpu.VMEM((t, d), BF16),
            pltpu.VMEM((g, QUAD, QUAD), F32),
            pltpu.VMEM((g, QUAD, QUAD), F32),
            pltpu.VMEM((8, d), F32),
            pltpu.SemaphoreType.DMA((n,)),
            pltpu.SemaphoreType.DMA((n,)),
            pltpu.SemaphoreType.DMA,
            pltpu.SemaphoreType.DMA((1 + 2 * (t // 256),)),
        ],
        compiler_params=pltpu.CompilerParams(vmem_limit_bytes=VMEM_LIMIT),
        cost_estimate=pl.CostEstimate(flops=2 * t * d * wide, bytes_accessed=12 << 20, transcendentals=t * d),
        name="project",
    )(me, tokens, *pieces)


def mix_kernel(pack_ref, st_in, mix_ref, read_ref, score_ref, inv_ref, kts_ref, mvs_ref, kt, mv, tot):
    d = mix_ref.shape[1]
    rows = mix_ref.shape[0]

    @pl.when(pl.program_id(0) == 0)
    def _():
        load_state(st_in, kt, mv, tot)

    c = CHUNK
    square = head_square()
    ones = (iota((c, c), 0) >= iota((c, c), 1)).astype(BF16)
    units = [(b, g) for b in range(rows // c) for g in range(d // QUAD)]
    at = {(b, g): (slice(b * c, (b + 1) * c), slice(g * QUAD, (g + 1) * QUAD)) for b, g in units}
    part = lambda p: {(b, g): pack_ref[at[b, g][0], p * d + g * QUAD : p * d + (g + 1) * QUAD] for b, g in units}
    q, k, v = part(0), part(1), part(2)
    written = {x: jnp.exp(y.astype(F32)).astype(BF16) for x, y in part(3).items()}
    wb = {x: blocks_of(written[x]) for x in units}
    pairs = {x: tri(mm(q[x], blocks_t(k[x])), True) for x in units}
    ktb, mvb, inv = {}, {}, {}
    for x in units:
        b, g = x
        ktb[x], mvb[x] = kt[g].astype(BF16), mv[g].astype(BF16)
        kts_ref[b, g] = ktb[x]
        mvs_ref[b, g] = mvb[x]
        kt[g] += jnp.where(square, t_mm(k[x], written[x]), 0.0)
        mv[g] += jnp.where(square, t_mm(written[x], v[x]), 0.0)
        total = mm(ones, written[x]) + tot[0:1, at[x][1]]
        tot[0:1, at[x][1]] = total[c - 1 : c, :]
        inv[x] = 1.0 / total
        inv_ref[at[x]] = inv[x]
    score = {x: (mm(pairs[x], wb[x]) + mm(q[x], ktb[x])) * SCALE * inv[x] for x in units}
    for x in units:
        score_ref[at[x]] = score[x]
    e = {x: jnp.exp(score[x] - per_head(score[x], jnp.max, -jnp.inf)) for x in units}
    read = {x: e[x] / per_head(e[x], jnp.sum, 0.0) for x in units}
    for x in units:
        read_ref[at[x]] = read[x]
    scaled = {x: (read[x] * inv[x]).astype(BF16) for x in units}
    recall = {x: tri(mm(scaled[x], blocks_t(written[x])), True) for x in units}
    for x in units:
        mix_ref[at[x]] = (mm(recall[x], blocks_of(v[x])) + mm(scaled[x], mvb[x])).astype(BF16)


def mix(packed, state, rows=256):
    t, wide = packed.shape
    d = wide // 4
    g = d // QUAD
    const = lambda *shape: pl.BlockSpec(shape, lambda i: (0,) * len(shape))
    per = rows // CHUNK
    row = lambda w: pl.BlockSpec((rows, w), lambda i: (i, 0))
    return pl.pallas_call(
        mix_kernel,
        grid=(t // rows,),
        in_specs=[row(wide), const(g, STATE, QUAD)],
        out_specs=[row(d)] * 4 + [pl.BlockSpec((per, g, QUAD, QUAD), lambda i: (i, 0, 0, 0))] * 2,
        out_shape=[jax.ShapeDtypeStruct((t, d), BF16)] + [jax.ShapeDtypeStruct((t, d), F32)] * 3
        + [jax.ShapeDtypeStruct((t // CHUNK, g, QUAD, QUAD), BF16)] * 2,
        scratch_shapes=[pltpu.VMEM((g, QUAD, QUAD), F32), pltpu.VMEM((g, QUAD, QUAD), F32), pltpu.VMEM((8, d), F32)],
        compiler_params=pltpu.CompilerParams(vmem_limit_bytes=VMEM_LIMIT),
        cost_estimate=pl.CostEstimate(flops=6 * 10**9, bytes_accessed=16 << 20, transcendentals=2 * t * d),
        name="mix",
    )(packed, state)


def ffn_kernel(n, me_ref, mixed_hbm, tok_hbm, cot_hbm, full_ref, out_hbm, gres_hbm, gmix_hbm, *refs):
    share_refs = refs[:4]
    (mixed, tok, cot, outs, gres, gmix, w_out, w_up, w_down, vecs, hid, gpre, fin, gbr, sems, osems) = refs[4:]
    me = me_ref[0]
    t, d = mixed.shape
    ff = w_up.shape[1]
    r = d // n
    mult = ff // d
    rows = 256
    part = 512
    steps = t // rows
    parts = ff // part

    def load(src, dst, i):
        copy = pltpu.make_async_copy(src, dst, sems.at[i])
        copy.start()
        return copy

    down_sem = 3
    early = [
        load(full_ref.at[:, pl.ds(2 * ff, d)], w_out, 0),
        load(mixed_hbm, mixed, 1),
        load(tok_hbm, tok, 2),
        load(full_ref.at[:, pl.ds(2 * ff + d, 128)], vecs, 4),
        load(full_ref.at[:, pl.ds(0, ff)], w_up, 5),
    ]
    late = [load(cot_hbm, cot, 6)]
    down = []
    for j in range(n):
        for m in range(mult):
            down.append((full_ref.at[pl.ds(j * r, r), pl.ds(ff + m * d, d)], w_down.at[pl.ds((j * mult + m) * r, r), :]))
    late += [load(src, dst, 7 + i) for i, (src, dst) in enumerate(down)]
    for c in early:
        c.wait()
    gain = spread_vector(vecs[...], 0, n, r, 1, r, d)
    b_up = spread_vector(vecs[...], 0, n, r, 2, r * mult, ff)
    b_down = spread_vector(vecs[...], 0, n, r, 3, r, d)

    sent = []

    def send(src, dst):
        copy = pltpu.make_async_copy(src, dst, osems.at[len(sent)])
        copy.start()
        sent.append(copy)

    ggain = jnp.zeros((1, d), F32)
    gbdown = jnp.zeros((1, d), F32)
    gbup = [jnp.zeros((1, part), F32)] * parts
    for i in range(steps):
        rs = pl.ds(i * rows, rows)
        resid = tok[rs, :].astype(F32) + mm(mixed[rs, :], w_out[...])
        normed, factor = normalize(resid)
        ffn_in = (normed * gain).astype(BF16)
        fin[rs, :] = ffn_in
        if i == 0:
            for c in late:
                c.wait()
        cot_b = cot[rs, :]
        cotf = cot_b.astype(F32)

        def entry(p):
            ps = slice(p * part, (p + 1) * part)
            return mm(ffn_in, w_up[:, ps]) + b_up[:, ps], mm_t(cot_b, w_down[ps, :])

        ready = entry(0)
        total = gin = None
        for p in range(parts):
            ps = slice(p * part, (p + 1) * part)
            pre, gh = ready
            if p + 1 < parts:
                ready = entry(p + 1)
            sig = 0.5 * jnp.tanh(0.5 * pre) + 0.5
            act = pre * sig
            gp = gh * (sig + act * (1.0 - sig))
            gbup[p] = gbup[p] + jnp.sum(gp, axis=0, keepdims=True)
            act, gp = act.astype(BF16), gp.astype(BF16)
            hid[rs, ps] = act
            gpre[rs, ps] = gp
            x, y = mm(act, w_down[ps, :]), mm_t(gp, w_up[:, ps])
            total, gin = (x, y) if p == 0 else (total + x, gin + y)
        outs[rs, :] = (resid + (total + b_down)).astype(BF16)
        send(outs.at[rs, :], out_hbm.at[rs, :])
        back = cotf + norm_back(gin * gain, normed, factor)
        gres[rs, :] = back
        send(gres.at[rs, :], gres_hbm.at[rs, :])
        back = back.astype(BF16)
        gbr[rs, :] = back
        gmix[rs, :] = mm_t(back, w_out[...]).astype(BF16)
        send(gmix.at[rs, :], gmix_hbm.at[rs, :])
        ggain += jnp.sum(gin * normed, axis=0, keepdims=True)
        gbdown += jnp.sum(cotf, axis=0, keepdims=True)

    def share(j, rows_of, ref, at, width):
        send(ref.at[rows_of(me ^ j), :], share_refs[j % 4].at[j // 4, :, pl.ds(at, width)])

    own_rows = lambda f: pl.ds(pl.multiple_of(f * r, r), r)
    for p in range(parts):
        ps = slice(p * part, (p + 1) * part)
        w_up[:, ps] = t_mm(fin[...], gpre[:, ps]).astype(BF16)
    for j in range(n):
        share(j, own_rows, w_up, 0, ff)
    w_out[...] = t_mm(mixed[...], gbr[...]).astype(BF16)
    va = gather_vector(ggain, 0, n, r)
    vb = gather_vector(jnp.concatenate(gbup, axis=1), 0, n, r * mult)
    vc = gather_vector(gbdown, 0, n, r)
    row = iota((r, 128), 0)
    pick = lambda v, j, i, rest: jnp.where(row == i, jnp.broadcast_to(v[j : j + 1].astype(F32), (r, 128)), rest)
    for j in range(n):
        tile = pick(va, j, 1, pick(vb, j, 2, pick(vc, j, 3, jnp.zeros((r, 128), F32))))
        vecs[j * r : (j + 1) * r, :] = tile.astype(BF16)
    for j in range(n):
        share(j, own_rows, w_out, 2 * ff, d)
        share(j, own_rows, vecs, 2 * ff + d, 128)
    for p in range(parts):
        ps = slice(p * part, (p + 1) * part)
        w_down[ps, :] = t_mm(hid[:, ps], cot[...]).astype(BF16)
    for j in range(n):
        for m in range(mult):
            share(j, lambda f: pl.ds(pl.multiple_of((f * mult + m) * r, r), r), w_down, ff + m * d, d)
    for c in sent:
        c.wait()


def ffn(me, mixed, tokens, cot, full, ff, n):
    t, d = tokens.shape
    hbm = pl.BlockSpec(memory_space=pl.ANY)
    moves = n * (ff // d)
    return pl.pallas_call(
        partial(ffn_kernel, n),
        in_specs=[pl.BlockSpec(memory_space=pltpu.SMEM)] + [hbm] * 4,
        out_specs=[hbm] * 7,
        out_shape=[
            jax.ShapeDtypeStruct((t, d), BF16),
            jax.ShapeDtypeStruct((t, d), F32),
            jax.ShapeDtypeStruct((t, d), BF16),
        ]
        + [jax.ShapeDtypeStruct((n // 4, d // n, full.shape[1]), BF16)] * 4,
        scratch_shapes=[pltpu.VMEM((t, d), BF16)] * 4
        + [pltpu.VMEM((t, d), F32), pltpu.VMEM((t, d), BF16)]
        + [
            pltpu.VMEM((d, d), BF16),
            pltpu.VMEM((d, ff), BF16),
            pltpu.VMEM((ff, d), BF16),
            pltpu.VMEM((d, 128), BF16),
            pltpu.VMEM((t, ff), BF16),
            pltpu.VMEM((t, ff), BF16),
            pltpu.VMEM((t, d), BF16),
            pltpu.VMEM((t, d), BF16),
            pltpu.SemaphoreType.DMA((7 + moves,)),
            pltpu.SemaphoreType.DMA((3 * (t // 256) + 3 * n + moves,)),
        ],
        compiler_params=pltpu.CompilerParams(vmem_limit_bytes=VMEM_LIMIT),
        cost_estimate=pl.CostEstimate(flops=12 * t * d * ff, bytes_accessed=20 << 20, transcendentals=t * ff),
        name="ffn",
    )(me, mixed, tokens, cot, full)


def read_back_kernel(pack_ref, gmix_ref, read_ref, score_ref, inv_ref, kts_ref, mvs_ref,
                     gq_ref, a_ref, u_ref, gtot_ref, st_ref, gk_ref, gv_ref, gt_ref):
    rows, d = gmix_ref.shape

    @pl.when(pl.program_id(0) == 0)
    def _():
        gk_ref[...] = jnp.zeros_like(gk_ref)
        gv_ref[...] = jnp.zeros_like(gv_ref)
        gt_ref[...] = jnp.zeros_like(gt_ref)

    c = CHUNK
    units = [(b, g) for b in range(rows // c) for g in range(d // QUAD)]
    at = {(b, g): (slice(b * c, (b + 1) * c), slice(g * QUAD, (g + 1) * QUAD)) for b, g in units}
    part = lambda p: {(b, g): pack_ref[at[b, g][0], p * d + g * QUAD : p * d + (g + 1) * QUAD] for b, g in units}
    q, k, v = part(0), part(1), part(2)
    written = {x: jnp.exp(y.astype(F32)).astype(BF16) for x, y in part(3).items()}
    wb = {x: blocks_of(written[x]) for x in units}
    gm = {x: gmix_ref[at[x]] for x in units}
    gpair = {x: tri(mm(gm[x], blocks_t(v[x])), True) for x in units}
    weighted = {x: (mm(gpair[x], wb[x]) + mm_t(gm[x], mvs_ref[x])) * inv_ref[at[x]] * read_ref[at[x]] for x in units}
    gscore = {x: weighted[x] - read_ref[at[x]] * per_head(weighted[x], jnp.sum, 0.0) for x in units}
    a, u = {}, {}
    for x in units:
        inv = inv_ref[at[x]]
        a[x] = (gscore[x] * inv * SCALE).astype(BF16)
        u[x] = (read_ref[at[x]] * inv).astype(BF16)
        a_ref[at[x]] = a[x]
        u_ref[at[x]] = u[x]
        gtot = (gscore[x] * score_ref[at[x]] + weighted[x]) * inv
        gtot_ref[at[x]] = gtot
        gt_ref[0:1, at[x][1]] += jnp.sum(gtot, axis=0, keepdims=True)
    spair = {x: tri(mm(a[x], blocks_t(written[x])), True) for x in units}
    for x in units:
        gq_ref[at[x]] = (mm(spair[x], blocks_of(k[x])) + mm_t(a[x], kts_ref[x])).astype(BF16)
    for g in range(d // QUAD):
        s = slice(g * QUAD, (g + 1) * QUAD)
        every = lambda y: jnp.concatenate([y[b, g] for b in range(rows // c)], axis=0)
        gk_ref[g] += t_mm(every(a), every(q))
        gv_ref[g] += t_mm(every(u), every(gm))

    @pl.when(pl.program_id(0) == pl.num_programs(0) - 1)
    def _():
        store_state(st_ref, gk_ref, gv_ref, gt_ref)


def read_back(packed, gmix, read, score, inv, kts, mvs, rows=512):
    t, wide = packed.shape
    d = wide // 4
    g = d // QUAD
    const = lambda *shape: pl.BlockSpec(shape, lambda i: (0,) * len(shape))
    per = rows // CHUNK
    row = lambda w: pl.BlockSpec((rows, w), lambda i: (i, 0))
    st = pl.BlockSpec((per, g, QUAD, QUAD), lambda i: (i, 0, 0, 0))
    return pl.pallas_call(
        read_back_kernel,
        grid=(t // rows,),
        in_specs=[row(wide), row(d), row(d), row(d), row(d), st, st],
        out_specs=[row(d)] * 4 + [const(g, STATE, QUAD)],
        out_shape=[jax.ShapeDtypeStruct((t, d), BF16)] * 3 + [jax.ShapeDtypeStruct((t, d), F32)]
        + [jax.ShapeDtypeStruct((g, STATE, QUAD), BF16)],
        scratch_shapes=[pltpu.VMEM((g, QUAD, QUAD), F32), pltpu.VMEM((g, QUAD, QUAD), F32), pltpu.VMEM((8, d), F32)],
        compiler_params=pltpu.CompilerParams(vmem_limit_bytes=VMEM_LIMIT),
        cost_estimate=pl.CostEstimate(flops=6 * 10**9, bytes_accessed=20 << 20, transcendentals=t * d),
        name="read_back",
    )(packed, gmix, read, score, inv, kts, mvs)


def write_back_kernel(n, me_ref, pack_ref, gmix_ref, a_ref, u_ref, gtot_ref, st_in, att_hbm, gq_hbm, out_ref, *refs):
    share_refs = refs[:4]
    gk, gv, gt, att, gq, grads, acc, isems, sems = refs[4:]
    rows, d = gmix_ref.shape
    loads = [pltpu.make_async_copy(att_hbm, att, isems.at[0]), pltpu.make_async_copy(gq_hbm, gq, isems.at[1])]

    @pl.when(pl.program_id(0) == 0)
    def _():
        for x in loads:
            x.start()
        load_state(st_in, gk, gv, gt)

    base = (pl.num_programs(0) - 1 - pl.program_id(0)) * rows
    c = CHUNK
    square = head_square()
    ones = (iota((c, c), 0) <= iota((c, c), 1)).astype(BF16)
    units = [(b, g) for b in reversed(range(rows // c)) for g in range(d // QUAD)]
    at = {(b, g): (slice(b * c, (b + 1) * c), slice(g * QUAD, (g + 1) * QUAD)) for b, g in units}
    part = lambda p: {(b, g): pack_ref[at[b, g][0], p * d + g * QUAD : p * d + (g + 1) * QUAD] for b, g in units}
    q, k, v = part(0), part(1), part(2)
    wf = {x: jnp.exp(y.astype(F32)) for x, y in part(3).items()}
    written = {x: wf[x].astype(BF16) for x in units}
    gm, a, u = ({x: ref[at[x]] for x in units} for ref in (gmix_ref, a_ref, u_ref))
    qb, gb, ab, ub = ({x: blocks_of(y[x]) for x in units} for y in (q, gm, a, u))
    gkb, gvb, after = {}, {}, {}
    for x in units:
        g = x[1]
        gkb[x], gvb[x] = gk[g].astype(BF16), gv[g].astype(BF16)
        gk[g] += jnp.where(square, t_mm(a[x], q[x]), 0.0)
        gv[g] += jnp.where(square, t_mm(u[x], gm[x]), 0.0)
        hi, lo = hi_lo(gtot_ref[at[x]])
        after[x] = mm(ones, hi) + mm(ones, lo) + gt[0:1, at[x][1]]
        gt[0:1, at[x][1]] = after[x][0:1, :]

    def out(p, x, y):
        y = y.astype(BF16)
        cols = slice(p * d + x[1] * QUAD, p * d + (x[1] + 1) * QUAD)
        out_ref[at[x][0], cols] = y
        grads[pl.ds(pl.multiple_of(base + x[0] * c, c), c), cols] = y

    st = {x: tri(mm(written[x], blocks_t(a[x])), False) for x in units}
    rt = {x: tri(mm(written[x], blocks_t(u[x])), False) for x in units}
    for x in units:
        out(0, x, mm(st[x], qb[x]) + mm(written[x], gkb[x]))
    for x in units:
        out(1, x, mm(rt[x], gb[x]) + mm(written[x], gvb[x]))
    pt = {x: tri(mm(k[x], blocks_t(q[x])), False) for x in units}
    gp = {x: tri(mm(v[x], blocks_t(gm[x])), False) for x in units}
    for x in units:
        gw = mm(pt[x], ab[x]) + mm(gp[x], ub[x]) + mm_t(k[x], gkb[x]) + mm_t(v[x], gvb[x])
        out(2, x, wf[x] * (gw - after[x]))

    @pl.when(pl.program_id(0) == pl.num_programs(0) - 1)
    def _():
        for x in loads:
            x.wait()
        r = d // n
        me = me_ref[0]
        acc[:, 0:d] = t_mm(att[...], gq[...]).astype(BF16)
        for p in range(3):
            acc[:, (p + 1) * d : (p + 2) * d] = t_mm(att[...], grads[:, p * d : (p + 1) * d]).astype(BF16)
        outs = []
        for j in range(n):
            frm = pl.multiple_of((me ^ j) * r, r)
            dst = share_refs[j % 4].at[j // 4]
            outs.append(pltpu.make_async_copy(acc.at[pl.ds(frm, r), :], dst, sems.at[j]))
        for x in outs:
            x.start()
        for x in outs:
            x.wait()


def write_back(me, packed, gmix, a, u, gtot, state, att, gq, n, rows=256):
    t, wide = packed.shape
    d = wide // 4
    g = d // QUAD
    r = d // n
    last = t // rows - 1
    const = lambda *shape: pl.BlockSpec(shape, lambda i: (0,) * len(shape))
    row = lambda w: pl.BlockSpec((rows, w), lambda i: (last - i, 0))
    hbm = pl.BlockSpec(memory_space=pl.ANY)
    return pl.pallas_call(
        partial(write_back_kernel, n),
        grid=(t // rows,),
        in_specs=[pl.BlockSpec(memory_space=pltpu.SMEM), row(wide), row(d), row(d), row(d), row(d), const(g, STATE, QUAD), hbm, hbm],
        out_specs=[row(3 * d)] + [hbm] * 4,
        out_shape=[jax.ShapeDtypeStruct((t, 3 * d), BF16)] + [jax.ShapeDtypeStruct((n // 4, r, wide), BF16)] * 4,
        scratch_shapes=[
            pltpu.VMEM((g, QUAD, QUAD), F32),
            pltpu.VMEM((g, QUAD, QUAD), F32),
            pltpu.VMEM((8, d), F32),
            pltpu.VMEM((t, d), BF16),
            pltpu.VMEM((t, d), BF16),
            pltpu.VMEM((t, 3 * d), BF16),
            pltpu.VMEM((d, wide), BF16),
            pltpu.SemaphoreType.DMA((2,)),
            pltpu.SemaphoreType.DMA((n,)),
        ],
        compiler_params=pltpu.CompilerParams(vmem_limit_bytes=VMEM_LIMIT),
        cost_estimate=pl.CostEstimate(flops=11 * 10**9, bytes_accessed=18 << 20, transcendentals=t * d),
        name="write_back",
    )(me, packed, gmix, a, u, gtot, state, att, gq)


def input_grad_kernel(gain_ref, tok_ref, gq_ref, gkvc_ref, w_ref, gres_ref, out_ref):
    d = tok_ref.shape[1]
    gain = gain_ref[0:1, :]
    gin = mm_t(gq_ref[...], w_ref[:, 0:d]) + mm_t(gkvc_ref[...], w_ref[:, d:])
    normed, factor = normalize(tok_ref[...].astype(F32))
    out_ref[...] = gres_ref[...] + norm_back(gin * gain, normed, factor)


def input_grad(gain, tokens, gq, gkvc, w, gres, rows=256):
    t, d = tokens.shape
    const = lambda *shape: pl.BlockSpec(shape, lambda i: (0,) * len(shape))
    row = lambda w: pl.BlockSpec((rows, w), lambda i: (i, 0))
    return pl.pallas_call(
        input_grad_kernel,
        grid=(t // rows,),
        in_specs=[const(8, d), row(d), row(d), row(3 * d), const(d, 4 * d), row(d)],
        out_specs=row(d),
        out_shape=jax.ShapeDtypeStruct((t, d), F32),
        compiler_params=pltpu.CompilerParams(vmem_limit_bytes=VMEM_LIMIT),
        cost_estimate=pl.CostEstimate(flops=8 * t * d * d, bytes_accessed=12 << 20, transcendentals=0),
        name="input_grad",
    )(gain, tokens, gq, gkvc, w, gres)


def swap(x, mask, n):
    return lax.ppermute(x, "fsdp", [(i, i ^ mask) for i in range(n)])


def after(x, *first):
    return lax.optimization_barrier((x, *first))[0]


def add(*items):
    return sum(x.astype(F32) for x in items).astype(BF16)


def along_z(shard, n):
    return [shard] + [swap(shard, 4 * k, n) for k in range(1, n // 4)]


def along_x(own, n):
    return [swap(x, 2, n) for x in own]


def shift(x, by, seqs):
    return lax.ppermute(x, "seq", [(i, i + by) for i in range(seqs) if 0 <= i + by < seqs])


def others(state, direction, seqs):
    if seqs == 1:
        return jnp.zeros_like(state)
    if seqs > 2:
        state = state.astype(F32)
    total = shift(state, direction, seqs)
    step = 1
    while step < seqs - 1:
        total = total + shift(total, direction * step, seqs)
        step *= 2
    return total


def on_device(n, seqs, tokens, w_query, w_key, w_value, w_control, w_out, w_up, w_down,
              gain_attn, gain_ffn, bias_up, bias_down, cotangent):
    r, d = w_query.shape
    ff = w_up.shape[1]
    mult = ff // d
    me = lax.axis_index("fsdp").astype(jnp.int32).reshape(1)
    first, second = pack(w_query, w_key, w_value, w_control, w_out, w_up, w_down, gain_attn, gain_ffn, bias_up, bias_down)
    depth = n // 4
    own = along_z(first, n)
    full = lax.all_gather(second, "fsdp", axis=0, tiled=True)
    across = along_x(own, n)
    cored = [[swap(x, 1, n) for x in group] for group in (own, across)]
    att_pieces = [x for quad in zip(own, cored[0], across, cored[1]) for x in quad]
    att_where = [(j, None) for j in range(n)]
    att, packed, state, w_att, gain = project(me, tokens, att_where, att_pieces)
    mixed, read, score, inv, kts, mvs = mix(packed, others(state, 1, seqs))
    layer_out, gres, gmix, *ffn_shares = ffn(me, mixed, tokens, cotangent, full, ff, n)
    order = range(depth - 1, -1, -1)

    def start_sum(shares):
        near, near_core, far, far_core = shares
        far_core = swap(far_core, 1, n)
        near_core = swap(near_core, 1, n)
        return near, near_core, {k: add(far[k], far_core[k]) for k in order}

    def cross(far, keys, *first):
        return {k: swap(after(far[k], *first) if first else far[k], 2, n) for k in keys}

    def along(part, k):
        return swap(part, 4 * k, n) if k else part

    def seq_sum(x):
        step = 1
        while step < seqs:
            x = add(x, lax.ppermute(x, "seq", [(i, i ^ step) for i in range(seqs)]))
            step *= 2
        return x.astype(F32)

    high, low = [k for k in order if k >= depth // 2], [k for k in order if k < depth // 2]
    near, near_core, far = start_sum(ffn_shares)
    crossed = cross(far, high)
    gq, a, u, gtot, gstate = read_back(packed, after(gmix, *far.values()), read, score, inv, kts, mvs)
    crossed |= cross(far, low, gq)
    mine = {k: add(after(near[k], gq), near_core[k], crossed[k]) for k in high}
    gkvc, *shares = write_back(
        me, packed, gmix, a, u, gtot, after(others(gstate, -1, seqs), *mine.values()), att, gq, n
    )
    mine |= {k: add(after(near[k], gkvc), near_core[k], crossed[k]) for k in low}
    ffn_parts = [along(mine[k], k) for k in order]
    near, near_core, far = start_sum(shares)
    crossed = cross(far, order)
    grad_tokens = input_grad(gain, tokens, after(gq, *far.values()), gkvc, w_att, gres)
    att_parts = [along(add(after(near[k], grad_tokens), near_core[k], crossed[k]), k) for k in order]
    ffn_share = seq_sum(add(*ffn_parts))
    att_share = seq_sum(add(*att_parts))
    gain_share = jnp.sum(att_share * first[:, : 4 * d].astype(F32), axis=1) / gain_attn.astype(F32)
    up, down, out, vec = (
        ffn_share[:, :ff],
        ffn_share[:, ff : 2 * ff],
        ffn_share[:, 2 * ff : 2 * ff + d],
        ffn_share[:, 2 * ff + d :],
    )
    down = jnp.concatenate([down[:, m * d : (m + 1) * d] for m in range(mult)], axis=0)
    return (
        layer_out,
        grad_tokens,
        att_share[:, 0:d],
        att_share[:, d : 2 * d],
        att_share[:, 2 * d : 3 * d],
        att_share[:, 3 * d :],
        out,
        up,
        down,
        gain_share,
        vec[1, :r],
        vec[2, : r * mult],
        vec[3, :r],
    )


def solution(mesh):
    tokens = P(("fsdp", "seq"), None)
    matrix = P("fsdp", None)
    vector = P("fsdp")
    return jax.shard_map(
        partial(on_device, mesh.shape["fsdp"], mesh.shape["seq"]),
        mesh=mesh,
        in_specs=(tokens,) + (matrix,) * 7 + (vector,) * 4 + (tokens,),
        out_specs=(tokens, tokens) + (matrix,) * 7 + (vector,) * 4,
        check_vma=False,
    )
```

```python
from functools import partial
import jax
import jax.numpy as jnp
from jax import lax
from jax.experimental import pallas as pl
from jax.experimental.pallas import tpu as pltpu
from jax.sharding import PartitionSpec as P

F32 = jnp.float32
BF16 = jnp.bfloat16
HEAD = 64
QUAD = 256
SCALE = HEAD ** -0.5
CHUNK = 128
VMEM_LIMIT = 60 * 1024 * 1024


def mm(a, b):
    return lax.dot_general(a, b, (((1,), (0,)), ((), ())), preferred_element_type=F32)


def mm_t(a, b):
    return lax.dot_general(a, b, (((1,), (1,)), ((), ())), preferred_element_type=F32)


def t_mm(a, b):
    return lax.dot_general(a, b, (((0,), (0,)), ((), ())), preferred_element_type=F32)


def iota(shape, dim):
    return lax.broadcasted_iota(jnp.int32, shape, dim)


def normalize(x):
    centred = x - jnp.mean(x, axis=-1, keepdims=True)
    spread = jnp.mean(centred * centred, axis=-1, keepdims=True)
    factor = lax.rsqrt(spread + 1e-05)
    return centred * factor, factor


def norm_back(g, normed, factor):
    first = jnp.mean(g, axis=-1, keepdims=True)
    second = jnp.mean(g * normed, axis=-1, keepdims=True)
    return factor * (g - first - normed * second)


def blocks_of(x):
    lane = iota(x.shape, 1) // HEAD
    zero = jnp.zeros_like(x)
    return jnp.concatenate([jnp.where(lane == h, x, zero) for h in range(4)], axis=0)


def blocks_t(x):
    xt = x.T
    row = iota(xt.shape, 0) // HEAD
    zero = jnp.zeros_like(xt)
    return jnp.concatenate([jnp.where(row == h, xt, zero) for h in range(4)], axis=1)


def tri(x, lower):
    c = x.shape[0]
    row, col = iota(x.shape, 0), iota(x.shape, 1) % c
    keep = row >= col if lower else row <= col
    return jnp.where(keep, x, 0.0).astype(BF16)


def per_head(x, op, neutral):
    parts = []
    for p in range(x.shape[1] // 128):
        v = x[:, p * 128 : (p + 1) * 128]
        low = iota(v.shape, 1) < HEAD
        a = op(jnp.where(low, v, neutral), axis=-1, keepdims=True)
        b = op(jnp.where(low, neutral, v), axis=-1, keepdims=True)
        parts.append(jnp.where(low, a, b))
    return jnp.concatenate(parts, axis=1)


def head_square():
    return iota((QUAD, QUAD), 0) // HEAD == iota((QUAD, QUAD), 1) // HEAD


STATE = 2 * HEAD + 16


def store_state(st_ref, first, second, total):
    square = head_square()
    for g in range(st_ref.shape[0]):
        for k, ref in enumerate((first, second)):
            x = jnp.where(square, ref[g], 0.0)
            st_ref[g, k * HEAD : (k + 1) * HEAD, :] = (x[0:64] + x[64:128] + x[128:192] + x[192:256]).astype(BF16)
        hi, lo = hi_lo(total[0:1, g * QUAD : (g + 1) * QUAD])
        row = iota((16, QUAD), 0)
        spread = lambda x: jnp.broadcast_to(x.astype(F32), (16, QUAD))
        st_ref[g, 2 * HEAD :, :] = jnp.where(row == 0, spread(hi), jnp.where(row == 1, spread(lo), 0.0)).astype(BF16)


def load_state(st_ref, first, second, total):
    square = head_square()
    for g in range(st_ref.shape[0]):
        for k, ref in enumerate((first, second)):
            x = st_ref[g, k * HEAD : (k + 1) * HEAD, :].astype(F32)
            ref[g] = jnp.where(square, jnp.concatenate([x] * 4, axis=0), 0.0)
        both = jnp.sum(st_ref[g, 2 * HEAD :, :].astype(F32), axis=0, keepdims=True)
        total[:, g * QUAD : (g + 1) * QUAD] = jnp.broadcast_to(both, (8, QUAD))


def hi_lo(x):
    hi = x.astype(BF16)
    return hi, (x - hi.astype(F32)).astype(BF16)


def spread_vector(vecs, me, n, r, k, each, total):
    pick = (iota((n, n * r), 1) == iota((n, n * r), 0) * r + k).astype(BF16)
    rows = mm(pick, vecs).astype(BF16)
    tile = (iota((128, total), 1) % each == iota((128, total), 0)).astype(BF16)
    wide = mm(rows, tile)
    own = iota((n, total), 1) // each == (iota((n, total), 0) ^ me)
    return jnp.sum(jnp.where(own, wide, 0.0), axis=0, keepdims=True)


def gather_vector(vec, me, n, each):
    total = vec.shape[1]
    own = iota((n, total), 1) // each == (iota((n, total), 0) ^ me)
    wide = jnp.where(own, vec, 0.0).astype(BF16)
    tile = (iota((128, total), 1) % each == iota((128, total), 0)).astype(BF16)
    return mm_t(wide, tile).astype(BF16)


def share_ref(refs, j, n):
    near, low, high, high_core, rest_core = refs
    a, k, half = j % 4, j // 4, n // 8
    if a == 0:
        return near.at[k]
    if a == 1:
        return rest_core.at[k]
    if k >= half:
        return (high if a == 2 else high_core).at[k - half]
    return low.at[k] if a == 2 else rest_core.at[2 * half + k]


def share_shapes(n, r, width):
    half = n // 8
    return [jax.ShapeDtypeStruct((c, r, width), BF16) for c in (2 * half, half, half, half, 3 * half)]


def piece_refs(where, refs):
    return [refs[a] if row is None else refs[a].at[row] for a, row in where]


def pack_kernel(q, k, v, c, o, up, down, gain_a, gain_f, b_up, b_down, first, second):
    r, d = q.shape
    ff = up.shape[1]
    for p, ref in enumerate((q, k, v, c)):
        first[:, p * d : (p + 1) * d] = ref[...]
    tile = jnp.zeros((r, 128), F32)
    row, col = iota((r, 128), 0), iota((r, 128), 1)
    for i, ref in enumerate((gain_a, gain_f, b_up, b_down)):
        length = ref.shape[1]
        wide = jnp.broadcast_to(ref[...].astype(F32), (r, length))
        if length < 128:
            wide = jnp.concatenate([wide, jnp.zeros((r, 128 - length), F32)], axis=1)
        tile = jnp.where(row == i, wide, tile)
    first[:, 4 * d :] = tile.astype(BF16)
    second[:, 2 * ff + d :] = tile.astype(BF16)
    second[:, :ff] = up[...]
    for m in range(ff // d):
        second[:, ff + m * d : ff + (m + 1) * d] = down[m * r : (m + 1) * r, :]
    second[:, 2 * ff : 2 * ff + d] = o[...]


def pack(q, k, v, c, o, up, down, gain_a, gain_f, b_up, b_down):
    r, d = q.shape
    ff = up.shape[1]
    return pl.pallas_call(
        pack_kernel,
        out_shape=[jax.ShapeDtypeStruct((r, 4 * d + 128), BF16), jax.ShapeDtypeStruct((r, 2 * ff + d + 128), BF16)],
        cost_estimate=pl.CostEstimate(flops=0, bytes_accessed=1 << 20, transcendentals=0),
        name="pack",
    )(q, k, v, c, o, up, down, *(x.reshape(1, -1) for x in (gain_a, gain_f, b_up, b_down)))


def stack_kernel(*refs):
    for i, ref in enumerate(refs[:-1]):
        refs[-1][i] = ref[...]


def stack(items):
    return pl.pallas_call(
        stack_kernel,
        out_shape=jax.ShapeDtypeStruct((len(items),) + items[0].shape, items[0].dtype),
        cost_estimate=pl.CostEstimate(flops=0, bytes_accessed=2 << 20, transcendentals=0),
        name="stack",
    )(*items)


def project_kernel(where, arrays, r, me_ref, tok_hbm, *refs):
    n = len(where)
    pieces = piece_refs(where, refs)
    (att_hbm, pack_hbm, st_ref, w_hbm, gain_ref,
     tok, att, pack, w_all, vecs, normed, written, first, second, total, sems, vsems, tsem, osems) = refs[arrays:]
    t, d = att.shape
    wide = 4 * d
    rows = 256
    me = me_ref[0]
    load = pltpu.make_async_copy(tok_hbm, tok, tsem)
    load.start()
    vector_copies, copies = [], []
    for j in range(n):
        at = pl.multiple_of((me ^ j) * r, r)
        copies.append(pltpu.make_async_copy(pieces[j].at[:, pl.ds(0, wide)], w_all.at[pl.ds(at, r), :], sems.at[j]))
        vector_copies.append(pltpu.make_async_copy(pieces[j].at[:, pl.ds(wide, 128)], vecs.at[pl.ds(j * r, r), :], vsems.at[j]))
    for c in vector_copies + copies:
        c.start()
    sent = []

    def send(src, dst):
        copy = pltpu.make_async_copy(src, dst, osems.at[len(sent)])
        copy.start()
        sent.append(copy)

    load.wait()
    for i in range(t // rows):
        rs = pl.ds(i * rows, rows)
        normed[rs, :], _ = normalize(tok[rs, :].astype(F32))
    for c in vector_copies:
        c.wait()
    gain = spread_vector(vecs[...], me, n, r, 0, r, d)
    gain_ref[...] = jnp.broadcast_to(gain, gain_ref.shape)
    for c in copies:
        c.wait()
    send(w_all, w_hbm)
    sums = jnp.zeros((1, d), F32)
    for i in range(t // rows):
        rs = pl.ds(i * rows, rows)
        x = (normed[rs, :] * gain).astype(BF16)
        att[rs, :] = x
        send(att.at[rs, :], att_hbm.at[rs, :])
        for p in (3, 1, 2, 0):
            full = mm(x, w_all[:, p * d : (p + 1) * d]).astype(BF16)
            pack[rs, p * d : (p + 1) * d] = full
            if p == 3:
                new = jnp.exp(full.astype(F32)).astype(BF16)
                written[rs, :] = new
                sums += jnp.sum(new.astype(F32), axis=0, keepdims=True)
        send(pack.at[rs, :], pack_hbm.at[rs, :])
    for g in range(d // QUAD):
        s = slice(g * QUAD, (g + 1) * QUAD)
        first[g] = t_mm(pack[:, d + g * QUAD : d + (g + 1) * QUAD], written[:, s])
        second[g] = t_mm(written[:, s], pack[:, 2 * d + g * QUAD : 2 * d + (g + 1) * QUAD])
    total[...] = jnp.broadcast_to(sums, total.shape)
    store_state(st_ref, first, second, total)
    for c in sent:
        c.wait()


def project(me, tokens, where, pieces):
    t, d = tokens.shape
    n = len(where)
    r = d // n
    wide = 4 * d
    g = d // QUAD
    hbm = pl.BlockSpec(memory_space=pl.ANY)
    vmem = pl.BlockSpec(memory_space=pltpu.VMEM)
    return pl.pallas_call(
        partial(project_kernel, where, len(pieces), r),
        in_specs=[pl.BlockSpec(memory_space=pltpu.SMEM)] + [hbm] * (1 + len(pieces)),
        out_specs=[hbm, hbm, vmem, hbm, vmem],
        out_shape=[
            jax.ShapeDtypeStruct((t, d), BF16),
            jax.ShapeDtypeStruct((t, wide), BF16),
            jax.ShapeDtypeStruct((g, STATE, QUAD), BF16),
            jax.ShapeDtypeStruct((d, wide), BF16),
            jax.ShapeDtypeStruct((8, d), F32),
        ],
        scratch_shapes=[
            pltpu.VMEM((t, d), BF16),
            pltpu.VMEM((t, d), BF16),
            pltpu.VMEM((t, wide), BF16),
            pltpu.VMEM((d, wide), BF16),
            pltpu.VMEM((n * r, 128), BF16),
            pltpu.VMEM((t, d), F32),
            pltpu.VMEM((t, d), BF16),
            pltpu.VMEM((g, QUAD, QUAD), F32),
            pltpu.VMEM((g, QUAD, QUAD), F32),
            pltpu.VMEM((8, d), F32),
            pltpu.SemaphoreType.DMA((n,)),
            pltpu.SemaphoreType.DMA((n,)),
            pltpu.SemaphoreType.DMA,
            pltpu.SemaphoreType.DMA((1 + 2 * (t // 256),)),
        ],
        compiler_params=pltpu.CompilerParams(vmem_limit_bytes=VMEM_LIMIT),
        cost_estimate=pl.CostEstimate(flops=2 * t * d * wide, bytes_accessed=12 << 20, transcendentals=t * d),
        name="project",
    )(me, tokens, *pieces)


def mix_kernel(pack_ref, st_in, mix_ref, read_ref, score_ref, inv_ref, kts_ref, mvs_ref, kt, mv, tot):
    d = mix_ref.shape[1]
    rows = mix_ref.shape[0]

    @pl.when(pl.program_id(0) == 0)
    def _():
        load_state(st_in, kt, mv, tot)

    c = CHUNK
    square = head_square()
    ones = (iota((c, c), 0) >= iota((c, c), 1)).astype(BF16)
    units = [(b, g) for b in range(rows // c) for g in range(d // QUAD)]
    at = {(b, g): (slice(b * c, (b + 1) * c), slice(g * QUAD, (g + 1) * QUAD)) for b, g in units}
    part = lambda p: {(b, g): pack_ref[at[b, g][0], p * d + g * QUAD : p * d + (g + 1) * QUAD] for b, g in units}
    q, k, v = part(0), part(1), part(2)
    written = {x: jnp.exp(y.astype(F32)).astype(BF16) for x, y in part(3).items()}
    wb = {x: blocks_of(written[x]) for x in units}
    pairs = {x: tri(mm(q[x], blocks_t(k[x])), True) for x in units}
    ktb, mvb, inv = {}, {}, {}
    for x in units:
        b, g = x
        ktb[x], mvb[x] = kt[g].astype(BF16), mv[g].astype(BF16)
        kts_ref[b, g] = ktb[x]
        mvs_ref[b, g] = mvb[x]
        kt[g] += jnp.where(square, t_mm(k[x], written[x]), 0.0)
        mv[g] += jnp.where(square, t_mm(written[x], v[x]), 0.0)
        total = mm(ones, written[x]) + tot[0:1, at[x][1]]
        tot[0:1, at[x][1]] = total[c - 1 : c, :]
        inv[x] = 1.0 / total
        inv_ref[at[x]] = inv[x]
    score = {x: (mm(pairs[x], wb[x]) + mm(q[x], ktb[x])) * SCALE * inv[x] for x in units}
    for x in units:
        score_ref[at[x]] = score[x]
    e = {x: jnp.exp(score[x] - per_head(score[x], jnp.max, -jnp.inf)) for x in units}
    read = {x: e[x] / per_head(e[x], jnp.sum, 0.0) for x in units}
    for x in units:
        read_ref[at[x]] = read[x]
    scaled = {x: (read[x] * inv[x]).astype(BF16) for x in units}
    recall = {x: tri(mm(scaled[x], blocks_t(written[x])), True) for x in units}
    for x in units:
        mix_ref[at[x]] = (mm(recall[x], blocks_of(v[x])) + mm(scaled[x], mvb[x])).astype(BF16)


def mix(packed, state, rows=256):
    t, wide = packed.shape
    d = wide // 4
    g = d // QUAD
    const = lambda *shape: pl.BlockSpec(shape, lambda i: (0,) * len(shape))
    per = rows // CHUNK
    row = lambda w: pl.BlockSpec((rows, w), lambda i: (i, 0))
    return pl.pallas_call(
        mix_kernel,
        grid=(t // rows,),
        in_specs=[row(wide), const(g, STATE, QUAD)],
        out_specs=[row(d)] * 4 + [pl.BlockSpec((per, g, QUAD, QUAD), lambda i: (i, 0, 0, 0))] * 2,
        out_shape=[jax.ShapeDtypeStruct((t, d), BF16)] + [jax.ShapeDtypeStruct((t, d), F32)] * 3
        + [jax.ShapeDtypeStruct((t // CHUNK, g, QUAD, QUAD), BF16)] * 2,
        scratch_shapes=[pltpu.VMEM((g, QUAD, QUAD), F32), pltpu.VMEM((g, QUAD, QUAD), F32), pltpu.VMEM((8, d), F32)],
        compiler_params=pltpu.CompilerParams(vmem_limit_bytes=VMEM_LIMIT),
        cost_estimate=pl.CostEstimate(flops=6 * 10**9, bytes_accessed=16 << 20, transcendentals=2 * t * d),
        name="mix",
    )(packed, state)


def ffn_kernel(n, me_ref, mixed_hbm, tok_hbm, cot_hbm, full_ref, kept_hbm, gres_hbm, gmix_hbm, hid_hbm, down_hbm, *refs):
    share_refs = refs[:5]
    (mixed, tok, cot, kept, gres, gmix, w_out, w_up, w_down, vecs, hid, gpre, fin, gbr, normed_f, sems, osems, dsem) = refs[5:]
    me = me_ref[0]
    t, d = mixed.shape
    ff = w_up.shape[1]
    r = d // n
    mult = ff // d
    rows = 512
    part = 512
    steps = t // rows
    parts = ff // part

    def load(src, dst, i):
        copy = pltpu.make_async_copy(src, dst, sems.at[i])
        copy.start()
        return copy

    down_sem = 3
    early = [
        load(full_ref.at[:, pl.ds(2 * ff, d)], w_out, 0),
        load(mixed_hbm, mixed, 1),
        load(tok_hbm, tok, 2),
        load(full_ref.at[:, pl.ds(2 * ff + d, 128)], vecs, 4),
    ]
    late = [load(full_ref.at[:, pl.ds(0, ff)], w_up, 5), load(cot_hbm, cot, 6)]
    down = []
    for j in range(n):
        for m in range(mult):
            down.append((full_ref.at[pl.ds(j * r, r), pl.ds(ff + m * d, d)], w_down.at[pl.ds((j * mult + m) * r, r), :]))
    late += [load(src, dst, 7 + i) for i, (src, dst) in enumerate(down)]
    for c in early:
        c.wait()
    gain = spread_vector(vecs[...], 0, n, r, 1, r, d)
    b_up = spread_vector(vecs[...], 0, n, r, 2, r * mult, ff)
    b_down = spread_vector(vecs[...], 0, n, r, 3, r, d)

    sent = []

    def send(src, dst):
        copy = pltpu.make_async_copy(src, dst, osems.at[len(sent)])
        copy.start()
        sent.append(copy)

    ggain = jnp.zeros((1, d), F32)
    gbdown = jnp.zeros((1, d), F32)
    gbup = [jnp.zeros((1, part), F32)] * parts
    factors = []
    for i in range(steps):
        rs = pl.ds(i * rows, rows)
        resid = tok[rs, :].astype(F32) + mm(mixed[rs, :], w_out[...])
        kept[rs, :] = resid + b_down
        send(kept.at[rs, :], kept_hbm.at[rs, :])
        x, factor = normalize(resid)
        normed_f[rs, :] = x
        factors.append(factor)
        fin[rs, :] = (x * gain).astype(BF16)
    for c in late:
        c.wait()
    keep_down = pltpu.make_async_copy(w_down, down_hbm, dsem)
    keep_down.start()
    for i in range(steps):
        rs = pl.ds(i * rows, rows)
        ffn_in, normed, factor = fin[rs, :], normed_f[rs, :], factors[i]
        cot_b = cot[rs, :]
        cotf = cot_b.astype(F32)

        def entry(p):
            ps = slice(p * part, (p + 1) * part)
            return mm(ffn_in, w_up[:, ps]) + b_up[:, ps], mm_t(cot_b, w_down[ps, :])

        ready = entry(0)
        gin = None
        for p in range(parts):
            ps = slice(p * part, (p + 1) * part)
            pre, gh = ready
            if p + 1 < parts:
                ready = entry(p + 1)
            sig = 0.5 * jnp.tanh(0.5 * pre) + 0.5
            act = pre * sig
            gp = gh * (sig + act * (1.0 - sig))
            gbup[p] = gbup[p] + jnp.sum(gp, axis=0, keepdims=True)
            act, gp = act.astype(BF16), gp.astype(BF16)
            hid[rs, ps] = act
            gpre[rs, ps] = gp
            x = mm_t(gp, w_up[:, ps])
            gin = x if p == 0 else gin + x
        send(hid.at[rs, :], hid_hbm.at[rs, :])
        back = cotf + norm_back(gin * gain, normed, factor)
        gres[rs, :] = back
        send(gres.at[rs, :], gres_hbm.at[rs, :])
        back = back.astype(BF16)
        gbr[rs, :] = back
        gmix[rs, :] = mm_t(back, w_out[...]).astype(BF16)
        send(gmix.at[rs, :], gmix_hbm.at[rs, :])
        ggain += jnp.sum(gin * normed, axis=0, keepdims=True)
        gbdown += jnp.sum(cotf, axis=0, keepdims=True)

    def share(j, rows_of, ref, at, width):
        send(ref.at[rows_of(me ^ j), :], share_ref(share_refs, j, n).at[:, pl.ds(at, width)])

    own_rows = lambda f: pl.ds(pl.multiple_of(f * r, r), r)
    keep_down.wait()
    for p in range(parts):
        ps = slice(p * part, (p + 1) * part)
        w_down[ps, :] = t_mm(hid[:, ps], cot[...]).astype(BF16)
    for j in range(n):
        for m in range(mult):
            share(j, lambda f: pl.ds(pl.multiple_of((f * mult + m) * r, r), r), w_down, ff + m * d, d)
    w_out[...] = t_mm(mixed[...], gbr[...]).astype(BF16)
    va = gather_vector(ggain, 0, n, r)
    vb = gather_vector(jnp.concatenate(gbup, axis=1), 0, n, r * mult)
    vc = gather_vector(gbdown, 0, n, r)
    row = iota((r, 128), 0)
    pick = lambda v, j, i, rest: jnp.where(row == i, jnp.broadcast_to(v[j : j + 1].astype(F32), (r, 128)), rest)
    for j in range(n):
        tile = pick(va, j, 1, pick(vb, j, 2, pick(vc, j, 3, jnp.zeros((r, 128), F32))))
        vecs[j * r : (j + 1) * r, :] = tile.astype(BF16)
    for j in range(n):
        share(j, own_rows, w_out, 2 * ff, d)
        share(j, own_rows, vecs, 2 * ff + d, 128)
    for p in range(parts):
        ps = slice(p * part, (p + 1) * part)
        w_up[:, ps] = t_mm(fin[...], gpre[:, ps]).astype(BF16)
    for j in range(n):
        share(j, own_rows, w_up, 0, ff)
    for c in sent:
        c.wait()


def ffn(me, mixed, tokens, cot, full, ff, n):
    t, d = tokens.shape
    hbm = pl.BlockSpec(memory_space=pl.ANY)
    moves = n * (ff // d)
    return pl.pallas_call(
        partial(ffn_kernel, n),
        in_specs=[pl.BlockSpec(memory_space=pltpu.SMEM)] + [hbm] * 4,
        out_specs=[hbm] * 10,
        out_shape=[
            jax.ShapeDtypeStruct((t, d), F32),
            jax.ShapeDtypeStruct((t, d), F32),
            jax.ShapeDtypeStruct((t, d), BF16),
            jax.ShapeDtypeStruct((t, ff), BF16),
            jax.ShapeDtypeStruct((ff, d), BF16),
        ]
        + share_shapes(n, d // n, full.shape[1]),
        scratch_shapes=[pltpu.VMEM((t, d), BF16)] * 3
        + [pltpu.VMEM((t, d), F32), pltpu.VMEM((t, d), F32), pltpu.VMEM((t, d), BF16)]
        + [
            pltpu.VMEM((d, d), BF16),
            pltpu.VMEM((d, ff), BF16),
            pltpu.VMEM((ff, d), BF16),
            pltpu.VMEM((d, 128), BF16),
            pltpu.VMEM((t, ff), BF16),
            pltpu.VMEM((t, ff), BF16),
            pltpu.VMEM((t, d), BF16),
            pltpu.VMEM((t, d), BF16),
            pltpu.VMEM((t, d), F32),
            pltpu.SemaphoreType.DMA((7 + moves,)),
            pltpu.SemaphoreType.DMA((4 * (t // 256) + 3 * n + moves,)),
            pltpu.SemaphoreType.DMA,
        ],
        compiler_params=pltpu.CompilerParams(vmem_limit_bytes=VMEM_LIMIT),
        cost_estimate=pl.CostEstimate(flops=11 * t * d * ff, bytes_accessed=20 << 20, transcendentals=t * ff),
        name="ffn",
    )(me, mixed, tokens, cot, full)


def ffn_out_kernel(hid_ref, kept_ref, down_ref, out_ref):
    out_ref[...] = (kept_ref[...] + mm(hid_ref[...], down_ref[...])).astype(BF16)


def ffn_out(hid, kept, down, rows=256):
    t, ff = hid.shape
    d = kept.shape[1]
    row = lambda w: pl.BlockSpec((rows, w), lambda i: (i, 0))
    return pl.pallas_call(
        ffn_out_kernel,
        grid=(t // rows,),
        in_specs=[row(ff), row(d), pl.BlockSpec((ff, d), lambda i: (0, 0))],
        out_specs=row(d),
        out_shape=jax.ShapeDtypeStruct((t, d), BF16),
        compiler_params=pltpu.CompilerParams(vmem_limit_bytes=VMEM_LIMIT),
        cost_estimate=pl.CostEstimate(flops=2 * t * d * ff, bytes_accessed=9 << 20, transcendentals=0),
        name="ffn_out",
    )(hid, kept, down)


def read_back_kernel(pack_ref, gmix_ref, read_ref, score_ref, inv_ref, kts_ref, mvs_ref,
                     gq_ref, a_ref, u_ref, gtot_ref, st_ref, gk_ref, gv_ref, gt_ref):
    rows, d = gmix_ref.shape

    @pl.when(pl.program_id(0) == 0)
    def _():
        gk_ref[...] = jnp.zeros_like(gk_ref)
        gv_ref[...] = jnp.zeros_like(gv_ref)
        gt_ref[...] = jnp.zeros_like(gt_ref)

    c = CHUNK
    units = [(b, g) for b in range(rows // c) for g in range(d // QUAD)]
    at = {(b, g): (slice(b * c, (b + 1) * c), slice(g * QUAD, (g + 1) * QUAD)) for b, g in units}
    part = lambda p: {(b, g): pack_ref[at[b, g][0], p * d + g * QUAD : p * d + (g + 1) * QUAD] for b, g in units}
    q, k, v = part(0), part(1), part(2)
    written = {x: jnp.exp(y.astype(F32)).astype(BF16) for x, y in part(3).items()}
    wb = {x: blocks_of(written[x]) for x in units}
    gm = {x: gmix_ref[at[x]] for x in units}
    gpair = {x: tri(mm(gm[x], blocks_t(v[x])), True) for x in units}
    weighted = {x: (mm(gpair[x], wb[x]) + mm_t(gm[x], mvs_ref[x])) * inv_ref[at[x]] * read_ref[at[x]] for x in units}
    gscore = {x: weighted[x] - read_ref[at[x]] * per_head(weighted[x], jnp.sum, 0.0) for x in units}
    a, u = {}, {}
    for x in units:
        inv = inv_ref[at[x]]
        a[x] = (gscore[x] * inv * SCALE).astype(BF16)
        u[x] = (read_ref[at[x]] * inv).astype(BF16)
        a_ref[at[x]] = a[x]
        u_ref[at[x]] = u[x]
        gtot = (gscore[x] * score_ref[at[x]] + weighted[x]) * inv
        gtot_ref[at[x]] = gtot
        gt_ref[0:1, at[x][1]] += jnp.sum(gtot, axis=0, keepdims=True)
    spair = {x: tri(mm(a[x], blocks_t(written[x])), True) for x in units}
    for x in units:
        gq_ref[at[x]] = (mm(spair[x], blocks_of(k[x])) + mm_t(a[x], kts_ref[x])).astype(BF16)
    for g in range(d // QUAD):
        s = slice(g * QUAD, (g + 1) * QUAD)
        every = lambda y: jnp.concatenate([y[b, g] for b in range(rows // c)], axis=0)
        gk_ref[g] += t_mm(every(a), every(q))
        gv_ref[g] += t_mm(every(u), every(gm))

    @pl.when(pl.program_id(0) == pl.num_programs(0) - 1)
    def _():
        store_state(st_ref, gk_ref, gv_ref, gt_ref)


def read_back(packed, gmix, read, score, inv, kts, mvs, rows=512):
    t, wide = packed.shape
    d = wide // 4
    g = d // QUAD
    const = lambda *shape: pl.BlockSpec(shape, lambda i: (0,) * len(shape))
    per = rows // CHUNK
    row = lambda w: pl.BlockSpec((rows, w), lambda i: (i, 0))
    st = pl.BlockSpec((per, g, QUAD, QUAD), lambda i: (i, 0, 0, 0))
    return pl.pallas_call(
        read_back_kernel,
        grid=(t // rows,),
        in_specs=[row(wide), row(d), row(d), row(d), row(d), st, st],
        out_specs=[row(d)] * 4 + [const(g, STATE, QUAD)],
        out_shape=[jax.ShapeDtypeStruct((t, d), BF16)] * 3 + [jax.ShapeDtypeStruct((t, d), F32)]
        + [jax.ShapeDtypeStruct((g, STATE, QUAD), BF16)],
        scratch_shapes=[pltpu.VMEM((g, QUAD, QUAD), F32), pltpu.VMEM((g, QUAD, QUAD), F32), pltpu.VMEM((8, d), F32)],
        compiler_params=pltpu.CompilerParams(vmem_limit_bytes=VMEM_LIMIT),
        cost_estimate=pl.CostEstimate(flops=6 * 10**9, bytes_accessed=20 << 20, transcendentals=t * d),
        name="read_back",
    )(packed, gmix, read, score, inv, kts, mvs)


def write_back_kernel(n, me_ref, pack_ref, gmix_ref, a_ref, u_ref, gtot_ref, st_in, att_hbm, gq_hbm, out_ref, *refs):
    share_refs = refs[:5]
    gk, gv, gt, att, gq, grads, acc, isems, sems = refs[5:]
    rows, d = gmix_ref.shape
    loads = [pltpu.make_async_copy(att_hbm, att, isems.at[0]), pltpu.make_async_copy(gq_hbm, gq, isems.at[1])]

    @pl.when(pl.program_id(0) == 0)
    def _():
        for x in loads:
            x.start()
        load_state(st_in, gk, gv, gt)

    base = (pl.num_programs(0) - 1 - pl.program_id(0)) * rows
    c = CHUNK
    square = head_square()
    ones = (iota((c, c), 0) <= iota((c, c), 1)).astype(BF16)
    units = [(b, g) for b in reversed(range(rows // c)) for g in range(d // QUAD)]
    at = {(b, g): (slice(b * c, (b + 1) * c), slice(g * QUAD, (g + 1) * QUAD)) for b, g in units}
    part = lambda p: {(b, g): pack_ref[at[b, g][0], p * d + g * QUAD : p * d + (g + 1) * QUAD] for b, g in units}
    q, k, v = part(0), part(1), part(2)
    wf = {x: jnp.exp(y.astype(F32)) for x, y in part(3).items()}
    written = {x: wf[x].astype(BF16) for x in units}
    gm, a, u = ({x: ref[at[x]] for x in units} for ref in (gmix_ref, a_ref, u_ref))
    qb, gb, ab, ub = ({x: blocks_of(y[x]) for x in units} for y in (q, gm, a, u))
    gkb, gvb, after = {}, {}, {}
    for x in units:
        g = x[1]
        gkb[x], gvb[x] = gk[g].astype(BF16), gv[g].astype(BF16)
        gk[g] += jnp.where(square, t_mm(a[x], q[x]), 0.0)
        gv[g] += jnp.where(square, t_mm(u[x], gm[x]), 0.0)
        hi, lo = hi_lo(gtot_ref[at[x]])
        after[x] = mm(ones, hi) + mm(ones, lo) + gt[0:1, at[x][1]]
        gt[0:1, at[x][1]] = after[x][0:1, :]

    def out(p, x, y):
        y = y.astype(BF16)
        cols = slice(p * d + x[1] * QUAD, p * d + (x[1] + 1) * QUAD)
        out_ref[at[x][0], cols] = y
        grads[pl.ds(pl.multiple_of(base + x[0] * c, c), c), cols] = y

    st = {x: tri(mm(written[x], blocks_t(a[x])), False) for x in units}
    rt = {x: tri(mm(written[x], blocks_t(u[x])), False) for x in units}
    for x in units:
        out(0, x, mm(st[x], qb[x]) + mm(written[x], gkb[x]))
    for x in units:
        out(1, x, mm(rt[x], gb[x]) + mm(written[x], gvb[x]))
    pt = {x: tri(mm(k[x], blocks_t(q[x])), False) for x in units}
    gp = {x: tri(mm(v[x], blocks_t(gm[x])), False) for x in units}
    for x in units:
        gw = mm(pt[x], ab[x]) + mm(gp[x], ub[x]) + mm_t(k[x], gkb[x]) + mm_t(v[x], gvb[x])
        out(2, x, wf[x] * (gw - after[x]))

    @pl.when(pl.program_id(0) == pl.num_programs(0) - 1)
    def _():
        for x in loads:
            x.wait()
        r = d // n
        me = me_ref[0]
        acc[:, 0:d] = t_mm(att[...], gq[...]).astype(BF16)
        for p in range(3):
            acc[:, (p + 1) * d : (p + 2) * d] = t_mm(att[...], grads[:, p * d : (p + 1) * d]).astype(BF16)
        outs = []
        for j in range(n):
            frm = pl.multiple_of((me ^ j) * r, r)
            dst = share_ref(share_refs, j, n)
            outs.append(pltpu.make_async_copy(acc.at[pl.ds(frm, r), :], dst, sems.at[j]))
        for x in outs:
            x.start()
        for x in outs:
            x.wait()


def write_back(me, packed, gmix, a, u, gtot, state, att, gq, n, rows=256):
    t, wide = packed.shape
    d = wide // 4
    g = d // QUAD
    r = d // n
    last = t // rows - 1
    const = lambda *shape: pl.BlockSpec(shape, lambda i: (0,) * len(shape))
    row = lambda w: pl.BlockSpec((rows, w), lambda i: (last - i, 0))
    hbm = pl.BlockSpec(memory_space=pl.ANY)
    return pl.pallas_call(
        partial(write_back_kernel, n),
        grid=(t // rows,),
        in_specs=[pl.BlockSpec(memory_space=pltpu.SMEM), row(wide), row(d), row(d), row(d), row(d), const(g, STATE, QUAD), hbm, hbm],
        out_specs=[row(3 * d)] + [hbm] * 5,
        out_shape=[jax.ShapeDtypeStruct((t, 3 * d), BF16)] + share_shapes(n, r, wide),
        scratch_shapes=[
            pltpu.VMEM((g, QUAD, QUAD), F32),
            pltpu.VMEM((g, QUAD, QUAD), F32),
            pltpu.VMEM((8, d), F32),
            pltpu.VMEM((t, d), BF16),
            pltpu.VMEM((t, d), BF16),
            pltpu.VMEM((t, 3 * d), BF16),
            pltpu.VMEM((d, wide), BF16),
            pltpu.SemaphoreType.DMA((2,)),
            pltpu.SemaphoreType.DMA((n,)),
        ],
        compiler_params=pltpu.CompilerParams(vmem_limit_bytes=VMEM_LIMIT),
        cost_estimate=pl.CostEstimate(flops=11 * 10**9, bytes_accessed=18 << 20, transcendentals=t * d),
        name="write_back",
    )(me, packed, gmix, a, u, gtot, state, att, gq)


def input_grad_kernel(gain_ref, tok_ref, gq_ref, gkvc_ref, w_ref, gres_ref, out_ref):
    d = tok_ref.shape[1]
    gain = gain_ref[0:1, :]
    gin = mm_t(gq_ref[...], w_ref[:, 0:d]) + mm_t(gkvc_ref[...], w_ref[:, d:])
    normed, factor = normalize(tok_ref[...].astype(F32))
    out_ref[...] = gres_ref[...] + norm_back(gin * gain, normed, factor)


def input_grad(gain, tokens, gq, gkvc, w, gres, rows=256):
    t, d = tokens.shape
    const = lambda *shape: pl.BlockSpec(shape, lambda i: (0,) * len(shape))
    row = lambda w: pl.BlockSpec((rows, w), lambda i: (i, 0))
    return pl.pallas_call(
        input_grad_kernel,
        grid=(t // rows,),
        in_specs=[const(8, d), row(d), row(d), row(3 * d), const(d, 4 * d), row(d)],
        out_specs=row(d),
        out_shape=jax.ShapeDtypeStruct((t, d), F32),
        compiler_params=pltpu.CompilerParams(vmem_limit_bytes=VMEM_LIMIT),
        cost_estimate=pl.CostEstimate(flops=8 * t * d * d, bytes_accessed=12 << 20, transcendentals=0),
        name="input_grad",
    )(gain, tokens, gq, gkvc, w, gres)


def swap(x, mask, n):
    return lax.ppermute(x, "fsdp", [(i, i ^ mask) for i in range(n)])


def after(x, *first):
    return lax.optimization_barrier((x, *first))[0]


def add(*items):
    return sum(x.astype(F32) for x in items).astype(BF16)


def along_z(shard, n):
    return [shard] + [swap(shard, 4 * k, n) for k in range(1, n // 4)]


def along_x(own, n):
    return [swap(x, 2, n) for x in own]


def shift(x, by, seqs):
    return lax.ppermute(x, "seq", [(i, i + by) for i in range(seqs) if 0 <= i + by < seqs])


def others(state, direction, seqs):
    if seqs == 1:
        return jnp.zeros_like(state)
    if seqs > 2:
        state = state.astype(F32)
    total = shift(state, direction, seqs)
    step = 1
    while step < seqs - 1:
        total = total + shift(total, direction * step, seqs)
        step *= 2
    return total


def on_device(n, seqs, tokens, w_query, w_key, w_value, w_control, w_out, w_up, w_down,
              gain_attn, gain_ffn, bias_up, bias_down, cotangent):
    r, d = w_query.shape
    ff = w_up.shape[1]
    mult = ff // d
    me = lax.axis_index("fsdp").astype(jnp.int32).reshape(1)
    first, second = pack(w_query, w_key, w_value, w_control, w_out, w_up, w_down, gain_attn, gain_ffn, bias_up, bias_down)
    depth = n // 4
    own = along_z(first, n)
    full = lax.all_gather(second, "fsdp", axis=0, tiled=True)
    across = along_x(own, n)
    cored = [[swap(x, 1, n) for x in group] for group in (own, across)]
    att_pieces = [x for quad in zip(own, cored[0], across, cored[1]) for x in quad]
    att_where = [(j, None) for j in range(n)]
    att, packed, state, w_att, gain = project(me, tokens, att_where, att_pieces)
    mixed, read, score, inv, kts, mvs = mix(packed, others(state, 1, seqs))
    kept, gres, gmix, hid, full_down, *ffn_shares = ffn(me, mixed, tokens, cotangent, full, ff, n)
    half = depth // 2

    def start_sum(shares, *first):
        near, low, high, high_core, rest = shares
        high = add(after(high, *first) if first else high, swap(high_core, 1, n))
        rest = swap(rest, 1, n)
        return (near, rest), add(low, rest[depth:]), high

    def joined(near, crossed, base, *first):
        own, core = near
        own = after(own, *first)
        return {base + i: add(own[base + i], core[base + i], crossed[i]) for i in range(half)}

    def along(part, k):
        return swap(part, 4 * k, n) if k else part

    def seq_sum(x):
        step = 1
        while step < seqs:
            x = add(x, lax.ppermute(x, "seq", [(i, i ^ step) for i in range(seqs)]))
            step *= 2
        return x.astype(F32)

    near, low, high = start_sum(ffn_shares)
    crossed_high = swap(high, 2, n)
    gq, a, u, gtot, gstate = read_back(packed, after(gmix, high), read, score, inv, kts, mvs)
    crossed_low = swap(after(low, gq), 2, n)
    mine = joined(near, crossed_high, half, gq)
    ffn_parts = [along(mine[k], k) for k in range(half, depth)]
    gkvc, *shares = write_back(
        me, packed, gmix, a, u, gtot, after(others(gstate, -1, seqs), *mine.values()), att, gq, n
    )
    mine = joined(near, crossed_low, 0, gkvc)
    att_near, att_low, att_high = start_sum(shares, *ffn_parts, *mine.values())
    ffn_parts += [along(mine[k], k) for k in range(half)]
    crossed_high, crossed_low = swap(att_high, 2, n), swap(att_low, 2, n)
    grad_tokens = input_grad(gain, tokens, after(gq, att_low, *mine.values()), gkvc, w_att, gres)
    ffn_sum = add(after(mine[0], grad_tokens), *(p for p in ffn_parts if p is not mine[0]))
    mine = joined(att_near, crossed_high, half, grad_tokens, ffn_sum) | joined(att_near, crossed_low, 0, grad_tokens)
    att_parts = [along(mine[k], k) for k in range(depth)]
    layer_out = ffn_out(after(hid, *mine.values()), kept, full_down)
    ffn_share = seq_sum(ffn_sum)
    att_share = seq_sum(add(*[after(p, layer_out) for p in att_parts]))
    gain_share = jnp.sum(att_share * first[:, : 4 * d].astype(F32), axis=1) / gain_attn.astype(F32)
    up, down, out, vec = (
        ffn_share[:, :ff],
        ffn_share[:, ff : 2 * ff],
        ffn_share[:, 2 * ff : 2 * ff + d],
        ffn_share[:, 2 * ff + d :],
    )
    down = jnp.concatenate([down[:, m * d : (m + 1) * d] for m in range(mult)], axis=0)
    return (
        layer_out,
        grad_tokens,
        att_share[:, 0:d],
        att_share[:, d : 2 * d],
        att_share[:, 2 * d : 3 * d],
        att_share[:, 3 * d :],
        out,
        up,
        down,
        gain_share,
        vec[1, :r],
        vec[2, : r * mult],
        vec[3, :r],
    )


def solution(mesh):
    tokens = P(("fsdp", "seq"), None)
    matrix = P("fsdp", None)
    vector = P("fsdp")
    return jax.shard_map(
        partial(on_device, mesh.shape["fsdp"], mesh.shape["seq"]),
        mesh=mesh,
        in_specs=(tokens,) + (matrix,) * 7 + (vector,) * 4 + (tokens,),
        out_specs=(tokens, tokens) + (matrix,) * 7 + (vector,) * 4,
        check_vma=False,
    )
```

```python
from functools import partial
import jax
import jax.numpy as jnp
from jax import lax
from jax.experimental import pallas as pl
from jax.experimental.pallas import tpu as pltpu
from jax.sharding import PartitionSpec as P

F32 = jnp.float32
BF16 = jnp.bfloat16
HEAD = 64
QUAD = 256
SCALE = HEAD ** -0.5
CHUNK = 128
VMEM_LIMIT = 60 * 1024 * 1024


def mm(a, b):
    return lax.dot_general(a, b, (((1,), (0,)), ((), ())), preferred_element_type=F32)


def mm_t(a, b):
    return lax.dot_general(a, b, (((1,), (1,)), ((), ())), preferred_element_type=F32)


def t_mm(a, b):
    return lax.dot_general(a, b, (((0,), (0,)), ((), ())), preferred_element_type=F32)


def iota(shape, dim):
    return lax.broadcasted_iota(jnp.int32, shape, dim)


def normalize(x):
    centred = x - jnp.mean(x, axis=-1, keepdims=True)
    spread = jnp.mean(centred * centred, axis=-1, keepdims=True)
    factor = lax.rsqrt(spread + 1e-05)
    return centred * factor, factor


def norm_back(g, normed, factor):
    first = jnp.mean(g, axis=-1, keepdims=True)
    second = jnp.mean(g * normed, axis=-1, keepdims=True)
    return factor * (g - first - normed * second)


def blocks_of(x):
    lane = iota(x.shape, 1) // HEAD
    zero = jnp.zeros_like(x)
    return jnp.concatenate([jnp.where(lane == h, x, zero) for h in range(4)], axis=0)


def blocks_t(x):
    xt = x.T
    row = iota(xt.shape, 0) // HEAD
    zero = jnp.zeros_like(xt)
    return jnp.concatenate([jnp.where(row == h, xt, zero) for h in range(4)], axis=1)


def tri(x, lower):
    c = x.shape[0]
    row, col = iota(x.shape, 0), iota(x.shape, 1) % c
    keep = row >= col if lower else row <= col
    return jnp.where(keep, x, 0.0).astype(BF16)


def per_head(x, op, neutral):
    parts = []
    for p in range(x.shape[1] // 128):
        v = x[:, p * 128 : (p + 1) * 128]
        low = iota(v.shape, 1) < HEAD
        a = op(jnp.where(low, v, neutral), axis=-1, keepdims=True)
        b = op(jnp.where(low, neutral, v), axis=-1, keepdims=True)
        parts.append(jnp.where(low, a, b))
    return jnp.concatenate(parts, axis=1)


def head_square():
    return iota((QUAD, QUAD), 0) // HEAD == iota((QUAD, QUAD), 1) // HEAD


STATE = 2 * HEAD + 16


def store_state(st_ref, first, second, total):
    square = head_square()
    for g in range(st_ref.shape[0]):
        for k, ref in enumerate((first, second)):
            x = jnp.where(square, ref[g], 0.0)
            st_ref[g, k * HEAD : (k + 1) * HEAD, :] = (x[0:64] + x[64:128] + x[128:192] + x[192:256]).astype(BF16)
        hi, lo = hi_lo(total[0:1, g * QUAD : (g + 1) * QUAD])
        row = iota((16, QUAD), 0)
        spread = lambda x: jnp.broadcast_to(x.astype(F32), (16, QUAD))
        st_ref[g, 2 * HEAD :, :] = jnp.where(row == 0, spread(hi), jnp.where(row == 1, spread(lo), 0.0)).astype(BF16)


def load_state(st_ref, first, second, total):
    square = head_square()
    for g in range(st_ref.shape[0]):
        for k, ref in enumerate((first, second)):
            x = st_ref[g, k * HEAD : (k + 1) * HEAD, :].astype(F32)
            ref[g] = jnp.where(square, jnp.concatenate([x] * 4, axis=0), 0.0)
        both = jnp.sum(st_ref[g, 2 * HEAD :, :].astype(F32), axis=0, keepdims=True)
        total[:, g * QUAD : (g + 1) * QUAD] = jnp.broadcast_to(both, (8, QUAD))


def hi_lo(x):
    hi = x.astype(BF16)
    return hi, (x - hi.astype(F32)).astype(BF16)


def spread_vector(vecs, me, n, r, k, each, total):
    pick = (iota((n, n * r), 1) == iota((n, n * r), 0) * r + k).astype(BF16)
    rows = mm(pick, vecs).astype(BF16)
    tile = (iota((128, total), 1) % each == iota((128, total), 0)).astype(BF16)
    wide = mm(rows, tile)
    own = iota((n, total), 1) // each == (iota((n, total), 0) ^ me)
    return jnp.sum(jnp.where(own, wide, 0.0), axis=0, keepdims=True)


def gather_vector(vec, me, n, each):
    total = vec.shape[1]
    own = iota((n, total), 1) // each == (iota((n, total), 0) ^ me)
    wide = jnp.where(own, vec, 0.0).astype(BF16)
    tile = (iota((128, total), 1) % each == iota((128, total), 0)).astype(BF16)
    return mm_t(wide, tile).astype(BF16)


def share_ref(refs, j, n):
    near, low, high, high_core, rest_core = refs
    a, k, half = j % 4, j // 4, n // 8
    if a == 0:
        return near.at[k]
    if a == 1:
        return rest_core.at[k]
    if k >= half:
        return (high if a == 2 else high_core).at[k - half]
    return low.at[k] if a == 2 else rest_core.at[2 * half + k]


def share_shapes(n, r, width):
    half = n // 8
    return [jax.ShapeDtypeStruct((c, r, width), BF16) for c in (2 * half, half, half, half, 3 * half)]


def piece_refs(where, refs):
    return [refs[a] if row is None else refs[a].at[row] for a, row in where]


def pack_kernel(q, k, v, c, o, up, down, gain_a, gain_f, b_up, b_down, first, second):
    r, d = q.shape
    ff = up.shape[1]
    for p, ref in enumerate((q, k, v, c)):
        first[:, p * d : (p + 1) * d] = ref[...]
    tile = jnp.zeros((r, 128), F32)
    row, col = iota((r, 128), 0), iota((r, 128), 1)
    for i, ref in enumerate((gain_a, gain_f, b_up, b_down)):
        length = ref.shape[1]
        wide = jnp.broadcast_to(ref[...].astype(F32), (r, length))
        if length < 128:
            wide = jnp.concatenate([wide, jnp.zeros((r, 128 - length), F32)], axis=1)
        tile = jnp.where(row == i, wide, tile)
    first[:, 4 * d :] = tile.astype(BF16)
    second[:, 2 * ff + d :] = tile.astype(BF16)
    second[:, :ff] = up[...]
    for m in range(ff // d):
        second[:, ff + m * d : ff + (m + 1) * d] = down[m * r : (m + 1) * r, :]
    second[:, 2 * ff : 2 * ff + d] = o[...]


def pack(q, k, v, c, o, up, down, gain_a, gain_f, b_up, b_down):
    r, d = q.shape
    ff = up.shape[1]
    return pl.pallas_call(
        pack_kernel,
        out_shape=[jax.ShapeDtypeStruct((r, 4 * d + 128), BF16), jax.ShapeDtypeStruct((r, 2 * ff + d + 128), BF16)],
        cost_estimate=pl.CostEstimate(flops=0, bytes_accessed=1 << 20, transcendentals=0),
        name="pack",
    )(q, k, v, c, o, up, down, *(x.reshape(1, -1) for x in (gain_a, gain_f, b_up, b_down)))


def stack_kernel(*refs):
    for i, ref in enumerate(refs[:-1]):
        refs[-1][i] = ref[...]


def stack(items):
    return pl.pallas_call(
        stack_kernel,
        out_shape=jax.ShapeDtypeStruct((len(items),) + items[0].shape, items[0].dtype),
        cost_estimate=pl.CostEstimate(flops=0, bytes_accessed=2 << 20, transcendentals=0),
        name="stack",
    )(*items)


def project_kernel(where, arrays, r, me_ref, tok_hbm, *refs):
    n = len(where)
    pieces = piece_refs(where, refs)
    (att_hbm, pack_hbm, st_ref, w_hbm, gain_ref,
     tok, att, pack, w_all, vecs, normed, written, first, second, total, sems, vsems, tsem, osems) = refs[arrays:]
    t, d = att.shape
    wide = 4 * d
    rows = 256
    me = me_ref[0]
    load = pltpu.make_async_copy(tok_hbm, tok, tsem)
    load.start()
    vector_copies, copies = [], []
    for j in range(n):
        at = pl.multiple_of((me ^ j) * r, r)
        copies.append(pltpu.make_async_copy(pieces[j].at[:, pl.ds(0, wide)], w_all.at[pl.ds(at, r), :], sems.at[j]))
        vector_copies.append(pltpu.make_async_copy(pieces[j].at[:, pl.ds(wide, 128)], vecs.at[pl.ds(j * r, r), :], vsems.at[j]))
    for c in vector_copies + copies:
        c.start()
    sent = []

    def send(src, dst):
        copy = pltpu.make_async_copy(src, dst, osems.at[len(sent)])
        copy.start()
        sent.append(copy)

    load.wait()
    for i in range(t // rows):
        rs = pl.ds(i * rows, rows)
        normed[rs, :], _ = normalize(tok[rs, :].astype(F32))
    for c in vector_copies:
        c.wait()
    gain = spread_vector(vecs[...], me, n, r, 0, r, d)
    gain_ref[...] = jnp.broadcast_to(gain, gain_ref.shape)
    for c in copies:
        c.wait()
    send(w_all, w_hbm)
    sums = jnp.zeros((1, d), F32)
    for i in range(t // rows):
        rs = pl.ds(i * rows, rows)
        x = (normed[rs, :] * gain).astype(BF16)
        att[rs, :] = x
        send(att.at[rs, :], att_hbm.at[rs, :])
        for p in (3, 1, 2, 0):
            full = mm(x, w_all[:, p * d : (p + 1) * d]).astype(BF16)
            pack[rs, p * d : (p + 1) * d] = full
            if p == 3:
                new = jnp.exp(full.astype(F32)).astype(BF16)
                written[rs, :] = new
                sums += jnp.sum(new.astype(F32), axis=0, keepdims=True)
        send(pack.at[rs, :], pack_hbm.at[rs, :])
    for g in range(d // QUAD):
        s = slice(g * QUAD, (g + 1) * QUAD)
        first[g] = t_mm(pack[:, d + g * QUAD : d + (g + 1) * QUAD], written[:, s])
        second[g] = t_mm(written[:, s], pack[:, 2 * d + g * QUAD : 2 * d + (g + 1) * QUAD])
    total[...] = jnp.broadcast_to(sums, total.shape)
    store_state(st_ref, first, second, total)
    for c in sent:
        c.wait()


def project(me, tokens, where, pieces):
    t, d = tokens.shape
    n = len(where)
    r = d // n
    wide = 4 * d
    g = d // QUAD
    hbm = pl.BlockSpec(memory_space=pl.ANY)
    vmem = pl.BlockSpec(memory_space=pltpu.VMEM)
    return pl.pallas_call(
        partial(project_kernel, where, len(pieces), r),
        in_specs=[pl.BlockSpec(memory_space=pltpu.SMEM)] + [hbm] * (1 + len(pieces)),
        out_specs=[hbm, hbm, vmem, hbm, vmem],
        out_shape=[
            jax.ShapeDtypeStruct((t, d), BF16),
            jax.ShapeDtypeStruct((t, wide), BF16),
            jax.ShapeDtypeStruct((g, STATE, QUAD), BF16),
            jax.ShapeDtypeStruct((d, wide), BF16),
            jax.ShapeDtypeStruct((8, d), F32),
        ],
        scratch_shapes=[
            pltpu.VMEM((t, d), BF16),
            pltpu.VMEM((t, d), BF16),
            pltpu.VMEM((t, wide), BF16),
            pltpu.VMEM((d, wide), BF16),
            pltpu.VMEM((n * r, 128), BF16),
            pltpu.VMEM((t, d), F32),
            pltpu.VMEM((t, d), BF16),
            pltpu.VMEM((g, QUAD, QUAD), F32),
            pltpu.VMEM((g, QUAD, QUAD), F32),
            pltpu.VMEM((8, d), F32),
            pltpu.SemaphoreType.DMA((n,)),
            pltpu.SemaphoreType.DMA((n,)),
            pltpu.SemaphoreType.DMA,
            pltpu.SemaphoreType.DMA((1 + 2 * (t // 256),)),
        ],
        compiler_params=pltpu.CompilerParams(vmem_limit_bytes=VMEM_LIMIT),
        cost_estimate=pl.CostEstimate(flops=2 * t * d * wide, bytes_accessed=12 << 20, transcendentals=t * d),
        name="project",
    )(me, tokens, *pieces)


def mix_kernel(pack_ref, st_in, mix_ref, read_ref, score_ref, inv_ref, kts_ref, mvs_ref, kt, mv, tot):
    d = mix_ref.shape[1]
    rows = mix_ref.shape[0]

    @pl.when(pl.program_id(0) == 0)
    def _():
        load_state(st_in, kt, mv, tot)

    c = CHUNK
    square = head_square()
    ones = (iota((c, c), 0) >= iota((c, c), 1)).astype(BF16)
    units = [(b, g) for b in range(rows // c) for g in range(d // QUAD)]
    at = {(b, g): (slice(b * c, (b + 1) * c), slice(g * QUAD, (g + 1) * QUAD)) for b, g in units}
    part = lambda p: {(b, g): pack_ref[at[b, g][0], p * d + g * QUAD : p * d + (g + 1) * QUAD] for b, g in units}
    q, k, v = part(0), part(1), part(2)
    written = {x: jnp.exp(y.astype(F32)).astype(BF16) for x, y in part(3).items()}
    wb = {x: blocks_of(written[x]) for x in units}
    pairs = {x: tri(mm(q[x], blocks_t(k[x])), True) for x in units}
    ktb, mvb, inv = {}, {}, {}
    for x in units:
        b, g = x
        ktb[x], mvb[x] = kt[g].astype(BF16), mv[g].astype(BF16)
        kts_ref[b, g] = ktb[x]
        mvs_ref[b, g] = mvb[x]
        kt[g] += jnp.where(square, t_mm(k[x], written[x]), 0.0)
        mv[g] += jnp.where(square, t_mm(written[x], v[x]), 0.0)
        total = mm(ones, written[x]) + tot[0:1, at[x][1]]
        tot[0:1, at[x][1]] = total[c - 1 : c, :]
        inv[x] = 1.0 / total
        inv_ref[at[x]] = inv[x]
    score = {x: (mm(pairs[x], wb[x]) + mm(q[x], ktb[x])) * SCALE * inv[x] for x in units}
    for x in units:
        score_ref[at[x]] = score[x]
    e = {x: jnp.exp(score[x] - per_head(score[x], jnp.max, -jnp.inf)) for x in units}
    read = {x: e[x] / per_head(e[x], jnp.sum, 0.0) for x in units}
    for x in units:
        read_ref[at[x]] = read[x]
    scaled = {x: (read[x] * inv[x]).astype(BF16) for x in units}
    recall = {x: tri(mm(scaled[x], blocks_t(written[x])), True) for x in units}
    for x in units:
        mix_ref[at[x]] = (mm(recall[x], blocks_of(v[x])) + mm(scaled[x], mvb[x])).astype(BF16)


def mix(packed, state, rows=256):
    t, wide = packed.shape
    d = wide // 4
    g = d // QUAD
    const = lambda *shape: pl.BlockSpec(shape, lambda i: (0,) * len(shape))
    per = rows // CHUNK
    row = lambda w: pl.BlockSpec((rows, w), lambda i: (i, 0))
    return pl.pallas_call(
        mix_kernel,
        grid=(t // rows,),
        in_specs=[row(wide), const(g, STATE, QUAD)],
        out_specs=[row(d)] * 4 + [pl.BlockSpec((per, g, QUAD, QUAD), lambda i: (i, 0, 0, 0))] * 2,
        out_shape=[jax.ShapeDtypeStruct((t, d), BF16)] + [jax.ShapeDtypeStruct((t, d), F32)] * 3
        + [jax.ShapeDtypeStruct((t // CHUNK, g, QUAD, QUAD), BF16)] * 2,
        scratch_shapes=[pltpu.VMEM((g, QUAD, QUAD), F32), pltpu.VMEM((g, QUAD, QUAD), F32), pltpu.VMEM((8, d), F32)],
        compiler_params=pltpu.CompilerParams(vmem_limit_bytes=VMEM_LIMIT),
        cost_estimate=pl.CostEstimate(flops=6 * 10**9, bytes_accessed=16 << 20, transcendentals=2 * t * d),
        name="mix",
    )(packed, state)


def ffn_kernel(n, me_ref, mixed_hbm, tok_hbm, cot_hbm, full_ref, kept_hbm, gres_hbm, gmix_hbm, hid_hbm, down_hbm, *refs):
    share_refs = refs[:5]
    (mixed, tok, cot, kept, gres, gmix, w_out, w_up, w_down, vecs, hid, gpre, fin, gbr, normed_f, sems, osems, dsem) = refs[5:]
    me = me_ref[0]
    t, d = mixed.shape
    ff = w_up.shape[1]
    r = d // n
    mult = ff // d
    rows = 512
    part = 512
    steps = t // rows
    parts = ff // part

    def load(src, dst, i):
        copy = pltpu.make_async_copy(src, dst, sems.at[i])
        copy.start()
        return copy

    down_sem = 3
    early = [
        load(full_ref.at[:, pl.ds(2 * ff, d)], w_out, 0),
        load(mixed_hbm, mixed, 1),
        load(tok_hbm, tok, 2),
        load(full_ref.at[:, pl.ds(2 * ff + d, 128)], vecs, 4),
    ]
    late = [load(full_ref.at[:, pl.ds(0, ff)], w_up, 5), load(cot_hbm, cot, 6)]
    down = []
    for j in range(n):
        for m in range(mult):
            down.append((full_ref.at[pl.ds(j * r, r), pl.ds(ff + m * d, d)], w_down.at[pl.ds((j * mult + m) * r, r), :]))
    late += [load(src, dst, 7 + i) for i, (src, dst) in enumerate(down)]
    for c in early:
        c.wait()
    gain = spread_vector(vecs[...], 0, n, r, 1, r, d)
    b_up = spread_vector(vecs[...], 0, n, r, 2, r * mult, ff)
    b_down = spread_vector(vecs[...], 0, n, r, 3, r, d)

    sent = []

    def send(src, dst):
        copy = pltpu.make_async_copy(src, dst, osems.at[len(sent)])
        copy.start()
        sent.append(copy)

    ggain = jnp.zeros((1, d), F32)
    gbdown = jnp.zeros((1, d), F32)
    gbup = [jnp.zeros((1, part), F32)] * parts
    factors = []
    for i in range(steps):
        rs = pl.ds(i * rows, rows)
        resid = tok[rs, :].astype(F32) + mm(mixed[rs, :], w_out[...])
        kept[rs, :] = resid + b_down
        send(kept.at[rs, :], kept_hbm.at[rs, :])
        x, factor = normalize(resid)
        normed_f[rs, :] = x
        factors.append(factor)
        fin[rs, :] = (x * gain).astype(BF16)
    for c in late:
        c.wait()
    keep_down = pltpu.make_async_copy(w_down, down_hbm, dsem)
    keep_down.start()
    for i in range(steps):
        rs = pl.ds(i * rows, rows)
        ffn_in, normed, factor = fin[rs, :], normed_f[rs, :], factors[i]
        cot_b = cot[rs, :]
        cotf = cot_b.astype(F32)

        def entry(p):
            ps = slice(p * part, (p + 1) * part)
            return mm(ffn_in, w_up[:, ps]) + b_up[:, ps], mm_t(cot_b, w_down[ps, :])

        ready = entry(0)
        gin = None
        for p in range(parts):
            ps = slice(p * part, (p + 1) * part)
            pre, gh = ready
            if p + 1 < parts:
                ready = entry(p + 1)
            sig = 0.5 * jnp.tanh(0.5 * pre) + 0.5
            act = pre * sig
            gp = gh * (sig + act * (1.0 - sig))
            gbup[p] = gbup[p] + jnp.sum(gp, axis=0, keepdims=True)
            act, gp = act.astype(BF16), gp.astype(BF16)
            hid[rs, ps] = act
            gpre[rs, ps] = gp
            x = mm_t(gp, w_up[:, ps])
            gin = x if p == 0 else gin + x
        send(hid.at[rs, :], hid_hbm.at[rs, :])
        back = cotf + norm_back(gin * gain, normed, factor)
        gres[rs, :] = back
        send(gres.at[rs, :], gres_hbm.at[rs, :])
        back = back.astype(BF16)
        gbr[rs, :] = back
        gmix[rs, :] = mm_t(back, w_out[...]).astype(BF16)
        send(gmix.at[rs, :], gmix_hbm.at[rs, :])
        ggain += jnp.sum(gin * normed, axis=0, keepdims=True)
        gbdown += jnp.sum(cotf, axis=0, keepdims=True)

    def share(j, rows_of, ref, at, width):
        send(ref.at[rows_of(me ^ j), :], share_ref(share_refs, j, n).at[:, pl.ds(at, width)])

    own_rows = lambda f: pl.ds(pl.multiple_of(f * r, r), r)
    keep_down.wait()
    for p in range(parts):
        ps = slice(p * part, (p + 1) * part)
        w_down[ps, :] = t_mm(hid[:, ps], cot[...]).astype(BF16)
    for j in range(n):
        for m in range(mult):
            share(j, lambda f: pl.ds(pl.multiple_of((f * mult + m) * r, r), r), w_down, ff + m * d, d)
    w_out[...] = t_mm(mixed[...], gbr[...]).astype(BF16)
    va = gather_vector(ggain, 0, n, r)
    vb = gather_vector(jnp.concatenate(gbup, axis=1), 0, n, r * mult)
    vc = gather_vector(gbdown, 0, n, r)
    row = iota((r, 128), 0)
    pick = lambda v, j, i, rest: jnp.where(row == i, jnp.broadcast_to(v[j : j + 1].astype(F32), (r, 128)), rest)
    for j in range(n):
        tile = pick(va, j, 1, pick(vb, j, 2, pick(vc, j, 3, jnp.zeros((r, 128), F32))))
        vecs[j * r : (j + 1) * r, :] = tile.astype(BF16)
    for j in range(n):
        share(j, own_rows, w_out, 2 * ff, d)
        share(j, own_rows, vecs, 2 * ff + d, 128)
    for p in range(parts):
        ps = slice(p * part, (p + 1) * part)
        w_up[:, ps] = t_mm(fin[...], gpre[:, ps]).astype(BF16)
    for j in range(n):
        share(j, own_rows, w_up, 0, ff)
    for c in sent:
        c.wait()


def ffn(me, mixed, tokens, cot, full, ff, n):
    t, d = tokens.shape
    hbm = pl.BlockSpec(memory_space=pl.ANY)
    moves = n * (ff // d)
    return pl.pallas_call(
        partial(ffn_kernel, n),
        in_specs=[pl.BlockSpec(memory_space=pltpu.SMEM)] + [hbm] * 4,
        out_specs=[hbm] * 10,
        out_shape=[
            jax.ShapeDtypeStruct((t, d), F32),
            jax.ShapeDtypeStruct((t, d), F32),
            jax.ShapeDtypeStruct((t, d), BF16),
            jax.ShapeDtypeStruct((t, ff), BF16),
            jax.ShapeDtypeStruct((ff, d), BF16),
        ]
        + share_shapes(n, d // n, full.shape[1]),
        scratch_shapes=[pltpu.VMEM((t, d), BF16)] * 3
        + [pltpu.VMEM((t, d), F32), pltpu.VMEM((t, d), F32), pltpu.VMEM((t, d), BF16)]
        + [
            pltpu.VMEM((d, d), BF16),
            pltpu.VMEM((d, ff), BF16),
            pltpu.VMEM((ff, d), BF16),
            pltpu.VMEM((d, 128), BF16),
            pltpu.VMEM((t, ff), BF16),
            pltpu.VMEM((t, ff), BF16),
            pltpu.VMEM((t, d), BF16),
            pltpu.VMEM((t, d), BF16),
            pltpu.VMEM((t, d), F32),
            pltpu.SemaphoreType.DMA((7 + moves,)),
            pltpu.SemaphoreType.DMA((4 * (t // 256) + 3 * n + moves,)),
            pltpu.SemaphoreType.DMA,
        ],
        compiler_params=pltpu.CompilerParams(vmem_limit_bytes=VMEM_LIMIT),
        cost_estimate=pl.CostEstimate(flops=11 * t * d * ff, bytes_accessed=20 << 20, transcendentals=t * ff),
        name="ffn",
    )(me, mixed, tokens, cot, full)


def ffn_out_kernel(hid_ref, kept_ref, down_ref, out_ref):
    out_ref[...] = (kept_ref[...] + mm(hid_ref[...], down_ref[...])).astype(BF16)


def ffn_out(hid, kept, down, rows=256):
    t, ff = hid.shape
    d = kept.shape[1]
    row = lambda w: pl.BlockSpec((rows, w), lambda i: (i, 0))
    return pl.pallas_call(
        ffn_out_kernel,
        grid=(t // rows,),
        in_specs=[row(ff), row(d), pl.BlockSpec((ff, d), lambda i: (0, 0))],
        out_specs=row(d),
        out_shape=jax.ShapeDtypeStruct((t, d), BF16),
        compiler_params=pltpu.CompilerParams(vmem_limit_bytes=VMEM_LIMIT),
        cost_estimate=pl.CostEstimate(flops=2 * t * d * ff, bytes_accessed=9 << 20, transcendentals=0),
        name="ffn_out",
    )(hid, kept, down)


def read_back_kernel(pack_ref, gmix_ref, read_ref, score_ref, inv_ref, kts_ref, mvs_ref,
                     gq_ref, a_ref, u_ref, gtot_ref, st_ref, gk_ref, gv_ref, gt_ref):
    rows, d = gmix_ref.shape

    @pl.when(pl.program_id(0) == 0)
    def _():
        gk_ref[...] = jnp.zeros_like(gk_ref)
        gv_ref[...] = jnp.zeros_like(gv_ref)
        gt_ref[...] = jnp.zeros_like(gt_ref)

    c = CHUNK
    units = [(b, g) for b in range(rows // c) for g in range(d // QUAD)]
    at = {(b, g): (slice(b * c, (b + 1) * c), slice(g * QUAD, (g + 1) * QUAD)) for b, g in units}
    part = lambda p: {(b, g): pack_ref[at[b, g][0], p * d + g * QUAD : p * d + (g + 1) * QUAD] for b, g in units}
    q, k, v = part(0), part(1), part(2)
    written = {x: jnp.exp(y.astype(F32)).astype(BF16) for x, y in part(3).items()}
    wb = {x: blocks_of(written[x]) for x in units}
    gm = {x: gmix_ref[at[x]] for x in units}
    gpair = {x: tri(mm(gm[x], blocks_t(v[x])), True) for x in units}
    weighted = {x: (mm(gpair[x], wb[x]) + mm_t(gm[x], mvs_ref[x])) * inv_ref[at[x]] * read_ref[at[x]] for x in units}
    gscore = {x: weighted[x] - read_ref[at[x]] * per_head(weighted[x], jnp.sum, 0.0) for x in units}
    a, u = {}, {}
    for x in units:
        inv = inv_ref[at[x]]
        a[x] = (gscore[x] * inv * SCALE).astype(BF16)
        u[x] = (read_ref[at[x]] * inv).astype(BF16)
        a_ref[at[x]] = a[x]
        u_ref[at[x]] = u[x]
        gtot = (gscore[x] * score_ref[at[x]] + weighted[x]) * inv
        gtot_ref[at[x]] = gtot
        gt_ref[0:1, at[x][1]] += jnp.sum(gtot, axis=0, keepdims=True)
    spair = {x: tri(mm(a[x], blocks_t(written[x])), True) for x in units}
    for x in units:
        gq_ref[at[x]] = (mm(spair[x], blocks_of(k[x])) + mm_t(a[x], kts_ref[x])).astype(BF16)
    for g in range(d // QUAD):
        s = slice(g * QUAD, (g + 1) * QUAD)
        every = lambda y: jnp.concatenate([y[b, g] for b in range(rows // c)], axis=0)
        gk_ref[g] += t_mm(every(a), every(q))
        gv_ref[g] += t_mm(every(u), every(gm))

    @pl.when(pl.program_id(0) == pl.num_programs(0) - 1)
    def _():
        store_state(st_ref, gk_ref, gv_ref, gt_ref)


def read_back(packed, gmix, read, score, inv, kts, mvs, rows=512):
    t, wide = packed.shape
    d = wide // 4
    g = d // QUAD
    const = lambda *shape: pl.BlockSpec(shape, lambda i: (0,) * len(shape))
    per = rows // CHUNK
    row = lambda w: pl.BlockSpec((rows, w), lambda i: (i, 0))
    st = pl.BlockSpec((per, g, QUAD, QUAD), lambda i: (i, 0, 0, 0))
    return pl.pallas_call(
        read_back_kernel,
        grid=(t // rows,),
        in_specs=[row(wide), row(d), row(d), row(d), row(d), st, st],
        out_specs=[row(d)] * 4 + [const(g, STATE, QUAD)],
        out_shape=[jax.ShapeDtypeStruct((t, d), BF16)] * 3 + [jax.ShapeDtypeStruct((t, d), F32)]
        + [jax.ShapeDtypeStruct((g, STATE, QUAD), BF16)],
        scratch_shapes=[pltpu.VMEM((g, QUAD, QUAD), F32), pltpu.VMEM((g, QUAD, QUAD), F32), pltpu.VMEM((8, d), F32)],
        compiler_params=pltpu.CompilerParams(vmem_limit_bytes=VMEM_LIMIT),
        cost_estimate=pl.CostEstimate(flops=6 * 10**9, bytes_accessed=20 << 20, transcendentals=t * d),
        name="read_back",
    )(packed, gmix, read, score, inv, kts, mvs)


def write_back_kernel(n, me_ref, pack_ref, gmix_ref, a_ref, u_ref, gtot_ref, st_in, att_hbm, gq_hbm, out_ref, *refs):
    share_refs = refs[:5]
    gk, gv, gt, att, gq, grads, acc, isems, sems = refs[5:]
    rows, d = gmix_ref.shape
    loads = [pltpu.make_async_copy(att_hbm, att, isems.at[0]), pltpu.make_async_copy(gq_hbm, gq, isems.at[1])]

    @pl.when(pl.program_id(0) == 0)
    def _():
        for x in loads:
            x.start()
        load_state(st_in, gk, gv, gt)

    base = (pl.num_programs(0) - 1 - pl.program_id(0)) * rows
    c = CHUNK
    square = head_square()
    ones = (iota((c, c), 0) <= iota((c, c), 1)).astype(BF16)
    units = [(b, g) for b in reversed(range(rows // c)) for g in range(d // QUAD)]
    at = {(b, g): (slice(b * c, (b + 1) * c), slice(g * QUAD, (g + 1) * QUAD)) for b, g in units}
    part = lambda p: {(b, g): pack_ref[at[b, g][0], p * d + g * QUAD : p * d + (g + 1) * QUAD] for b, g in units}
    q, k, v = part(0), part(1), part(2)
    wf = {x: jnp.exp(y.astype(F32)) for x, y in part(3).items()}
    written = {x: wf[x].astype(BF16) for x in units}
    gm, a, u = ({x: ref[at[x]] for x in units} for ref in (gmix_ref, a_ref, u_ref))
    qb, gb, ab, ub = ({x: blocks_of(y[x]) for x in units} for y in (q, gm, a, u))
    gkb, gvb, after = {}, {}, {}
    for x in units:
        g = x[1]
        gkb[x], gvb[x] = gk[g].astype(BF16), gv[g].astype(BF16)
        gk[g] += jnp.where(square, t_mm(a[x], q[x]), 0.0)
        gv[g] += jnp.where(square, t_mm(u[x], gm[x]), 0.0)
        hi, lo = hi_lo(gtot_ref[at[x]])
        after[x] = mm(ones, hi) + mm(ones, lo) + gt[0:1, at[x][1]]
        gt[0:1, at[x][1]] = after[x][0:1, :]

    def out(p, x, y):
        y = y.astype(BF16)
        cols = slice(p * d + x[1] * QUAD, p * d + (x[1] + 1) * QUAD)
        out_ref[at[x][0], cols] = y
        grads[pl.ds(pl.multiple_of(base + x[0] * c, c), c), cols] = y

    st = {x: tri(mm(written[x], blocks_t(a[x])), False) for x in units}
    rt = {x: tri(mm(written[x], blocks_t(u[x])), False) for x in units}
    for x in units:
        out(0, x, mm(st[x], qb[x]) + mm(written[x], gkb[x]))
    for x in units:
        out(1, x, mm(rt[x], gb[x]) + mm(written[x], gvb[x]))
    pt = {x: tri(mm(k[x], blocks_t(q[x])), False) for x in units}
    gp = {x: tri(mm(v[x], blocks_t(gm[x])), False) for x in units}
    for x in units:
        gw = mm(pt[x], ab[x]) + mm(gp[x], ub[x]) + mm_t(k[x], gkb[x]) + mm_t(v[x], gvb[x])
        out(2, x, wf[x] * (gw - after[x]))

    @pl.when(pl.program_id(0) == pl.num_programs(0) - 1)
    def _():
        for x in loads:
            x.wait()
        r = d // n
        me = me_ref[0]
        acc[:, 0:d] = t_mm(att[...], gq[...]).astype(BF16)
        for p in range(3):
            acc[:, (p + 1) * d : (p + 2) * d] = t_mm(att[...], grads[:, p * d : (p + 1) * d]).astype(BF16)
        outs = []
        for j in range(n):
            frm = pl.multiple_of((me ^ j) * r, r)
            dst = share_ref(share_refs, j, n)
            outs.append(pltpu.make_async_copy(acc.at[pl.ds(frm, r), :], dst, sems.at[j]))
        for x in outs:
            x.start()
        for x in outs:
            x.wait()


def write_back(me, packed, gmix, a, u, gtot, state, att, gq, n, rows=256):
    t, wide = packed.shape
    d = wide // 4
    g = d // QUAD
    r = d // n
    last = t // rows - 1
    const = lambda *shape: pl.BlockSpec(shape, lambda i: (0,) * len(shape))
    row = lambda w: pl.BlockSpec((rows, w), lambda i: (last - i, 0))
    hbm = pl.BlockSpec(memory_space=pl.ANY)
    return pl.pallas_call(
        partial(write_back_kernel, n),
        grid=(t // rows,),
        in_specs=[pl.BlockSpec(memory_space=pltpu.SMEM), row(wide), row(d), row(d), row(d), row(d), const(g, STATE, QUAD), hbm, hbm],
        out_specs=[row(3 * d)] + [hbm] * 5,
        out_shape=[jax.ShapeDtypeStruct((t, 3 * d), BF16)] + share_shapes(n, r, wide),
        scratch_shapes=[
            pltpu.VMEM((g, QUAD, QUAD), F32),
            pltpu.VMEM((g, QUAD, QUAD), F32),
            pltpu.VMEM((8, d), F32),
            pltpu.VMEM((t, d), BF16),
            pltpu.VMEM((t, d), BF16),
            pltpu.VMEM((t, 3 * d), BF16),
            pltpu.VMEM((d, wide), BF16),
            pltpu.SemaphoreType.DMA((2,)),
            pltpu.SemaphoreType.DMA((n,)),
        ],
        compiler_params=pltpu.CompilerParams(vmem_limit_bytes=VMEM_LIMIT),
        cost_estimate=pl.CostEstimate(flops=11 * 10**9, bytes_accessed=18 << 20, transcendentals=t * d),
        name="write_back",
    )(me, packed, gmix, a, u, gtot, state, att, gq)


def input_grad_kernel(gain_ref, tok_ref, gq_ref, gkvc_ref, w_ref, gres_ref, out_ref):
    d = tok_ref.shape[1]
    gain = gain_ref[0:1, :]
    gin = mm_t(gq_ref[...], w_ref[:, 0:d]) + mm_t(gkvc_ref[...], w_ref[:, d:])
    normed, factor = normalize(tok_ref[...].astype(F32))
    out_ref[...] = gres_ref[...] + norm_back(gin * gain, normed, factor)


def input_grad(gain, tokens, gq, gkvc, w, gres, rows=256):
    t, d = tokens.shape
    const = lambda *shape: pl.BlockSpec(shape, lambda i: (0,) * len(shape))
    row = lambda w: pl.BlockSpec((rows, w), lambda i: (i, 0))
    return pl.pallas_call(
        input_grad_kernel,
        grid=(t // rows,),
        in_specs=[const(8, d), row(d), row(d), row(3 * d), const(d, 4 * d), row(d)],
        out_specs=row(d),
        out_shape=jax.ShapeDtypeStruct((t, d), F32),
        compiler_params=pltpu.CompilerParams(vmem_limit_bytes=VMEM_LIMIT),
        cost_estimate=pl.CostEstimate(flops=8 * t * d * d, bytes_accessed=12 << 20, transcendentals=0),
        name="input_grad",
    )(gain, tokens, gq, gkvc, w, gres)


def swap(x, mask, n):
    return lax.ppermute(x, "fsdp", [(i, i ^ mask) for i in range(n)])


def after(x, *first):
    return lax.optimization_barrier((x, *first))[0]


def add(*items):
    return sum(x.astype(F32) for x in items).astype(BF16)


def along_z(shard, n):
    return [shard] + [swap(shard, 4 * k, n) for k in range(1, n // 4)]


def along_x(own, n):
    return [swap(x, 2, n) for x in own]


def shift(x, by, seqs):
    return lax.ppermute(x, "seq", [(i, i + by) for i in range(seqs) if 0 <= i + by < seqs])


def others(state, direction, seqs):
    if seqs == 1:
        return jnp.zeros_like(state)
    if seqs > 2:
        state = state.astype(F32)
    total = shift(state, direction, seqs)
    step = 1
    while step < seqs - 1:
        total = total + shift(total, direction * step, seqs)
        step *= 2
    return total


def on_device(n, seqs, tokens, w_query, w_key, w_value, w_control, w_out, w_up, w_down,
              gain_attn, gain_ffn, bias_up, bias_down, cotangent):
    r, d = w_query.shape
    ff = w_up.shape[1]
    mult = ff // d
    me = lax.axis_index("fsdp").astype(jnp.int32).reshape(1)
    first, second = pack(w_query, w_key, w_value, w_control, w_out, w_up, w_down, gain_attn, gain_ffn, bias_up, bias_down)
    depth = n // 4
    own = along_z(first, n)
    full = lax.all_gather(second, "fsdp", axis=0, tiled=True)
    across = along_x(own, n)
    cored = [[swap(x, 1, n) for x in group] for group in (own, across)]
    att_pieces = [x for quad in zip(own, cored[0], across, cored[1]) for x in quad]
    att_where = [(j, None) for j in range(n)]
    att, packed, state, w_att, gain = project(me, tokens, att_where, att_pieces)
    mixed, read, score, inv, kts, mvs = mix(packed, others(state, 1, seqs))
    kept, gres, gmix, hid, full_down, *ffn_shares = ffn(me, mixed, tokens, cotangent, full, ff, n)
    half = depth // 2

    def start_sum(shares, *first):
        near, low, high, high_core, rest = shares
        high = add(after(high, *first) if first else high, swap(high_core, 1, n))
        rest = swap(rest, 1, n)
        return (near, rest), add(low, rest[depth:]), high

    def joined(near, crossed, base, *first):
        own, core = near
        own = after(own, *first)
        return {base + i: add(own[base + i], core[base + i], crossed[i]) for i in range(half)}

    def along(part, k):
        return swap(part, 4 * k, n) if k else part

    def seq_sum(x):
        step = 1
        while step < seqs:
            x = add(x, lax.ppermute(x, "seq", [(i, i ^ step) for i in range(seqs)]))
            step *= 2
        return x.astype(F32)

    near, low, high = start_sum(ffn_shares)
    crossed_high = swap(high, 2, n)
    gq, a, u, gtot, gstate = read_back(packed, after(gmix, high), read, score, inv, kts, mvs)
    crossed_low = swap(after(low, gq), 2, n)
    mine = joined(near, crossed_high, half, gq)
    ffn_parts = [along(mine[k], k) for k in range(half, depth)]
    gkvc, *shares = write_back(
        me, packed, gmix, a, u, gtot, after(others(gstate, -1, seqs), *mine.values()), att, gq, n
    )
    mine = joined(near, crossed_low, 0, gkvc)
    att_near, att_low, att_high = start_sum(shares, *ffn_parts[-1:], *mine.values())
    ffn_parts += [along(mine[k], k) for k in range(half)]
    crossed_high, crossed_low = swap(att_high, 2, n), swap(att_low, 2, n)
    layer_out = ffn_out(after(hid, att_low, mine[0]), kept, full_down)
    ffn_sum = add(after(mine[0], layer_out), *(p for p in ffn_parts if p is not mine[0]))
    mine = joined(att_near, crossed_high, half, layer_out)
    att_parts = [along(mine[k], k) for k in range(half, depth)]
    mine = joined(att_near, crossed_low, 0, layer_out, *mine.values())
    att_parts += [along(mine[k], k) for k in range(half)]
    grad_tokens = input_grad(gain, tokens, after(gq, *mine.values(), ffn_sum), gkvc, w_att, gres)
    ffn_share = seq_sum(ffn_sum)
    att_sum = add(*[after(p, grad_tokens) for p in att_parts])
    att_share = seq_sum(att_sum)
    gain_share = jnp.sum(att_share * first[:, : 4 * d].astype(F32), axis=1) / gain_attn.astype(F32)
    up, down, out, vec = (
        ffn_share[:, :ff],
        ffn_share[:, ff : 2 * ff],
        ffn_share[:, 2 * ff : 2 * ff + d],
        ffn_share[:, 2 * ff + d :],
    )
    down = jnp.concatenate([down[:, m * d : (m + 1) * d] for m in range(mult)], axis=0)
    return (
        layer_out,
        grad_tokens,
        att_share[:, 0:d],
        att_share[:, d : 2 * d],
        att_share[:, 2 * d : 3 * d],
        att_share[:, 3 * d :],
        out,
        up,
        down,
        gain_share,
        vec[1, :r],
        vec[2, : r * mult],
        vec[3, :r],
    )


def solution(mesh):
    tokens = P(("fsdp", "seq"), None)
    matrix = P("fsdp", None)
    vector = P("fsdp")
    return jax.shard_map(
        partial(on_device, mesh.shape["fsdp"], mesh.shape["seq"]),
        mesh=mesh,
        in_specs=(tokens,) + (matrix,) * 7 + (vector,) * 4 + (tokens,),
        out_specs=(tokens, tokens) + (matrix,) * 7 + (vector,) * 4,
        check_vma=False,
    )
```

```python
from functools import partial
import jax
import jax.numpy as jnp
from jax import lax
from jax.experimental import pallas as pl
from jax.experimental.pallas import tpu as pltpu
from jax.sharding import PartitionSpec as P

F32 = jnp.float32
BF16 = jnp.bfloat16
HEAD = 64
QUAD = 256
SCALE = HEAD ** -0.5
CHUNK = 128
VMEM_LIMIT = 60 * 1024 * 1024


def mm(a, b):
    return lax.dot_general(a, b, (((1,), (0,)), ((), ())), preferred_element_type=F32)


def mm_t(a, b):
    return lax.dot_general(a, b, (((1,), (1,)), ((), ())), preferred_element_type=F32)


def t_mm(a, b):
    return lax.dot_general(a, b, (((0,), (0,)), ((), ())), preferred_element_type=F32)


def iota(shape, dim):
    return lax.broadcasted_iota(jnp.int32, shape, dim)


def normalize(x):
    centred = x - jnp.mean(x, axis=-1, keepdims=True)
    spread = jnp.mean(centred * centred, axis=-1, keepdims=True)
    factor = lax.rsqrt(spread + 1e-05)
    return centred * factor, factor


def norm_back(g, normed, factor):
    first = jnp.mean(g, axis=-1, keepdims=True)
    second = jnp.mean(g * normed, axis=-1, keepdims=True)
    return factor * (g - first - normed * second)


def blocks_of(x):
    lane = iota(x.shape, 1) // HEAD
    zero = jnp.zeros_like(x)
    return jnp.concatenate([jnp.where(lane == h, x, zero) for h in range(4)], axis=0)


def blocks_t(x):
    xt = x.T
    row = iota(xt.shape, 0) // HEAD
    zero = jnp.zeros_like(xt)
    return jnp.concatenate([jnp.where(row == h, xt, zero) for h in range(4)], axis=1)


def tri(x, lower):
    c = x.shape[0]
    row, col = iota(x.shape, 0), iota(x.shape, 1) % c
    keep = row >= col if lower else row <= col
    return jnp.where(keep, x, 0.0).astype(BF16)


def per_head(x, op, neutral):
    parts = []
    for p in range(x.shape[1] // 128):
        v = x[:, p * 128 : (p + 1) * 128]
        low = iota(v.shape, 1) < HEAD
        a = op(jnp.where(low, v, neutral), axis=-1, keepdims=True)
        b = op(jnp.where(low, neutral, v), axis=-1, keepdims=True)
        parts.append(jnp.where(low, a, b))
    return jnp.concatenate(parts, axis=1)


def head_square():
    return iota((QUAD, QUAD), 0) // HEAD == iota((QUAD, QUAD), 1) // HEAD


STATE = 2 * HEAD + 16


def store_state(st_ref, first, second, total):
    square = head_square()
    for g in range(st_ref.shape[0]):
        for k, ref in enumerate((first, second)):
            x = jnp.where(square, ref[g], 0.0)
            st_ref[g, k * HEAD : (k + 1) * HEAD, :] = (x[0:64] + x[64:128] + x[128:192] + x[192:256]).astype(BF16)
        hi, lo = hi_lo(total[0:1, g * QUAD : (g + 1) * QUAD])
        row = iota((16, QUAD), 0)
        spread = lambda x: jnp.broadcast_to(x.astype(F32), (16, QUAD))
        st_ref[g, 2 * HEAD :, :] = jnp.where(row == 0, spread(hi), jnp.where(row == 1, spread(lo), 0.0)).astype(BF16)


def load_state(st_ref, first, second, total):
    square = head_square()
    for g in range(st_ref.shape[0]):
        for k, ref in enumerate((first, second)):
            x = st_ref[g, k * HEAD : (k + 1) * HEAD, :].astype(F32)
            ref[g] = jnp.where(square, jnp.concatenate([x] * 4, axis=0), 0.0)
        both = jnp.sum(st_ref[g, 2 * HEAD :, :].astype(F32), axis=0, keepdims=True)
        total[:, g * QUAD : (g + 1) * QUAD] = jnp.broadcast_to(both, (8, QUAD))


def hi_lo(x):
    hi = x.astype(BF16)
    return hi, (x - hi.astype(F32)).astype(BF16)


def spread_vector(vecs, me, n, r, k, each, total):
    pick = (iota((n, n * r), 1) == iota((n, n * r), 0) * r + k).astype(BF16)
    rows = mm(pick, vecs).astype(BF16)
    tile = (iota((128, total), 1) % each == iota((128, total), 0)).astype(BF16)
    wide = mm(rows, tile)
    own = iota((n, total), 1) // each == (iota((n, total), 0) ^ me)
    return jnp.sum(jnp.where(own, wide, 0.0), axis=0, keepdims=True)


def gather_vector(vec, me, n, each):
    total = vec.shape[1]
    own = iota((n, total), 1) // each == (iota((n, total), 0) ^ me)
    wide = jnp.where(own, vec, 0.0).astype(BF16)
    tile = (iota((128, total), 1) % each == iota((128, total), 0)).astype(BF16)
    return mm_t(wide, tile).astype(BF16)


def share_ref(refs, j, n):
    near, low, high, high_core, rest_core = refs
    a, k, half = j % 4, j // 4, n // 8
    if a == 0:
        return near.at[k]
    if a == 1:
        return rest_core.at[k]
    if k >= half:
        return (high if a == 2 else high_core).at[k - half]
    return low.at[k] if a == 2 else rest_core.at[2 * half + k]


def share_shapes(n, r, width):
    half = n // 8
    return [jax.ShapeDtypeStruct((c, r, width), BF16) for c in (2 * half, half, half, half, 3 * half)]


def piece_refs(where, refs):
    return [refs[a] if row is None else refs[a].at[row] for a, row in where]


def pack_kernel(q, k, v, c, o, up, down, gain_a, gain_f, b_up, b_down, first, second):
    r, d = q.shape
    ff = up.shape[1]
    for p, ref in enumerate((q, k, v, c)):
        first[:, p * d : (p + 1) * d] = ref[...]
    tile = jnp.zeros((r, 128), F32)
    row, col = iota((r, 128), 0), iota((r, 128), 1)
    for i, ref in enumerate((gain_a, gain_f, b_up, b_down)):
        length = ref.shape[1]
        wide = jnp.broadcast_to(ref[...].astype(F32), (r, length))
        if length < 128:
            wide = jnp.concatenate([wide, jnp.zeros((r, 128 - length), F32)], axis=1)
        tile = jnp.where(row == i, wide, tile)
    first[:, 4 * d :] = tile.astype(BF16)
    second[:, 2 * ff + d :] = tile.astype(BF16)
    second[:, :ff] = up[...]
    for m in range(ff // d):
        second[:, ff + m * d : ff + (m + 1) * d] = down[m * r : (m + 1) * r, :]
    second[:, 2 * ff : 2 * ff + d] = o[...]


def pack(q, k, v, c, o, up, down, gain_a, gain_f, b_up, b_down):
    r, d = q.shape
    ff = up.shape[1]
    return pl.pallas_call(
        pack_kernel,
        out_shape=[jax.ShapeDtypeStruct((r, 4 * d + 128), BF16), jax.ShapeDtypeStruct((r, 2 * ff + d + 128), BF16)],
        cost_estimate=pl.CostEstimate(flops=0, bytes_accessed=1 << 20, transcendentals=0),
        name="pack",
    )(q, k, v, c, o, up, down, *(x.reshape(1, -1) for x in (gain_a, gain_f, b_up, b_down)))


def stack_kernel(*refs):
    for i, ref in enumerate(refs[:-1]):
        refs[-1][i] = ref[...]


def stack(items):
    return pl.pallas_call(
        stack_kernel,
        out_shape=jax.ShapeDtypeStruct((len(items),) + items[0].shape, items[0].dtype),
        cost_estimate=pl.CostEstimate(flops=0, bytes_accessed=2 << 20, transcendentals=0),
        name="stack",
    )(*items)


def project_kernel(where, arrays, r, me_ref, tok_hbm, *refs):
    n = len(where)
    pieces = piece_refs(where, refs)
    (att_hbm, pack_hbm, st_ref, w_hbm, gain_ref,
     tok, att, pack, w_all, vecs, normed, written, first, second, total, sems, vsems, tsem, osems) = refs[arrays:]
    t, d = att.shape
    wide = 4 * d
    rows = 256
    me = me_ref[0]
    load = pltpu.make_async_copy(tok_hbm, tok, tsem)
    load.start()
    vector_copies, copies = [], []
    for j in range(n):
        at = pl.multiple_of((me ^ j) * r, r)
        copies.append(pltpu.make_async_copy(pieces[j].at[:, pl.ds(0, wide)], w_all.at[pl.ds(at, r), :], sems.at[j]))
        vector_copies.append(pltpu.make_async_copy(pieces[j].at[:, pl.ds(wide, 128)], vecs.at[pl.ds(j * r, r), :], vsems.at[j]))
    for c in vector_copies + copies:
        c.start()
    sent = []

    def send(src, dst):
        copy = pltpu.make_async_copy(src, dst, osems.at[len(sent)])
        copy.start()
        sent.append(copy)

    load.wait()
    for i in range(t // rows):
        rs = pl.ds(i * rows, rows)
        normed[rs, :], _ = normalize(tok[rs, :].astype(F32))
    for c in vector_copies:
        c.wait()
    gain = spread_vector(vecs[...], me, n, r, 0, r, d)
    gain_ref[...] = jnp.broadcast_to(gain, gain_ref.shape)
    for c in copies:
        c.wait()
    send(w_all, w_hbm)
    sums = jnp.zeros((1, d), F32)
    for i in range(t // rows):
        rs = pl.ds(i * rows, rows)
        x = (normed[rs, :] * gain).astype(BF16)
        att[rs, :] = x
        send(att.at[rs, :], att_hbm.at[rs, :])
        for p in (3, 1, 2, 0):
            full = mm(x, w_all[:, p * d : (p + 1) * d]).astype(BF16)
            pack[rs, p * d : (p + 1) * d] = full
            if p == 3:
                new = jnp.exp(full.astype(F32)).astype(BF16)
                written[rs, :] = new
                sums += jnp.sum(new.astype(F32), axis=0, keepdims=True)
        send(pack.at[rs, :], pack_hbm.at[rs, :])
    for g in range(d // QUAD):
        s = slice(g * QUAD, (g + 1) * QUAD)
        first[g] = t_mm(pack[:, d + g * QUAD : d + (g + 1) * QUAD], written[:, s])
        second[g] = t_mm(written[:, s], pack[:, 2 * d + g * QUAD : 2 * d + (g + 1) * QUAD])
    total[...] = jnp.broadcast_to(sums, total.shape)
    store_state(st_ref, first, second, total)
    for c in sent:
        c.wait()


def project(me, tokens, where, pieces):
    t, d = tokens.shape
    n = len(where)
    r = d // n
    wide = 4 * d
    g = d // QUAD
    hbm = pl.BlockSpec(memory_space=pl.ANY)
    vmem = pl.BlockSpec(memory_space=pltpu.VMEM)
    return pl.pallas_call(
        partial(project_kernel, where, len(pieces), r),
        in_specs=[pl.BlockSpec(memory_space=pltpu.SMEM)] + [hbm] * (1 + len(pieces)),
        out_specs=[hbm, hbm, vmem, hbm, vmem],
        out_shape=[
            jax.ShapeDtypeStruct((t, d), BF16),
            jax.ShapeDtypeStruct((t, wide), BF16),
            jax.ShapeDtypeStruct((g, STATE, QUAD), BF16),
            jax.ShapeDtypeStruct((d, wide), BF16),
            jax.ShapeDtypeStruct((8, d), F32),
        ],
        scratch_shapes=[
            pltpu.VMEM((t, d), BF16),
            pltpu.VMEM((t, d), BF16),
            pltpu.VMEM((t, wide), BF16),
            pltpu.VMEM((d, wide), BF16),
            pltpu.VMEM((n * r, 128), BF16),
            pltpu.VMEM((t, d), F32),
            pltpu.VMEM((t, d), BF16),
            pltpu.VMEM((g, QUAD, QUAD), F32),
            pltpu.VMEM((g, QUAD, QUAD), F32),
            pltpu.VMEM((8, d), F32),
            pltpu.SemaphoreType.DMA((n,)),
            pltpu.SemaphoreType.DMA((n,)),
            pltpu.SemaphoreType.DMA,
            pltpu.SemaphoreType.DMA((1 + 2 * (t // 256),)),
        ],
        compiler_params=pltpu.CompilerParams(vmem_limit_bytes=VMEM_LIMIT),
        cost_estimate=pl.CostEstimate(flops=2 * t * d * wide, bytes_accessed=12 << 20, transcendentals=t * d),
        name="project",
    )(me, tokens, *pieces)


def mix_kernel(pack_ref, st_in, mix_ref, read_ref, score_ref, inv_ref, kts_ref, mvs_ref, kt, mv, tot):
    d = mix_ref.shape[1]
    rows = mix_ref.shape[0]

    @pl.when(pl.program_id(0) == 0)
    def _():
        load_state(st_in, kt, mv, tot)

    c = CHUNK
    square = head_square()
    ones = (iota((c, c), 0) >= iota((c, c), 1)).astype(BF16)
    units = [(b, g) for b in range(rows // c) for g in range(d // QUAD)]
    at = {(b, g): (slice(b * c, (b + 1) * c), slice(g * QUAD, (g + 1) * QUAD)) for b, g in units}
    part = lambda p: {(b, g): pack_ref[at[b, g][0], p * d + g * QUAD : p * d + (g + 1) * QUAD] for b, g in units}
    q, k, v = part(0), part(1), part(2)
    written = {x: jnp.exp(y.astype(F32)).astype(BF16) for x, y in part(3).items()}
    wb = {x: blocks_of(written[x]) for x in units}
    pairs = {x: tri(mm(q[x], blocks_t(k[x])), True) for x in units}
    ktb, mvb, inv = {}, {}, {}
    for x in units:
        b, g = x
        ktb[x], mvb[x] = kt[g].astype(BF16), mv[g].astype(BF16)
        kts_ref[b, g] = ktb[x]
        mvs_ref[b, g] = mvb[x]
        kt[g] += jnp.where(square, t_mm(k[x], written[x]), 0.0)
        mv[g] += jnp.where(square, t_mm(written[x], v[x]), 0.0)
        total = mm(ones, written[x]) + tot[0:1, at[x][1]]
        tot[0:1, at[x][1]] = total[c - 1 : c, :]
        inv[x] = 1.0 / total
        inv_ref[at[x]] = inv[x]
    score = {x: (mm(pairs[x], wb[x]) + mm(q[x], ktb[x])) * SCALE * inv[x] for x in units}
    for x in units:
        score_ref[at[x]] = score[x]
    e = {x: jnp.exp(score[x] - per_head(score[x], jnp.max, -jnp.inf)) for x in units}
    read = {x: e[x] / per_head(e[x], jnp.sum, 0.0) for x in units}
    for x in units:
        read_ref[at[x]] = read[x]
    scaled = {x: (read[x] * inv[x]).astype(BF16) for x in units}
    recall = {x: tri(mm(scaled[x], blocks_t(written[x])), True) for x in units}
    for x in units:
        mix_ref[at[x]] = (mm(recall[x], blocks_of(v[x])) + mm(scaled[x], mvb[x])).astype(BF16)


def mix(packed, state, rows=256):
    t, wide = packed.shape
    d = wide // 4
    g = d // QUAD
    const = lambda *shape: pl.BlockSpec(shape, lambda i: (0,) * len(shape))
    per = rows // CHUNK
    row = lambda w: pl.BlockSpec((rows, w), lambda i: (i, 0))
    return pl.pallas_call(
        mix_kernel,
        grid=(t // rows,),
        in_specs=[row(wide), const(g, STATE, QUAD)],
        out_specs=[row(d)] * 4 + [pl.BlockSpec((per, g, QUAD, QUAD), lambda i: (i, 0, 0, 0))] * 2,
        out_shape=[jax.ShapeDtypeStruct((t, d), BF16)] + [jax.ShapeDtypeStruct((t, d), F32)] * 3
        + [jax.ShapeDtypeStruct((t // CHUNK, g, QUAD, QUAD), BF16)] * 2,
        scratch_shapes=[pltpu.VMEM((g, QUAD, QUAD), F32), pltpu.VMEM((g, QUAD, QUAD), F32), pltpu.VMEM((8, d), F32)],
        compiler_params=pltpu.CompilerParams(vmem_limit_bytes=VMEM_LIMIT),
        cost_estimate=pl.CostEstimate(flops=6 * 10**9, bytes_accessed=16 << 20, transcendentals=2 * t * d),
        name="mix",
    )(packed, state)


def ffn_kernel(n, me_ref, mixed_hbm, tok_hbm, cot_hbm, full_ref, kept_hbm, gres_hbm, gmix_hbm, hid_hbm, down_hbm, *refs):
    share_refs = refs[:5]
    (mixed, tok, cot, kept, gres, gmix, w_out, w_up, w_down, vecs, hid, gpre, fin, gbr, normed_f, sems, osems, dsem) = refs[5:]
    me = me_ref[0]
    t, d = mixed.shape
    ff = w_up.shape[1]
    r = d // n
    mult = ff // d
    rows = 512
    part = 512
    steps = t // rows
    parts = ff // part

    def load(src, dst, i):
        copy = pltpu.make_async_copy(src, dst, sems.at[i])
        copy.start()
        return copy

    down_sem = 3
    early = [
        load(full_ref.at[:, pl.ds(2 * ff, d)], w_out, 0),
        load(mixed_hbm, mixed, 1),
        load(tok_hbm, tok, 2),
        load(full_ref.at[:, pl.ds(2 * ff + d, 128)], vecs, 4),
    ]
    late = [load(full_ref.at[:, pl.ds(0, ff)], w_up, 5), load(cot_hbm, cot, 6)]
    down = []
    for j in range(n):
        for m in range(mult):
            down.append((full_ref.at[pl.ds(j * r, r), pl.ds(ff + m * d, d)], w_down.at[pl.ds((j * mult + m) * r, r), :]))
    late += [load(src, dst, 7 + i) for i, (src, dst) in enumerate(down)]
    for c in early:
        c.wait()
    gain = spread_vector(vecs[...], 0, n, r, 1, r, d)
    b_up = spread_vector(vecs[...], 0, n, r, 2, r * mult, ff)
    b_down = spread_vector(vecs[...], 0, n, r, 3, r, d)

    sent = []

    def send(src, dst):
        copy = pltpu.make_async_copy(src, dst, osems.at[len(sent)])
        copy.start()
        sent.append(copy)

    ggain = jnp.zeros((1, d), F32)
    gbdown = jnp.zeros((1, d), F32)
    gbup = [jnp.zeros((1, part), F32)] * parts
    factors = []
    for i in range(steps):
        rs = pl.ds(i * rows, rows)
        resid = tok[rs, :].astype(F32) + mm(mixed[rs, :], w_out[...])
        kept[rs, :] = resid + b_down
        send(kept.at[rs, :], kept_hbm.at[rs, :])
        x, factor = normalize(resid)
        normed_f[rs, :] = x
        factors.append(factor)
        fin[rs, :] = (x * gain).astype(BF16)
    for c in late:
        c.wait()
    keep_down = pltpu.make_async_copy(w_down, down_hbm, dsem)
    keep_down.start()
    for i in range(steps):
        rs = pl.ds(i * rows, rows)
        ffn_in, normed, factor = fin[rs, :], normed_f[rs, :], factors[i]
        cot_b = cot[rs, :]
        cotf = cot_b.astype(F32)

        def entry(p):
            ps = slice(p * part, (p + 1) * part)
            return mm(ffn_in, w_up[:, ps]) + b_up[:, ps], mm_t(cot_b, w_down[ps, :])

        ready = entry(0)
        gin = None
        for p in range(parts):
            ps = slice(p * part, (p + 1) * part)
            pre, gh = ready
            if p + 1 < parts:
                ready = entry(p + 1)
            sig = 0.5 * jnp.tanh(0.5 * pre) + 0.5
            act = pre * sig
            gp = gh * (sig + act * (1.0 - sig))
            gbup[p] = gbup[p] + jnp.sum(gp, axis=0, keepdims=True)
            act, gp = act.astype(BF16), gp.astype(BF16)
            hid[rs, ps] = act
            gpre[rs, ps] = gp
            x = mm_t(gp, w_up[:, ps])
            gin = x if p == 0 else gin + x
        send(hid.at[rs, :], hid_hbm.at[rs, :])
        back = cotf + norm_back(gin * gain, normed, factor)
        gres[rs, :] = back
        send(gres.at[rs, :], gres_hbm.at[rs, :])
        back = back.astype(BF16)
        gbr[rs, :] = back
        gmix[rs, :] = mm_t(back, w_out[...]).astype(BF16)
        send(gmix.at[rs, :], gmix_hbm.at[rs, :])
        ggain += jnp.sum(gin * normed, axis=0, keepdims=True)
        gbdown += jnp.sum(cotf, axis=0, keepdims=True)

    def share(j, rows_of, ref, at, width):
        send(ref.at[rows_of(me ^ j), :], share_ref(share_refs, j, n).at[:, pl.ds(at, width)])

    own_rows = lambda f: pl.ds(pl.multiple_of(f * r, r), r)
    keep_down.wait()
    for p in range(parts):
        ps = slice(p * part, (p + 1) * part)
        w_down[ps, :] = t_mm(hid[:, ps], cot[...]).astype(BF16)
    for j in range(n):
        for m in range(mult):
            share(j, lambda f: pl.ds(pl.multiple_of((f * mult + m) * r, r), r), w_down, ff + m * d, d)
    w_out[...] = t_mm(mixed[...], gbr[...]).astype(BF16)
    va = gather_vector(ggain, 0, n, r)
    vb = gather_vector(jnp.concatenate(gbup, axis=1), 0, n, r * mult)
    vc = gather_vector(gbdown, 0, n, r)
    row = iota((r, 128), 0)
    pick = lambda v, j, i, rest: jnp.where(row == i, jnp.broadcast_to(v[j : j + 1].astype(F32), (r, 128)), rest)
    for j in range(n):
        tile = pick(va, j, 1, pick(vb, j, 2, pick(vc, j, 3, jnp.zeros((r, 128), F32))))
        vecs[j * r : (j + 1) * r, :] = tile.astype(BF16)
    for j in range(n):
        share(j, own_rows, w_out, 2 * ff, d)
        share(j, own_rows, vecs, 2 * ff + d, 128)
    for p in range(parts):
        ps = slice(p * part, (p + 1) * part)
        w_up[:, ps] = t_mm(fin[...], gpre[:, ps]).astype(BF16)
    for j in range(n):
        share(j, own_rows, w_up, 0, ff)
    for c in sent:
        c.wait()


def ffn(me, mixed, tokens, cot, full, ff, n):
    t, d = tokens.shape
    hbm = pl.BlockSpec(memory_space=pl.ANY)
    moves = n * (ff // d)
    return pl.pallas_call(
        partial(ffn_kernel, n),
        in_specs=[pl.BlockSpec(memory_space=pltpu.SMEM)] + [hbm] * 4,
        out_specs=[hbm] * 10,
        out_shape=[
            jax.ShapeDtypeStruct((t, d), F32),
            jax.ShapeDtypeStruct((t, d), F32),
            jax.ShapeDtypeStruct((t, d), BF16),
            jax.ShapeDtypeStruct((t, ff), BF16),
            jax.ShapeDtypeStruct((ff, d), BF16),
        ]
        + share_shapes(n, d // n, full.shape[1]),
        scratch_shapes=[pltpu.VMEM((t, d), BF16)] * 3
        + [pltpu.VMEM((t, d), F32), pltpu.VMEM((t, d), F32), pltpu.VMEM((t, d), BF16)]
        + [
            pltpu.VMEM((d, d), BF16),
            pltpu.VMEM((d, ff), BF16),
            pltpu.VMEM((ff, d), BF16),
            pltpu.VMEM((d, 128), BF16),
            pltpu.VMEM((t, ff), BF16),
            pltpu.VMEM((t, ff), BF16),
            pltpu.VMEM((t, d), BF16),
            pltpu.VMEM((t, d), BF16),
            pltpu.VMEM((t, d), F32),
            pltpu.SemaphoreType.DMA((7 + moves,)),
            pltpu.SemaphoreType.DMA((4 * (t // 256) + 3 * n + moves,)),
            pltpu.SemaphoreType.DMA,
        ],
        compiler_params=pltpu.CompilerParams(vmem_limit_bytes=VMEM_LIMIT),
        cost_estimate=pl.CostEstimate(flops=11 * t * d * ff, bytes_accessed=20 << 20, transcendentals=t * ff),
        name="ffn",
    )(me, mixed, tokens, cot, full)


def ffn_out_kernel(hid_ref, kept_ref, down_ref, out_ref):
    out_ref[...] = (kept_ref[...] + mm(hid_ref[...], down_ref[...])).astype(BF16)


def ffn_out(hid, kept, down, rows=512):
    t, ff = hid.shape
    d = kept.shape[1]
    row = lambda w: pl.BlockSpec((rows, w), lambda i: (i, 0))
    return pl.pallas_call(
        ffn_out_kernel,
        grid=(t // rows,),
        in_specs=[row(ff), row(d), pl.BlockSpec((ff, d), lambda i: (0, 0))],
        out_specs=row(d),
        out_shape=jax.ShapeDtypeStruct((t, d), BF16),
        compiler_params=pltpu.CompilerParams(vmem_limit_bytes=VMEM_LIMIT),
        cost_estimate=pl.CostEstimate(flops=2 * t * d * ff, bytes_accessed=9 << 20, transcendentals=0),
        name="ffn_out",
    )(hid, kept, down)


def read_back_kernel(pack_ref, gmix_ref, read_ref, score_ref, inv_ref, kts_ref, mvs_ref,
                     gq_ref, a_ref, u_ref, gtot_ref, st_ref, gk_ref, gv_ref, gt_ref):
    rows, d = gmix_ref.shape

    @pl.when(pl.program_id(0) == 0)
    def _():
        gk_ref[...] = jnp.zeros_like(gk_ref)
        gv_ref[...] = jnp.zeros_like(gv_ref)
        gt_ref[...] = jnp.zeros_like(gt_ref)

    c = CHUNK
    units = [(b, g) for b in range(rows // c) for g in range(d // QUAD)]
    at = {(b, g): (slice(b * c, (b + 1) * c), slice(g * QUAD, (g + 1) * QUAD)) for b, g in units}
    part = lambda p: {(b, g): pack_ref[at[b, g][0], p * d + g * QUAD : p * d + (g + 1) * QUAD] for b, g in units}
    q, k, v = part(0), part(1), part(2)
    written = {x: jnp.exp(y.astype(F32)).astype(BF16) for x, y in part(3).items()}
    wb = {x: blocks_of(written[x]) for x in units}
    gm = {x: gmix_ref[at[x]] for x in units}
    gpair = {x: tri(mm(gm[x], blocks_t(v[x])), True) for x in units}
    weighted = {x: (mm(gpair[x], wb[x]) + mm_t(gm[x], mvs_ref[x])) * inv_ref[at[x]] * read_ref[at[x]] for x in units}
    gscore = {x: weighted[x] - read_ref[at[x]] * per_head(weighted[x], jnp.sum, 0.0) for x in units}
    a, u = {}, {}
    for x in units:
        inv = inv_ref[at[x]]
        a[x] = (gscore[x] * inv * SCALE).astype(BF16)
        u[x] = (read_ref[at[x]] * inv).astype(BF16)
        a_ref[at[x]] = a[x]
        u_ref[at[x]] = u[x]
        gtot = (gscore[x] * score_ref[at[x]] + weighted[x]) * inv
        gtot_ref[at[x]] = gtot
        gt_ref[0:1, at[x][1]] += jnp.sum(gtot, axis=0, keepdims=True)
    spair = {x: tri(mm(a[x], blocks_t(written[x])), True) for x in units}
    for x in units:
        gq_ref[at[x]] = (mm(spair[x], blocks_of(k[x])) + mm_t(a[x], kts_ref[x])).astype(BF16)
    for g in range(d // QUAD):
        s = slice(g * QUAD, (g + 1) * QUAD)
        every = lambda y: jnp.concatenate([y[b, g] for b in range(rows // c)], axis=0)
        gk_ref[g] += t_mm(every(a), every(q))
        gv_ref[g] += t_mm(every(u), every(gm))

    @pl.when(pl.program_id(0) == pl.num_programs(0) - 1)
    def _():
        store_state(st_ref, gk_ref, gv_ref, gt_ref)


def read_back(packed, gmix, read, score, inv, kts, mvs, rows=512):
    t, wide = packed.shape
    d = wide // 4
    g = d // QUAD
    const = lambda *shape: pl.BlockSpec(shape, lambda i: (0,) * len(shape))
    per = rows // CHUNK
    row = lambda w: pl.BlockSpec((rows, w), lambda i: (i, 0))
    st = pl.BlockSpec((per, g, QUAD, QUAD), lambda i: (i, 0, 0, 0))
    return pl.pallas_call(
        read_back_kernel,
        grid=(t // rows,),
        in_specs=[row(wide), row(d), row(d), row(d), row(d), st, st],
        out_specs=[row(d)] * 4 + [const(g, STATE, QUAD)],
        out_shape=[jax.ShapeDtypeStruct((t, d), BF16)] * 3 + [jax.ShapeDtypeStruct((t, d), F32)]
        + [jax.ShapeDtypeStruct((g, STATE, QUAD), BF16)],
        scratch_shapes=[pltpu.VMEM((g, QUAD, QUAD), F32), pltpu.VMEM((g, QUAD, QUAD), F32), pltpu.VMEM((8, d), F32)],
        compiler_params=pltpu.CompilerParams(vmem_limit_bytes=VMEM_LIMIT),
        cost_estimate=pl.CostEstimate(flops=6 * 10**9, bytes_accessed=20 << 20, transcendentals=t * d),
        name="read_back",
    )(packed, gmix, read, score, inv, kts, mvs)


def write_back_kernel(n, me_ref, pack_ref, gmix_ref, a_ref, u_ref, gtot_ref, st_in, att_hbm, gq_hbm, out_ref, *refs):
    share_refs = refs[:5]
    gk, gv, gt, att, gq, grads, acc, isems, sems = refs[5:]
    rows, d = gmix_ref.shape
    loads = [pltpu.make_async_copy(att_hbm, att, isems.at[0]), pltpu.make_async_copy(gq_hbm, gq, isems.at[1])]

    @pl.when(pl.program_id(0) == 0)
    def _():
        for x in loads:
            x.start()
        load_state(st_in, gk, gv, gt)

    base = (pl.num_programs(0) - 1 - pl.program_id(0)) * rows
    c = CHUNK
    square = head_square()
    ones = (iota((c, c), 0) <= iota((c, c), 1)).astype(BF16)
    units = [(b, g) for b in reversed(range(rows // c)) for g in range(d // QUAD)]
    at = {(b, g): (slice(b * c, (b + 1) * c), slice(g * QUAD, (g + 1) * QUAD)) for b, g in units}
    part = lambda p: {(b, g): pack_ref[at[b, g][0], p * d + g * QUAD : p * d + (g + 1) * QUAD] for b, g in units}
    q, k, v = part(0), part(1), part(2)
    wf = {x: jnp.exp(y.astype(F32)) for x, y in part(3).items()}
    written = {x: wf[x].astype(BF16) for x in units}
    gm, a, u = ({x: ref[at[x]] for x in units} for ref in (gmix_ref, a_ref, u_ref))
    qb, gb, ab, ub = ({x: blocks_of(y[x]) for x in units} for y in (q, gm, a, u))
    gkb, gvb, after = {}, {}, {}
    for x in units:
        g = x[1]
        gkb[x], gvb[x] = gk[g].astype(BF16), gv[g].astype(BF16)
        gk[g] += jnp.where(square, t_mm(a[x], q[x]), 0.0)
        gv[g] += jnp.where(square, t_mm(u[x], gm[x]), 0.0)
        hi, lo = hi_lo(gtot_ref[at[x]])
        after[x] = mm(ones, hi) + mm(ones, lo) + gt[0:1, at[x][1]]
        gt[0:1, at[x][1]] = after[x][0:1, :]

    def out(p, x, y):
        y = y.astype(BF16)
        cols = slice(p * d + x[1] * QUAD, p * d + (x[1] + 1) * QUAD)
        out_ref[at[x][0], cols] = y
        grads[pl.ds(pl.multiple_of(base + x[0] * c, c), c), cols] = y

    st = {x: tri(mm(written[x], blocks_t(a[x])), False) for x in units}
    rt = {x: tri(mm(written[x], blocks_t(u[x])), False) for x in units}
    for x in units:
        out(0, x, mm(st[x], qb[x]) + mm(written[x], gkb[x]))
    for x in units:
        out(1, x, mm(rt[x], gb[x]) + mm(written[x], gvb[x]))
    pt = {x: tri(mm(k[x], blocks_t(q[x])), False) for x in units}
    gp = {x: tri(mm(v[x], blocks_t(gm[x])), False) for x in units}
    for x in units:
        gw = mm(pt[x], ab[x]) + mm(gp[x], ub[x]) + mm_t(k[x], gkb[x]) + mm_t(v[x], gvb[x])
        out(2, x, wf[x] * (gw - after[x]))

    @pl.when(pl.program_id(0) == pl.num_programs(0) - 1)
    def _():
        for x in loads:
            x.wait()
        r = d // n
        me = me_ref[0]
        acc[:, 0:d] = t_mm(att[...], gq[...]).astype(BF16)
        for p in range(3):
            acc[:, (p + 1) * d : (p + 2) * d] = t_mm(att[...], grads[:, p * d : (p + 1) * d]).astype(BF16)
        outs = []
        for j in range(n):
            frm = pl.multiple_of((me ^ j) * r, r)
            dst = share_ref(share_refs, j, n)
            outs.append(pltpu.make_async_copy(acc.at[pl.ds(frm, r), :], dst, sems.at[j]))
        for x in outs:
            x.start()
        for x in outs:
            x.wait()


def write_back(me, packed, gmix, a, u, gtot, state, att, gq, n, rows=256):
    t, wide = packed.shape
    d = wide // 4
    g = d // QUAD
    r = d // n
    last = t // rows - 1
    const = lambda *shape: pl.BlockSpec(shape, lambda i: (0,) * len(shape))
    row = lambda w: pl.BlockSpec((rows, w), lambda i: (last - i, 0))
    hbm = pl.BlockSpec(memory_space=pl.ANY)
    return pl.pallas_call(
        partial(write_back_kernel, n),
        grid=(t // rows,),
        in_specs=[pl.BlockSpec(memory_space=pltpu.SMEM), row(wide), row(d), row(d), row(d), row(d), const(g, STATE, QUAD), hbm, hbm],
        out_specs=[row(3 * d)] + [hbm] * 5,
        out_shape=[jax.ShapeDtypeStruct((t, 3 * d), BF16)] + share_shapes(n, r, wide),
        scratch_shapes=[
            pltpu.VMEM((g, QUAD, QUAD), F32),
            pltpu.VMEM((g, QUAD, QUAD), F32),
            pltpu.VMEM((8, d), F32),
            pltpu.VMEM((t, d), BF16),
            pltpu.VMEM((t, d), BF16),
            pltpu.VMEM((t, 3 * d), BF16),
            pltpu.VMEM((d, wide), BF16),
            pltpu.SemaphoreType.DMA((2,)),
            pltpu.SemaphoreType.DMA((n,)),
        ],
        compiler_params=pltpu.CompilerParams(vmem_limit_bytes=VMEM_LIMIT),
        cost_estimate=pl.CostEstimate(flops=11 * 10**9, bytes_accessed=18 << 20, transcendentals=t * d),
        name="write_back",
    )(me, packed, gmix, a, u, gtot, state, att, gq)


def input_grad_kernel(gain_ref, tok_ref, gq_ref, gkvc_ref, w_ref, gres_ref, out_ref):
    rows, d = tok_ref.shape
    gain = gain_ref[0:1, :]
    part = 256
    cuts = [slice(i, i + part) for i in range(0, rows, part)]
    product = lambda s: mm_t(gq_ref[s, :], w_ref[:, 0:d]) + mm_t(gkvc_ref[s, :], w_ref[:, d:])
    gin = product(cuts[0])
    for i, s in enumerate(cuts):
        coming = product(cuts[i + 1]) if i + 1 < len(cuts) else None
        normed, factor = normalize(tok_ref[s, :].astype(F32))
        out_ref[s, :] = gres_ref[s, :] + norm_back(gin * gain, normed, factor)
        gin = coming


def input_grad(gain, tokens, gq, gkvc, w, gres, rows=512):
    t, d = tokens.shape
    const = lambda *shape: pl.BlockSpec(shape, lambda i: (0,) * len(shape))
    row = lambda w: pl.BlockSpec((rows, w), lambda i: (i, 0))
    return pl.pallas_call(
        input_grad_kernel,
        grid=(t // rows,),
        in_specs=[const(8, d), row(d), row(d), row(3 * d), const(d, 4 * d), row(d)],
        out_specs=row(d),
        out_shape=jax.ShapeDtypeStruct((t, d), F32),
        compiler_params=pltpu.CompilerParams(vmem_limit_bytes=VMEM_LIMIT),
        cost_estimate=pl.CostEstimate(flops=8 * t * d * d, bytes_accessed=12 << 20, transcendentals=0),
        name="input_grad",
    )(gain, tokens, gq, gkvc, w, gres)


def swap(x, mask, n):
    return lax.ppermute(x, "fsdp", [(i, i ^ mask) for i in range(n)])


def after(x, *first):
    return lax.optimization_barrier((x, *first))[0]


def add(*items):
    return sum(x.astype(F32) for x in items).astype(BF16)


def along_z(shard, n):
    return [shard] + [swap(shard, 4 * k, n) for k in range(1, n // 4)]


def along_x(own, n):
    return [swap(x, 2, n) for x in own]


def shift(x, by, seqs):
    return lax.ppermute(x, "seq", [(i, i + by) for i in range(seqs) if 0 <= i + by < seqs])


def others(state, direction, seqs):
    if seqs == 1:
        return jnp.zeros_like(state)
    if seqs > 2:
        state = state.astype(F32)
    total = shift(state, direction, seqs)
    step = 1
    while step < seqs - 1:
        total = total + shift(total, direction * step, seqs)
        step *= 2
    return total


def on_device(n, seqs, tokens, w_query, w_key, w_value, w_control, w_out, w_up, w_down,
              gain_attn, gain_ffn, bias_up, bias_down, cotangent):
    r, d = w_query.shape
    ff = w_up.shape[1]
    mult = ff // d
    me = lax.axis_index("fsdp").astype(jnp.int32).reshape(1)
    first, second = pack(w_query, w_key, w_value, w_control, w_out, w_up, w_down, gain_attn, gain_ffn, bias_up, bias_down)
    depth = n // 4
    own = along_z(first, n)
    full = lax.all_gather(second, "fsdp", axis=0, tiled=True)
    across = along_x(own, n)
    cored = [[swap(x, 1, n) for x in group] for group in (own, across)]
    att_pieces = [x for quad in zip(own, cored[0], across, cored[1]) for x in quad]
    att_where = [(j, None) for j in range(n)]
    att, packed, state, w_att, gain = project(me, tokens, att_where, att_pieces)
    mixed, read, score, inv, kts, mvs = mix(packed, others(state, 1, seqs))
    kept, gres, gmix, hid, full_down, *ffn_shares = ffn(me, mixed, tokens, cotangent, full, ff, n)
    half = depth // 2

    def start_sum(shares, *first):
        near, low, high, high_core, rest = shares
        high = add(after(high, *first) if first else high, swap(high_core, 1, n))
        rest = swap(rest, 1, n)
        return (near, rest), add(low, rest[depth:]), high

    def joined(near, crossed, base, *first):
        own, core = near
        own = after(own, *first)
        return {base + i: add(own[base + i], core[base + i], crossed[i]) for i in range(half)}

    def along(part, k):
        return swap(part, 4 * k, n) if k else part

    def seq_sum(x):
        step = 1
        while step < seqs:
            x = add(x, lax.ppermute(x, "seq", [(i, i ^ step) for i in range(seqs)]))
            step *= 2
        return x.astype(F32)

    near, low, high = start_sum(ffn_shares)
    crossed_high = swap(high, 2, n)
    gq, a, u, gtot, gstate = read_back(packed, after(gmix, high), read, score, inv, kts, mvs)
    crossed_low = swap(after(low, gq), 2, n)
    mine = joined(near, crossed_high, half, gq)
    ffn_parts = [along(mine[k], k) for k in range(half, depth)]
    gkvc, *shares = write_back(
        me, packed, gmix, a, u, gtot, after(others(gstate, -1, seqs), *mine.values()), att, gq, n
    )
    mine = joined(near, crossed_low, 0, gkvc)
    att_near, att_low, att_high = start_sum(shares, *ffn_parts[-1:], *mine.values())
    ffn_parts += [along(mine[k], k) for k in range(half)]
    crossed_high, crossed_low = swap(att_high, 2, n), swap(att_low, 2, n)
    layer_out = ffn_out(after(hid, att_low, mine[0]), kept, full_down)
    ffn_sum = add(after(mine[0], layer_out), *(p for p in ffn_parts if p is not mine[0]))
    mine = joined(att_near, crossed_high, half, layer_out)
    att_parts = [along(mine[k], k) for k in range(half, depth)]
    mine = joined(att_near, crossed_low, 0, layer_out, *mine.values())
    att_parts += [along(mine[k], k) for k in range(half)]
    grad_tokens = input_grad(gain, tokens, after(gq, *mine.values(), ffn_sum), gkvc, w_att, gres)
    ffn_share = seq_sum(ffn_sum)
    att_sum = add(*[after(p, grad_tokens) for p in att_parts])
    att_share = seq_sum(att_sum)
    gain_share = jnp.sum(att_share * first[:, : 4 * d].astype(F32), axis=1) / gain_attn.astype(F32)
    up, down, out, vec = (
        ffn_share[:, :ff],
        ffn_share[:, ff : 2 * ff],
        ffn_share[:, 2 * ff : 2 * ff + d],
        ffn_share[:, 2 * ff + d :],
    )
    down = jnp.concatenate([down[:, m * d : (m + 1) * d] for m in range(mult)], axis=0)
    return (
        layer_out,
        grad_tokens,
        att_share[:, 0:d],
        att_share[:, d : 2 * d],
        att_share[:, 2 * d : 3 * d],
        att_share[:, 3 * d :],
        out,
        up,
        down,
        gain_share,
        vec[1, :r],
        vec[2, : r * mult],
        vec[3, :r],
    )


def solution(mesh):
    tokens = P(("fsdp", "seq"), None)
    matrix = P("fsdp", None)
    vector = P("fsdp")
    return jax.shard_map(
        partial(on_device, mesh.shape["fsdp"], mesh.shape["seq"]),
        mesh=mesh,
        in_specs=(tokens,) + (matrix,) * 7 + (vector,) * 4 + (tokens,),
        out_specs=(tokens, tokens) + (matrix,) * 7 + (vector,) * 4,
        check_vma=False,
    )
```

```python
from functools import partial
import jax
import jax.numpy as jnp
from jax import lax
from jax.experimental import pallas as pl
from jax.experimental.pallas import tpu as pltpu
from jax.sharding import PartitionSpec as P

F32 = jnp.float32
BF16 = jnp.bfloat16
HEAD = 64
QUAD = 256
SCALE = HEAD ** -0.5
CHUNK = 128
VMEM_LIMIT = 60 * 1024 * 1024


def mm(a, b):
    return lax.dot_general(a, b, (((1,), (0,)), ((), ())), preferred_element_type=F32)


def mm_t(a, b):
    return lax.dot_general(a, b, (((1,), (1,)), ((), ())), preferred_element_type=F32)


def t_mm(a, b):
    return lax.dot_general(a, b, (((0,), (0,)), ((), ())), preferred_element_type=F32)


def iota(shape, dim):
    return lax.broadcasted_iota(jnp.int32, shape, dim)


def normalize(x):
    centred = x - jnp.mean(x, axis=-1, keepdims=True)
    spread = jnp.mean(centred * centred, axis=-1, keepdims=True)
    factor = lax.rsqrt(spread + 1e-05)
    return centred * factor, factor


def norm_back(g, normed, factor):
    first = jnp.mean(g, axis=-1, keepdims=True)
    second = jnp.mean(g * normed, axis=-1, keepdims=True)
    return factor * (g - first - normed * second)


def blocks_of(x):
    lane = iota(x.shape, 1) // HEAD
    zero = jnp.zeros_like(x)
    return jnp.concatenate([jnp.where(lane == h, x, zero) for h in range(4)], axis=0)


def blocks_t(x):
    xt = x.T
    row = iota(xt.shape, 0) // HEAD
    zero = jnp.zeros_like(xt)
    return jnp.concatenate([jnp.where(row == h, xt, zero) for h in range(4)], axis=1)


def tri(x, lower):
    c = x.shape[0]
    row, col = iota(x.shape, 0), iota(x.shape, 1) % c
    keep = row >= col if lower else row <= col
    return jnp.where(keep, x, 0.0).astype(BF16)


def per_head(x, op, neutral):
    parts = []
    for p in range(x.shape[1] // 128):
        v = x[:, p * 128 : (p + 1) * 128]
        low = iota(v.shape, 1) < HEAD
        a = op(jnp.where(low, v, neutral), axis=-1, keepdims=True)
        b = op(jnp.where(low, neutral, v), axis=-1, keepdims=True)
        parts.append(jnp.where(low, a, b))
    return jnp.concatenate(parts, axis=1)


def head_square():
    return iota((QUAD, QUAD), 0) // HEAD == iota((QUAD, QUAD), 1) // HEAD


STATE = 2 * HEAD + 16


def store_state(st_ref, first, second, total):
    square = head_square()
    for g in range(st_ref.shape[0]):
        for k, ref in enumerate((first, second)):
            x = jnp.where(square, ref[g], 0.0)
            st_ref[g, k * HEAD : (k + 1) * HEAD, :] = (x[0:64] + x[64:128] + x[128:192] + x[192:256]).astype(BF16)
        hi, lo = hi_lo(total[0:1, g * QUAD : (g + 1) * QUAD])
        row = iota((16, QUAD), 0)
        spread = lambda x: jnp.broadcast_to(x.astype(F32), (16, QUAD))
        st_ref[g, 2 * HEAD :, :] = jnp.where(row == 0, spread(hi), jnp.where(row == 1, spread(lo), 0.0)).astype(BF16)


def load_state(st_ref, first, second, total):
    square = head_square()
    for g in range(st_ref.shape[0]):
        for k, ref in enumerate((first, second)):
            x = st_ref[g, k * HEAD : (k + 1) * HEAD, :].astype(F32)
            ref[g] = jnp.where(square, jnp.concatenate([x] * 4, axis=0), 0.0)
        both = jnp.sum(st_ref[g, 2 * HEAD :, :].astype(F32), axis=0, keepdims=True)
        total[:, g * QUAD : (g + 1) * QUAD] = jnp.broadcast_to(both, (8, QUAD))


def hi_lo(x):
    hi = x.astype(BF16)
    return hi, (x - hi.astype(F32)).astype(BF16)


def spread_vector(vecs, me, n, r, k, each, total):
    pick = (iota((n, n * r), 1) == iota((n, n * r), 0) * r + k).astype(BF16)
    rows = mm(pick, vecs).astype(BF16)
    tile = (iota((128, total), 1) % each == iota((128, total), 0)).astype(BF16)
    wide = mm(rows, tile)
    own = iota((n, total), 1) // each == (iota((n, total), 0) ^ me)
    return jnp.sum(jnp.where(own, wide, 0.0), axis=0, keepdims=True)


def gather_vector(vec, me, n, each):
    total = vec.shape[1]
    own = iota((n, total), 1) // each == (iota((n, total), 0) ^ me)
    wide = jnp.where(own, vec, 0.0).astype(BF16)
    tile = (iota((128, total), 1) % each == iota((128, total), 0)).astype(BF16)
    return mm_t(wide, tile).astype(BF16)


def share_ref(refs, j, n):
    near, low, high, high_core, rest_core = refs
    a, k, half = j % 4, j // 4, n // 8
    if a == 0:
        return near.at[k]
    if a == 1:
        return rest_core.at[k]
    if k >= half:
        return (high if a == 2 else high_core).at[k - half]
    return low.at[k] if a == 2 else rest_core.at[2 * half + k]


def share_shapes(n, r, width):
    half = n // 8
    return [jax.ShapeDtypeStruct((c, r, width), BF16) for c in (2 * half, half, half, half, 3 * half)]


def piece_refs(where, refs):
    return [refs[a] if row is None else refs[a].at[row] for a, row in where]


def pack_kernel(q, k, v, c, o, up, down, gain_a, gain_f, b_up, b_down, first, second):
    r, d = q.shape
    ff = up.shape[1]
    for p, ref in enumerate((q, k, v, c)):
        first[:, p * d : (p + 1) * d] = ref[...]
    tile = jnp.zeros((r, 128), F32)
    row, col = iota((r, 128), 0), iota((r, 128), 1)
    for i, ref in enumerate((gain_a, gain_f, b_up, b_down)):
        length = ref.shape[1]
        wide = jnp.broadcast_to(ref[...].astype(F32), (r, length))
        if length < 128:
            wide = jnp.concatenate([wide, jnp.zeros((r, 128 - length), F32)], axis=1)
        tile = jnp.where(row == i, wide, tile)
    first[:, 4 * d :] = tile.astype(BF16)
    second[:, 2 * ff + d :] = tile.astype(BF16)
    second[:, :ff] = up[...]
    for m in range(ff // d):
        second[:, ff + m * d : ff + (m + 1) * d] = down[m * r : (m + 1) * r, :]
    second[:, 2 * ff : 2 * ff + d] = o[...]


def pack(q, k, v, c, o, up, down, gain_a, gain_f, b_up, b_down):
    r, d = q.shape
    ff = up.shape[1]
    return pl.pallas_call(
        pack_kernel,
        out_shape=[jax.ShapeDtypeStruct((r, 4 * d + 128), BF16), jax.ShapeDtypeStruct((r, 2 * ff + d + 128), BF16)],
        cost_estimate=pl.CostEstimate(flops=0, bytes_accessed=1 << 20, transcendentals=0),
        name="pack",
    )(q, k, v, c, o, up, down, *(x.reshape(1, -1) for x in (gain_a, gain_f, b_up, b_down)))


def stack_kernel(*refs):
    for i, ref in enumerate(refs[:-1]):
        refs[-1][i] = ref[...]


def stack(items):
    return pl.pallas_call(
        stack_kernel,
        out_shape=jax.ShapeDtypeStruct((len(items),) + items[0].shape, items[0].dtype),
        cost_estimate=pl.CostEstimate(flops=0, bytes_accessed=2 << 20, transcendentals=0),
        name="stack",
    )(*items)


def project_kernel(where, arrays, r, me_ref, tok_hbm, *refs):
    n = len(where)
    pieces = piece_refs(where, refs)
    (att_hbm, pack_hbm, st_ref, w_hbm, gain_ref,
     tok, att, pack, w_all, vecs, normed, written, first, second, total, sems, vsems, tsem, osems) = refs[arrays:]
    t, d = att.shape
    wide = 4 * d
    rows = 256
    me = me_ref[0]
    load = pltpu.make_async_copy(tok_hbm, tok, tsem)
    load.start()
    vector_copies, copies = [], []
    for j in range(n):
        at = pl.multiple_of((me ^ j) * r, r)
        copies.append(pltpu.make_async_copy(pieces[j].at[:, pl.ds(0, wide)], w_all.at[pl.ds(at, r), :], sems.at[j]))
        vector_copies.append(pltpu.make_async_copy(pieces[j].at[:, pl.ds(wide, 128)], vecs.at[pl.ds(j * r, r), :], vsems.at[j]))
    for c in vector_copies + copies:
        c.start()
    sent = []

    def send(src, dst):
        copy = pltpu.make_async_copy(src, dst, osems.at[len(sent)])
        copy.start()
        sent.append(copy)

    load.wait()
    for i in range(t // rows):
        rs = pl.ds(i * rows, rows)
        normed[rs, :], _ = normalize(tok[rs, :].astype(F32))
    for c in vector_copies:
        c.wait()
    gain = spread_vector(vecs[...], me, n, r, 0, r, d)
    gain_ref[...] = jnp.broadcast_to(gain, gain_ref.shape)
    for c in copies:
        c.wait()
    send(w_all, w_hbm)
    sums = jnp.zeros((1, d), F32)
    for i in range(t // rows):
        rs = pl.ds(i * rows, rows)
        x = (normed[rs, :] * gain).astype(BF16)
        att[rs, :] = x
        send(att.at[rs, :], att_hbm.at[rs, :])
        for p in (3, 1, 2, 0):
            full = mm(x, w_all[:, p * d : (p + 1) * d]).astype(BF16)
            pack[rs, p * d : (p + 1) * d] = full
            if p == 3:
                new = jnp.exp(full.astype(F32)).astype(BF16)
                written[rs, :] = new
                sums += jnp.sum(new.astype(F32), axis=0, keepdims=True)
        send(pack.at[rs, :], pack_hbm.at[rs, :])
    for g in range(d // QUAD):
        s = slice(g * QUAD, (g + 1) * QUAD)
        first[g] = t_mm(pack[:, d + g * QUAD : d + (g + 1) * QUAD], written[:, s])
        second[g] = t_mm(written[:, s], pack[:, 2 * d + g * QUAD : 2 * d + (g + 1) * QUAD])
    total[...] = jnp.broadcast_to(sums, total.shape)
    store_state(st_ref, first, second, total)
    for c in sent:
        c.wait()


def project(me, tokens, where, pieces):
    t, d = tokens.shape
    n = len(where)
    r = d // n
    wide = 4 * d
    g = d // QUAD
    hbm = pl.BlockSpec(memory_space=pl.ANY)
    vmem = pl.BlockSpec(memory_space=pltpu.VMEM)
    return pl.pallas_call(
        partial(project_kernel, where, len(pieces), r),
        in_specs=[pl.BlockSpec(memory_space=pltpu.SMEM)] + [hbm] * (1 + len(pieces)),
        out_specs=[hbm, hbm, vmem, hbm, vmem],
        out_shape=[
            jax.ShapeDtypeStruct((t, d), BF16),
            jax.ShapeDtypeStruct((t, wide), BF16),
            jax.ShapeDtypeStruct((g, STATE, QUAD), BF16),
            jax.ShapeDtypeStruct((d, wide), BF16),
            jax.ShapeDtypeStruct((8, d), F32),
        ],
        scratch_shapes=[
            pltpu.VMEM((t, d), BF16),
            pltpu.VMEM((t, d), BF16),
            pltpu.VMEM((t, wide), BF16),
            pltpu.VMEM((d, wide), BF16),
            pltpu.VMEM((n * r, 128), BF16),
            pltpu.VMEM((t, d), F32),
            pltpu.VMEM((t, d), BF16),
            pltpu.VMEM((g, QUAD, QUAD), F32),
            pltpu.VMEM((g, QUAD, QUAD), F32),
            pltpu.VMEM((8, d), F32),
            pltpu.SemaphoreType.DMA((n,)),
            pltpu.SemaphoreType.DMA((n,)),
            pltpu.SemaphoreType.DMA,
            pltpu.SemaphoreType.DMA((1 + 2 * (t // 256),)),
        ],
        compiler_params=pltpu.CompilerParams(vmem_limit_bytes=VMEM_LIMIT),
        cost_estimate=pl.CostEstimate(flops=2 * t * d * wide, bytes_accessed=12 << 20, transcendentals=t * d),
        name="project",
    )(me, tokens, *pieces)


def mix_kernel(pack_ref, st_in, mix_ref, read_ref, score_ref, inv_ref, kts_ref, mvs_ref, kt, mv, tot):
    d = mix_ref.shape[1]
    rows = mix_ref.shape[0]

    @pl.when(pl.program_id(0) == 0)
    def _():
        load_state(st_in, kt, mv, tot)

    c = CHUNK
    square = head_square()
    ones = (iota((c, c), 0) >= iota((c, c), 1)).astype(BF16)
    units = [(b, g) for b in range(rows // c) for g in range(d // QUAD)]
    at = {(b, g): (slice(b * c, (b + 1) * c), slice(g * QUAD, (g + 1) * QUAD)) for b, g in units}
    part = lambda p: {(b, g): pack_ref[at[b, g][0], p * d + g * QUAD : p * d + (g + 1) * QUAD] for b, g in units}
    q, k, v = part(0), part(1), part(2)
    written = {x: jnp.exp(y.astype(F32)).astype(BF16) for x, y in part(3).items()}
    wb = {x: blocks_of(written[x]) for x in units}
    pairs = {x: tri(mm(q[x], blocks_t(k[x])), True) for x in units}
    ktb, mvb, inv = {}, {}, {}
    for x in units:
        b, g = x
        ktb[x], mvb[x] = kt[g].astype(BF16), mv[g].astype(BF16)
        kts_ref[b, g] = ktb[x]
        mvs_ref[b, g] = mvb[x]
        kt[g] += jnp.where(square, t_mm(k[x], written[x]), 0.0)
        mv[g] += jnp.where(square, t_mm(written[x], v[x]), 0.0)
        total = mm(ones, written[x]) + tot[0:1, at[x][1]]
        tot[0:1, at[x][1]] = total[c - 1 : c, :]
        inv[x] = 1.0 / total
        inv_ref[at[x]] = inv[x]
    score = {x: (mm(pairs[x], wb[x]) + mm(q[x], ktb[x])) * SCALE * inv[x] for x in units}
    for x in units:
        score_ref[at[x]] = score[x]
    e = {x: jnp.exp(score[x] - per_head(score[x], jnp.max, -jnp.inf)) for x in units}
    read = {x: e[x] / per_head(e[x], jnp.sum, 0.0) for x in units}
    for x in units:
        read_ref[at[x]] = read[x]
    scaled = {x: (read[x] * inv[x]).astype(BF16) for x in units}
    recall = {x: tri(mm(scaled[x], blocks_t(written[x])), True) for x in units}
    for x in units:
        mix_ref[at[x]] = (mm(recall[x], blocks_of(v[x])) + mm(scaled[x], mvb[x])).astype(BF16)


def mix(packed, state, rows=256):
    t, wide = packed.shape
    d = wide // 4
    g = d // QUAD
    const = lambda *shape: pl.BlockSpec(shape, lambda i: (0,) * len(shape))
    per = rows // CHUNK
    row = lambda w: pl.BlockSpec((rows, w), lambda i: (i, 0))
    return pl.pallas_call(
        mix_kernel,
        grid=(t // rows,),
        in_specs=[row(wide), const(g, STATE, QUAD)],
        out_specs=[row(d)] * 4 + [pl.BlockSpec((per, g, QUAD, QUAD), lambda i: (i, 0, 0, 0))] * 2,
        out_shape=[jax.ShapeDtypeStruct((t, d), BF16)] + [jax.ShapeDtypeStruct((t, d), F32)] * 3
        + [jax.ShapeDtypeStruct((t // CHUNK, g, QUAD, QUAD), BF16)] * 2,
        scratch_shapes=[pltpu.VMEM((g, QUAD, QUAD), F32), pltpu.VMEM((g, QUAD, QUAD), F32), pltpu.VMEM((8, d), F32)],
        compiler_params=pltpu.CompilerParams(vmem_limit_bytes=VMEM_LIMIT),
        cost_estimate=pl.CostEstimate(flops=6 * 10**9, bytes_accessed=16 << 20, transcendentals=2 * t * d),
        name="mix",
    )(packed, state)


def ffn_kernel(n, me_ref, mixed_hbm, tok_hbm, cot_hbm, full_ref, kept_hbm, gres_hbm, gmix_hbm, hid_hbm, down_hbm, *refs):
    share_refs = refs[:5]
    (mixed, tok, cot, kept, gres, gmix, w_out, w_up, w_down, vecs, hid, gpre, fin, gbr, normed_f, sems, osems, dsem) = refs[5:]
    me = me_ref[0]
    t, d = mixed.shape
    ff = w_up.shape[1]
    r = d // n
    mult = ff // d
    rows = 512
    part = 512
    steps = t // rows
    parts = ff // part

    def load(src, dst, i):
        copy = pltpu.make_async_copy(src, dst, sems.at[i])
        copy.start()
        return copy

    down_sem = 3
    early = [
        load(full_ref.at[:, pl.ds(2 * ff, d)], w_out, 0),
        load(mixed_hbm, mixed, 1),
        load(tok_hbm, tok, 2),
        load(full_ref.at[:, pl.ds(2 * ff + d, 128)], vecs, 4),
    ]
    late = [load(full_ref.at[:, pl.ds(0, ff)], w_up, 5), load(cot_hbm, cot, 6)]
    down = []
    for j in range(n):
        for m in range(mult):
            down.append((full_ref.at[pl.ds(j * r, r), pl.ds(ff + m * d, d)], w_down.at[pl.ds((j * mult + m) * r, r), :]))
    late += [load(src, dst, 7 + i) for i, (src, dst) in enumerate(down)]
    for c in early:
        c.wait()
    gain = spread_vector(vecs[...], 0, n, r, 1, r, d)
    b_up = spread_vector(vecs[...], 0, n, r, 2, r * mult, ff)
    b_down = spread_vector(vecs[...], 0, n, r, 3, r, d)

    sent = []

    def send(src, dst):
        copy = pltpu.make_async_copy(src, dst, osems.at[len(sent)])
        copy.start()
        sent.append(copy)

    ggain = jnp.zeros((1, d), F32)
    gbdown = jnp.zeros((1, d), F32)
    gbup = [jnp.zeros((1, part), F32)] * parts
    factors = []
    for i in range(steps):
        rs = pl.ds(i * rows, rows)
        resid = tok[rs, :].astype(F32) + mm(mixed[rs, :], w_out[...])
        kept[rs, :] = resid + b_down
        send(kept.at[rs, :], kept_hbm.at[rs, :])
        x, factor = normalize(resid)
        normed_f[rs, :] = x
        factors.append(factor)
        fin[rs, :] = (x * gain).astype(BF16)
    for c in late:
        c.wait()
    keep_down = pltpu.make_async_copy(w_down, down_hbm, dsem)
    keep_down.start()
    for i in range(steps):
        rs = pl.ds(i * rows, rows)
        ffn_in, normed, factor = fin[rs, :], normed_f[rs, :], factors[i]
        cot_b = cot[rs, :]
        cotf = cot_b.astype(F32)

        def entry(p):
            ps = slice(p * part, (p + 1) * part)
            return mm(ffn_in, w_up[:, ps]) + b_up[:, ps], mm_t(cot_b, w_down[ps, :])

        ready = entry(0)
        gin = None
        for p in range(parts):
            ps = slice(p * part, (p + 1) * part)
            pre, gh = ready
            if p + 1 < parts:
                ready = entry(p + 1)
            sig = 0.5 * jnp.tanh(0.5 * pre) + 0.5
            act = pre * sig
            gp = gh * (sig + act * (1.0 - sig))
            gbup[p] = gbup[p] + jnp.sum(gp, axis=0, keepdims=True)
            act, gp = act.astype(BF16), gp.astype(BF16)
            hid[rs, ps] = act
            gpre[rs, ps] = gp
            x = mm_t(gp, w_up[:, ps])
            gin = x if p == 0 else gin + x
        send(hid.at[rs, :], hid_hbm.at[rs, :])
        back = cotf + norm_back(gin * gain, normed, factor)
        gres[rs, :] = back
        send(gres.at[rs, :], gres_hbm.at[rs, :])
        back = back.astype(BF16)
        gbr[rs, :] = back
        gmix[rs, :] = mm_t(back, w_out[...]).astype(BF16)
        send(gmix.at[rs, :], gmix_hbm.at[rs, :])
        ggain += jnp.sum(gin * normed, axis=0, keepdims=True)
        gbdown += jnp.sum(cotf, axis=0, keepdims=True)

    def share(j, rows_of, ref, at, width):
        send(ref.at[rows_of(me ^ j), :], share_ref(share_refs, j, n).at[:, pl.ds(at, width)])

    own_rows = lambda f: pl.ds(pl.multiple_of(f * r, r), r)
    keep_down.wait()
    for p in range(parts):
        ps = slice(p * part, (p + 1) * part)
        w_down[ps, :] = t_mm(hid[:, ps], cot[...]).astype(BF16)
    for j in range(n):
        for m in range(mult):
            share(j, lambda f: pl.ds(pl.multiple_of((f * mult + m) * r, r), r), w_down, ff + m * d, d)
    w_out[...] = t_mm(mixed[...], gbr[...]).astype(BF16)
    va = gather_vector(ggain, 0, n, r)
    vb = gather_vector(jnp.concatenate(gbup, axis=1), 0, n, r * mult)
    vc = gather_vector(gbdown, 0, n, r)
    row = iota((r, 128), 0)
    pick = lambda v, j, i, rest: jnp.where(row == i, jnp.broadcast_to(v[j : j + 1].astype(F32), (r, 128)), rest)
    for j in range(n):
        tile = pick(va, j, 1, pick(vb, j, 2, pick(vc, j, 3, jnp.zeros((r, 128), F32))))
        vecs[j * r : (j + 1) * r, :] = tile.astype(BF16)
    for j in range(n):
        share(j, own_rows, w_out, 2 * ff, d)
        share(j, own_rows, vecs, 2 * ff + d, 128)
    for p in range(parts):
        ps = slice(p * part, (p + 1) * part)
        w_up[:, ps] = t_mm(fin[...], gpre[:, ps]).astype(BF16)
    for j in range(n):
        share(j, own_rows, w_up, 0, ff)
    for c in sent:
        c.wait()


def ffn(me, mixed, tokens, cot, full, ff, n):
    t, d = tokens.shape
    hbm = pl.BlockSpec(memory_space=pl.ANY)
    moves = n * (ff // d)
    return pl.pallas_call(
        partial(ffn_kernel, n),
        in_specs=[pl.BlockSpec(memory_space=pltpu.SMEM)] + [hbm] * 4,
        out_specs=[hbm] * 10,
        out_shape=[
            jax.ShapeDtypeStruct((t, d), F32),
            jax.ShapeDtypeStruct((t, d), F32),
            jax.ShapeDtypeStruct((t, d), BF16),
            jax.ShapeDtypeStruct((t, ff), BF16),
            jax.ShapeDtypeStruct((ff, d), BF16),
        ]
        + share_shapes(n, d // n, full.shape[1]),
        scratch_shapes=[pltpu.VMEM((t, d), BF16)] * 3
        + [pltpu.VMEM((t, d), F32), pltpu.VMEM((t, d), F32), pltpu.VMEM((t, d), BF16)]
        + [
            pltpu.VMEM((d, d), BF16),
            pltpu.VMEM((d, ff), BF16),
            pltpu.VMEM((ff, d), BF16),
            pltpu.VMEM((d, 128), BF16),
            pltpu.VMEM((t, ff), BF16),
            pltpu.VMEM((t, ff), BF16),
            pltpu.VMEM((t, d), BF16),
            pltpu.VMEM((t, d), BF16),
            pltpu.VMEM((t, d), F32),
            pltpu.SemaphoreType.DMA((7 + moves,)),
            pltpu.SemaphoreType.DMA((4 * (t // 256) + 3 * n + moves,)),
            pltpu.SemaphoreType.DMA,
        ],
        compiler_params=pltpu.CompilerParams(vmem_limit_bytes=VMEM_LIMIT),
        cost_estimate=pl.CostEstimate(flops=11 * t * d * ff, bytes_accessed=20 << 20, transcendentals=t * ff),
        name="ffn",
    )(me, mixed, tokens, cot, full)


def ffn_out_kernel(hid_ref, kept_ref, down_ref, out_ref):
    out_ref[...] = (kept_ref[...] + mm(hid_ref[...], down_ref[...])).astype(BF16)


def ffn_out(hid, kept, down, rows=512):
    t, ff = hid.shape
    d = kept.shape[1]
    row = lambda w: pl.BlockSpec((rows, w), lambda i: (i, 0))
    return pl.pallas_call(
        ffn_out_kernel,
        grid=(t // rows,),
        in_specs=[row(ff), row(d), pl.BlockSpec((ff, d), lambda i: (0, 0))],
        out_specs=row(d),
        out_shape=jax.ShapeDtypeStruct((t, d), BF16),
        compiler_params=pltpu.CompilerParams(vmem_limit_bytes=VMEM_LIMIT),
        cost_estimate=pl.CostEstimate(flops=2 * t * d * ff, bytes_accessed=9 << 20, transcendentals=0),
        name="ffn_out",
    )(hid, kept, down)


def read_back_kernel(pack_ref, gmix_ref, read_ref, score_ref, inv_ref, kts_ref, mvs_ref,
                     gq_ref, a_ref, u_ref, gtot_ref, st_ref, gk_ref, gv_ref, gt_ref):
    rows, d = gmix_ref.shape

    @pl.when(pl.program_id(0) == 0)
    def _():
        gk_ref[...] = jnp.zeros_like(gk_ref)
        gv_ref[...] = jnp.zeros_like(gv_ref)
        gt_ref[...] = jnp.zeros_like(gt_ref)

    c = CHUNK
    units = [(b, g) for b in range(rows // c) for g in range(d // QUAD)]
    at = {(b, g): (slice(b * c, (b + 1) * c), slice(g * QUAD, (g + 1) * QUAD)) for b, g in units}
    part = lambda p: {(b, g): pack_ref[at[b, g][0], p * d + g * QUAD : p * d + (g + 1) * QUAD] for b, g in units}
    q, k, v = part(0), part(1), part(2)
    written = {x: jnp.exp(y.astype(F32)).astype(BF16) for x, y in part(3).items()}
    wb = {x: blocks_of(written[x]) for x in units}
    gm = {x: gmix_ref[at[x]] for x in units}
    gpair = {x: tri(mm(gm[x], blocks_t(v[x])), True) for x in units}
    weighted = {x: (mm(gpair[x], wb[x]) + mm_t(gm[x], mvs_ref[x])) * inv_ref[at[x]] * read_ref[at[x]] for x in units}
    gscore = {x: weighted[x] - read_ref[at[x]] * per_head(weighted[x], jnp.sum, 0.0) for x in units}
    a, u = {}, {}
    for x in units:
        inv = inv_ref[at[x]]
        a[x] = (gscore[x] * inv * SCALE).astype(BF16)
        u[x] = (read_ref[at[x]] * inv).astype(BF16)
        a_ref[at[x]] = a[x]
        u_ref[at[x]] = u[x]
        gtot = (gscore[x] * score_ref[at[x]] + weighted[x]) * inv
        gtot_ref[at[x]] = gtot
        gt_ref[0:1, at[x][1]] += jnp.sum(gtot, axis=0, keepdims=True)
    spair = {x: tri(mm(a[x], blocks_t(written[x])), True) for x in units}
    for x in units:
        gq_ref[at[x]] = (mm(spair[x], blocks_of(k[x])) + mm_t(a[x], kts_ref[x])).astype(BF16)
    for g in range(d // QUAD):
        s = slice(g * QUAD, (g + 1) * QUAD)
        every = lambda y: jnp.concatenate([y[b, g] for b in range(rows // c)], axis=0)
        gk_ref[g] += t_mm(every(a), every(q))
        gv_ref[g] += t_mm(every(u), every(gm))

    @pl.when(pl.program_id(0) == pl.num_programs(0) - 1)
    def _():
        store_state(st_ref, gk_ref, gv_ref, gt_ref)


def read_back(packed, gmix, read, score, inv, kts, mvs, rows=512):
    t, wide = packed.shape
    d = wide // 4
    g = d // QUAD
    const = lambda *shape: pl.BlockSpec(shape, lambda i: (0,) * len(shape))
    per = rows // CHUNK
    row = lambda w: pl.BlockSpec((rows, w), lambda i: (i, 0))
    st = pl.BlockSpec((per, g, QUAD, QUAD), lambda i: (i, 0, 0, 0))
    return pl.pallas_call(
        read_back_kernel,
        grid=(t // rows,),
        in_specs=[row(wide), row(d), row(d), row(d), row(d), st, st],
        out_specs=[row(d)] * 4 + [const(g, STATE, QUAD)],
        out_shape=[jax.ShapeDtypeStruct((t, d), BF16)] * 3 + [jax.ShapeDtypeStruct((t, d), F32)]
        + [jax.ShapeDtypeStruct((g, STATE, QUAD), BF16)],
        scratch_shapes=[pltpu.VMEM((g, QUAD, QUAD), F32), pltpu.VMEM((g, QUAD, QUAD), F32), pltpu.VMEM((8, d), F32)],
        compiler_params=pltpu.CompilerParams(vmem_limit_bytes=VMEM_LIMIT),
        cost_estimate=pl.CostEstimate(flops=6 * 10**9, bytes_accessed=20 << 20, transcendentals=t * d),
        name="read_back",
    )(packed, gmix, read, score, inv, kts, mvs)


def write_back_kernel(n, me_ref, pack_ref, gmix_ref, a_ref, u_ref, gtot_ref, st_in, att_hbm, gq_hbm, out_ref, *refs):
    share_refs = refs[:5]
    gk, gv, gt, att, gq, grads, acc, isems, sems = refs[5:]
    rows, d = gmix_ref.shape
    loads = [pltpu.make_async_copy(att_hbm, att, isems.at[0]), pltpu.make_async_copy(gq_hbm, gq, isems.at[1])]

    @pl.when(pl.program_id(0) == 0)
    def _():
        for x in loads:
            x.start()
        load_state(st_in, gk, gv, gt)

    base = (pl.num_programs(0) - 1 - pl.program_id(0)) * rows
    c = CHUNK
    square = head_square()
    ones = (iota((c, c), 0) <= iota((c, c), 1)).astype(BF16)
    units = [(b, g) for b in reversed(range(rows // c)) for g in range(d // QUAD)]
    at = {(b, g): (slice(b * c, (b + 1) * c), slice(g * QUAD, (g + 1) * QUAD)) for b, g in units}
    part = lambda p: {(b, g): pack_ref[at[b, g][0], p * d + g * QUAD : p * d + (g + 1) * QUAD] for b, g in units}
    q, k, v = part(0), part(1), part(2)
    wf = {x: jnp.exp(y.astype(F32)) for x, y in part(3).items()}
    written = {x: wf[x].astype(BF16) for x in units}
    gm, a, u = ({x: ref[at[x]] for x in units} for ref in (gmix_ref, a_ref, u_ref))
    qb, gb, ab, ub = ({x: blocks_of(y[x]) for x in units} for y in (q, gm, a, u))
    gkb, gvb, after = {}, {}, {}
    for x in units:
        g = x[1]
        gkb[x], gvb[x] = gk[g].astype(BF16), gv[g].astype(BF16)
        gk[g] += jnp.where(square, t_mm(a[x], q[x]), 0.0)
        gv[g] += jnp.where(square, t_mm(u[x], gm[x]), 0.0)
        hi, lo = hi_lo(gtot_ref[at[x]])
        after[x] = mm(ones, hi) + mm(ones, lo) + gt[0:1, at[x][1]]
        gt[0:1, at[x][1]] = after[x][0:1, :]

    def out(p, x, y):
        y = y.astype(BF16)
        cols = slice(p * d + x[1] * QUAD, p * d + (x[1] + 1) * QUAD)
        out_ref[at[x][0], cols] = y
        grads[pl.ds(pl.multiple_of(base + x[0] * c, c), c), cols] = y

    st = {x: tri(mm(written[x], blocks_t(a[x])), False) for x in units}
    rt = {x: tri(mm(written[x], blocks_t(u[x])), False) for x in units}
    for x in units:
        out(0, x, mm(st[x], qb[x]) + mm(written[x], gkb[x]))
    for x in units:
        out(1, x, mm(rt[x], gb[x]) + mm(written[x], gvb[x]))
    pt = {x: tri(mm(k[x], blocks_t(q[x])), False) for x in units}
    gp = {x: tri(mm(v[x], blocks_t(gm[x])), False) for x in units}
    for x in units:
        gw = mm(pt[x], ab[x]) + mm(gp[x], ub[x]) + mm_t(k[x], gkb[x]) + mm_t(v[x], gvb[x])
        out(2, x, wf[x] * (gw - after[x]))

    @pl.when(pl.program_id(0) == pl.num_programs(0) - 1)
    def _():
        for x in loads:
            x.wait()
        r = d // n
        me = me_ref[0]
        acc[:, 0:d] = t_mm(att[...], gq[...]).astype(BF16)
        for p in range(3):
            acc[:, (p + 1) * d : (p + 2) * d] = t_mm(att[...], grads[:, p * d : (p + 1) * d]).astype(BF16)
        outs = []
        for j in range(n):
            frm = pl.multiple_of((me ^ j) * r, r)
            dst = share_ref(share_refs, j, n)
            outs.append(pltpu.make_async_copy(acc.at[pl.ds(frm, r), :], dst, sems.at[j]))
        for x in outs:
            x.start()
        for x in outs:
            x.wait()


def write_back(me, packed, gmix, a, u, gtot, state, att, gq, n, rows=256):
    t, wide = packed.shape
    d = wide // 4
    g = d // QUAD
    r = d // n
    last = t // rows - 1
    const = lambda *shape: pl.BlockSpec(shape, lambda i: (0,) * len(shape))
    row = lambda w: pl.BlockSpec((rows, w), lambda i: (last - i, 0))
    hbm = pl.BlockSpec(memory_space=pl.ANY)
    return pl.pallas_call(
        partial(write_back_kernel, n),
        grid=(t // rows,),
        in_specs=[pl.BlockSpec(memory_space=pltpu.SMEM), row(wide), row(d), row(d), row(d), row(d), const(g, STATE, QUAD), hbm, hbm],
        out_specs=[row(3 * d)] + [hbm] * 5,
        out_shape=[jax.ShapeDtypeStruct((t, 3 * d), BF16)] + share_shapes(n, r, wide),
        scratch_shapes=[
            pltpu.VMEM((g, QUAD, QUAD), F32),
            pltpu.VMEM((g, QUAD, QUAD), F32),
            pltpu.VMEM((8, d), F32),
            pltpu.VMEM((t, d), BF16),
            pltpu.VMEM((t, d), BF16),
            pltpu.VMEM((t, 3 * d), BF16),
            pltpu.VMEM((d, wide), BF16),
            pltpu.SemaphoreType.DMA((2,)),
            pltpu.SemaphoreType.DMA((n,)),
        ],
        compiler_params=pltpu.CompilerParams(vmem_limit_bytes=VMEM_LIMIT),
        cost_estimate=pl.CostEstimate(flops=11 * 10**9, bytes_accessed=18 << 20, transcendentals=t * d),
        name="write_back",
    )(me, packed, gmix, a, u, gtot, state, att, gq)


def input_grad_kernel(gain_ref, tok_ref, gq_ref, gkvc_ref, w_ref, gres_ref, out_ref):
    d = tok_ref.shape[1]
    gain = gain_ref[0:1, :]
    gin = mm_t(gq_ref[...], w_ref[:, 0:d]) + mm_t(gkvc_ref[...], w_ref[:, d:])
    normed, factor = normalize(tok_ref[...].astype(F32))
    out_ref[...] = gres_ref[...] + norm_back(gin * gain, normed, factor)


def input_grad(gain, tokens, gq, gkvc, w, gres, rows=256):
    t, d = tokens.shape
    const = lambda *shape: pl.BlockSpec(shape, lambda i: (0,) * len(shape))
    row = lambda w: pl.BlockSpec((rows, w), lambda i: (i, 0))
    return pl.pallas_call(
        input_grad_kernel,
        grid=(t // rows,),
        in_specs=[const(8, d), row(d), row(d), row(3 * d), const(d, 4 * d), row(d)],
        out_specs=row(d),
        out_shape=jax.ShapeDtypeStruct((t, d), F32),
        compiler_params=pltpu.CompilerParams(vmem_limit_bytes=VMEM_LIMIT),
        cost_estimate=pl.CostEstimate(flops=8 * t * d * d, bytes_accessed=12 << 20, transcendentals=0),
        name="input_grad",
    )(gain, tokens, gq, gkvc, w, gres)


def swap(x, mask, n):
    return lax.ppermute(x, "fsdp", [(i, i ^ mask) for i in range(n)])


def after(x, *first):
    return lax.optimization_barrier((x, *first))[0]


def add(*items):
    return sum(x.astype(F32) for x in items).astype(BF16)


def along_z(shard, n):
    return [shard] + [swap(shard, 4 * k, n) for k in range(1, n // 4)]


def along_x(own, n):
    return [swap(x, 2, n) for x in own]


def shift(x, by, seqs):
    return lax.ppermute(x, "seq", [(i, i + by) for i in range(seqs) if 0 <= i + by < seqs])


def others(state, direction, seqs):
    if seqs == 1:
        return jnp.zeros_like(state)
    if seqs > 2:
        state = state.astype(F32)
    total = shift(state, direction, seqs)
    step = 1
    while step < seqs - 1:
        total = total + shift(total, direction * step, seqs)
        step *= 2
    return total


def on_device(n, seqs, tokens, w_query, w_key, w_value, w_control, w_out, w_up, w_down,
              gain_attn, gain_ffn, bias_up, bias_down, cotangent):
    r, d = w_query.shape
    ff = w_up.shape[1]
    mult = ff // d
    me = lax.axis_index("fsdp").astype(jnp.int32).reshape(1)
    first, second = pack(w_query, w_key, w_value, w_control, w_out, w_up, w_down, gain_attn, gain_ffn, bias_up, bias_down)
    depth = n // 4
    own = along_z(first, n)
    full = lax.all_gather(second, "fsdp", axis=0, tiled=True)
    across = along_x(own, n)
    cored = [[swap(x, 1, n) for x in group] for group in (own, across)]
    att_pieces = [x for quad in zip(own, cored[0], across, cored[1]) for x in quad]
    att_where = [(j, None) for j in range(n)]
    att, packed, state, w_att, gain = project(me, tokens, att_where, att_pieces)
    mixed, read, score, inv, kts, mvs = mix(packed, others(state, 1, seqs))
    kept, gres, gmix, hid, full_down, *ffn_shares = ffn(me, mixed, tokens, cotangent, full, ff, n)
    half = depth // 2

    def start_sum(shares, *first):
        near, low, high, high_core, rest = shares
        high = add(after(high, *first) if first else high, swap(high_core, 1, n))
        rest = swap(rest, 1, n)
        return (near, rest), add(low, rest[depth:]), high

    def joined(near, crossed, base, *first):
        own, core = near
        own = after(own, *first)
        return {base + i: add(own[base + i], core[base + i], crossed[i]) for i in range(half)}

    def along(part, k):
        return swap(part, 4 * k, n) if k else part

    def seq_sum(x):
        step = 1
        while step < seqs:
            x = add(x, lax.ppermute(x, "seq", [(i, i ^ step) for i in range(seqs)]))
            step *= 2
        return x.astype(F32)

    near, low, high = start_sum(ffn_shares)
    crossed_high = swap(high, 2, n)
    gq, a, u, gtot, gstate = read_back(packed, after(gmix, high), read, score, inv, kts, mvs)
    crossed_low = swap(after(low, gq), 2, n)
    mine = joined(near, crossed_high, half, gq)
    ffn_parts = [along(mine[k], k) for k in range(half, depth)]
    gkvc, *shares = write_back(
        me, packed, gmix, a, u, gtot, after(others(gstate, -1, seqs), *mine.values()), att, gq, n
    )
    mine = joined(near, crossed_low, 0, gkvc)
    att_near, att_low, att_high = start_sum(shares, *ffn_parts[-1:], *mine.values())
    ffn_parts += [along(mine[k], k) for k in range(half)]
    crossed_high, crossed_low = swap(att_high, 2, n), swap(att_low, 2, n)
    layer_out = ffn_out(after(hid, att_low, mine[0]), kept, full_down)
    ffn_sum = add(after(mine[0], layer_out), *(p for p in ffn_parts if p is not mine[0]))
    mine = joined(att_near, crossed_high, half, layer_out)
    att_parts = [along(mine[k], k) for k in range(half, depth)]
    mine = joined(att_near, crossed_low, 0, layer_out, *mine.values())
    att_parts += [along(mine[k], k) for k in range(half)]
    grad_tokens = input_grad(gain, tokens, after(gq, *mine.values(), ffn_sum), gkvc, w_att, gres)
    ffn_share = seq_sum(ffn_sum)
    att_sum = add(*[after(p, grad_tokens) for p in att_parts])
    att_share = seq_sum(att_sum)
    gain_share = jnp.sum(att_share * first[:, : 4 * d].astype(F32), axis=1) / gain_attn.astype(F32)
    up, down, out, vec = (
        ffn_share[:, :ff],
        ffn_share[:, ff : 2 * ff],
        ffn_share[:, 2 * ff : 2 * ff + d],
        ffn_share[:, 2 * ff + d :],
    )
    down = jnp.concatenate([down[:, m * d : (m + 1) * d] for m in range(mult)], axis=0)
    return (
        layer_out,
        grad_tokens,
        att_share[:, 0:d],
        att_share[:, d : 2 * d],
        att_share[:, 2 * d : 3 * d],
        att_share[:, 3 * d :],
        out,
        up,
        down,
        gain_share,
        vec[1, :r],
        vec[2, : r * mult],
        vec[3, :r],
    )


def solution(mesh):
    tokens = P(("fsdp", "seq"), None)
    matrix = P("fsdp", None)
    vector = P("fsdp")
    return jax.shard_map(
        partial(on_device, mesh.shape["fsdp"], mesh.shape["seq"]),
        mesh=mesh,
        in_specs=(tokens,) + (matrix,) * 7 + (vector,) * 4 + (tokens,),
        out_specs=(tokens, tokens) + (matrix,) * 7 + (vector,) * 4,
        check_vma=False,
    )
```
